256 devices in a mesh: gx: 16 (over x, z_hi), gy: 16 (over y, z_lo, core).
Axes of the slice: x: 4, y: 4, z: 8 (z_hi: 4, z_lo: 2; z = z_hi * 2 + z_lo), core: 2. Of those that a mesh axis runs over, the one named last changes fastest.
Arguments:
- in_field: float32 [1, 64, 128, 256], P(None, 'gx', 'gy'), may hold values from -6 to 6
- cotangent: float32 [1, 64, 128, 256], P(None, 'gx', 'gy'), may hold values from -6 to 6
- w_first: float32 [27, 8, 1], replicated, may hold values from -1.25 to 1.25
- w_down: float32 [16, 8, 2, 2, 2], replicated, may hold values from -0.75 to 0.75
- w_coarse: float32 [27, 16, 16], replicated, may hold values from -0.3125 to 0.3125
- w_up: float32 [8, 16, 2, 2, 2], replicated, may hold values from -1.5 to 1.5
- w_joined: float32 [27, 8, 16], replicated, may hold values from -0.3125 to 0.3125
- w_final: float32 [1, 8], replicated, may hold values from -2 to 2
Outputs:
- imitated: float32 [1, 64, 128, 256], P(None, 'gx', 'gy')
- grad_first: float32 [27, 8, 1], replicated
- grad_down: float32 [16, 8, 2, 2, 2], replicated
- grad_coarse: float32 [27, 16, 16], replicated
- grad_up: float32 [8, 16, 2, 2, 2], replicated
- grad_joined: float32 [27, 8, 16], replicated
- grad_final: float32 [1, 8], replicated
The draws below stay inside these ranges and needn't reach their ends.
All inputs are finite; a program needn't handle non-finite values.
Results may differ from the reference program's by a relative error of at most 0.0003.
Values sent between devices are 32-bit elements; how exact they have to be, the bound alone decides.
No kernel may reach another device: no remote copies, remote signals or barrier semaphores. Data moves between devices by JAX's collectives and lax.ppermute only.
A program may use at most 128 MiB of HBM per device.

```python
import math
import jax
import jax.numpy as jnp
from jax import lax

CIN = 1
C1 = 8
C2 = 16
NX = 64
NY = 128
NZ = 256


def level_of(stream_key, extent, shards, smallest, largest):
    def one(axis_at, shards_of):
        heights = jax.random.uniform(jax.random.fold_in(jax.random.fold_in(stream_key, 6), axis_at), (shards_of,), jnp.float32, smallest / len(shards), largest / len(shards))
        return jnp.repeat(jnp.exp(heights), extent[axis_at] // shards_of).reshape((-1,) + (1,) * (len(extent) - axis_at - 1))

    loudness = one(*shards[0])
    for cut in shards[1:]:
        loudness = loudness * one(*cut)
    return loudness


def noise(rng, extent, width, limit, split=(), held_as=jnp.bfloat16):
    values = jax.random.normal(rng, extent, jnp.float32) * width
    if len(split) > 0:
        values = level_of(rng, extent, split, -0.22, 0.18) * values
    return jnp.clip(values, min=-limit, max=limit).astype(held_as)


def setup_inputs(seed: int = 0) -> dict:
    keys = jax.random.split(jax.random.key(seed), 9)
    in_field = noise(keys[0], (CIN, NX, NY, NZ), 1.0, 6.0, ((1, 16), (2, 16)), jnp.float32)
    cotangent = noise(keys[1], (CIN, NX, NY, NZ), 1.0, 6.0, ((1, 16), (2, 16)), jnp.float32)
    w_first = noise(keys[2], (27, C1, CIN), (27 * CIN) ** -0.5, 1.25, (), jnp.float32)
    w_down = noise(keys[3], (C2, C1, 2, 2, 2), (8 * C1) ** -0.5, 0.75, (), jnp.float32)
    w_coarse = noise(keys[4], (27, C2, C2), (27 * C2) ** -0.5, 0.3125, (), jnp.float32)
    w_up = noise(keys[5], (C1, C2, 2, 2, 2), C2 ** -0.5, 1.5, (), jnp.float32)
    w_joined = noise(keys[6], (27, C1, 2 * C1), (54 * C1) ** -0.5, 0.3125, (), jnp.float32)
    w_final = noise(keys[7], (CIN, C1), C1 ** -0.5, 2.0, (), jnp.float32)
    return dict(in_field=in_field, cotangent=cotangent, w_first=w_first, w_down=w_down, w_coarse=w_coarse, w_up=w_up, w_joined=w_joined, w_final=w_final)


HIGH = lax.Precision.HIGHEST
TAP_OFFSETS = [(a, b, c) for a in range(3) for b in range(3) for c in range(3)]

def conv_valid(padded, weight):
    size_x = padded.shape[1] - 2
    size_y = padded.shape[2] - 2
    size_z = padded.shape[3] - 2
    total = jnp.zeros((weight.shape[1], size_x, size_y, size_z), jnp.float32)
    for tap_index, (first, second, third) in enumerate(TAP_OFFSETS):
        view = padded[:, first:first + size_x, second:second + size_y, third:third + size_z]
        total = total + jnp.einsum('oi,ixyz->oxyz', weight[tap_index], view, precision=HIGH)
    return total

def pad_all(field):
    return jnp.pad(field, ((0, 0), (1, 1), (1, 1), (1, 1)))

def down_apply(field, weight):
    chans, size_x, size_y, size_z = field.shape
    blocks = field.reshape(chans, size_x // 2, 2, size_y // 2, 2, size_z // 2, 2)
    return jnp.einsum('oiabc,ixaybzc->oxyz', weight, blocks, precision=HIGH)

def up_apply(field, weight):
    chans, size_x, size_y, size_z = field.shape
    result = jnp.einsum('oiabc,ixyz->oxaybzc', weight, field, precision=HIGH)
    return result.reshape(weight.shape[0], 2 * size_x, 2 * size_y, 2 * size_z)

def network(in_field, w_first, w_down, w_coarse, w_up, w_joined, w_final):
    act_first = jax.nn.silu(conv_valid(pad_all(in_field), w_first))
    act_down = jax.nn.silu(down_apply(act_first, w_down))
    act_coarse = jax.nn.silu(conv_valid(pad_all(act_down), w_coarse))
    joined = jnp.concatenate([act_first, up_apply(act_coarse, w_up)], axis=0)
    act_joined = jax.nn.silu(conv_valid(pad_all(joined), w_joined))
    return jnp.einsum('oi,ixyz->oxyz', w_final, act_joined, precision=HIGH)

def reference(in_field, cotangent, w_first, w_down, w_coarse, w_up, w_joined, w_final):

    def apply_weights(first, down, coarse, upper, joined, final):
        return network(in_field, first, down, coarse, upper, joined, final)
    imitated, pullback = jax.vjp(apply_weights, w_first, w_down, w_coarse, w_up, w_joined, w_final)
    scale = 1.0 / math.sqrt(NX * NY * NZ)
    grads = pullback(cotangent * scale)
    return (imitated, grads[0], grads[1], grads[2], grads[3], grads[4], grads[5])
```

```python
import math

import jax
import jax.numpy as jnp
from jax import lax
from jax.experimental import pallas as pl
from jax.experimental.pallas import tpu as pltpu
from jax.sharding import PartitionSpec as P

F32 = jnp.float32
BF16 = jnp.bfloat16


def nn(a, b):
    return lax.dot_general(a, b, (((1,), (0,)), ((), ())), preferred_element_type=F32)


def nt(a, b):
    return lax.dot_general(a, b, (((1,), (1,)), ((), ())), preferred_element_type=F32)


def split(x):
    high = x.astype(BF16)
    return high, (x - high.astype(F32)).astype(BF16)


def rows(parts):
    return jnp.concatenate(parts, axis=0)


def lanes(parts):
    return jnp.concatenate(parts, axis=1)


def stacked(weight):
    return rows(list(split(weight)))


def mm3(both, high, low):
    count = both.shape[0] // 2
    first = nn(both, high)
    return first[:count] + first[count:] + nn(both[:count], low)


def nt3(left_high, left_low, right_high, right_low):
    count = left_high.shape[0]
    first = nt(rows([left_high, left_low]), right_high)
    return first[:count] + first[count:] + nt(left_high, right_low)


def roll(x, shift):
    shift = shift % x.shape[1]
    return x if shift == 0 else pltpu.roll(x, shift, 1)


def sigmoid(x):
    return 1.0 / (1.0 + jnp.exp(-x))


def slope(pre):
    sig = sigmoid(pre)
    return sig + pre * sig * (1.0 - sig)


def lane_of(shape):
    return lax.broadcasted_iota(jnp.int32, shape, len(shape) - 1)


def back_one(x):
    return jnp.where(lane_of(x.shape) == 0, 0.0, pltpu.roll(x, 1, 1))


def ahead_one(x):
    return jnp.where(lane_of(x.shape) == 127, 0.0, pltpu.roll(x, 127, 1))


def four_depths(field):
    count = field.shape[0]
    even, odd = field[:, :8], field[:, 8:]
    before = back_one(odd.reshape(count * 8, 128)).reshape(count, 8, 128)
    after = ahead_one(even.reshape(count * 8, 128)).reshape(count, 8, 128)
    return jnp.concatenate([before, even, odd, after], axis=1)


def three_depths(field):
    count = field.shape[0]
    flat = field.reshape(count * 16, 128)
    return jnp.concatenate(
        [back_one(flat).reshape(count, 16, 128), field, ahead_one(flat).reshape(count, 16, 128)],
        axis=1,
    )


def inside(at, extent):
    return jnp.where((at >= 0) & (at < extent), 1.0, 0.0).astype(F32)


def kernel(
    pos, fe, ce, b_first, b_down, b_down_t, b_coarse, b_coarse_t, b_up, b_up_t, b_joined, b_joined_t,
    wf_lanes, wf_col,
    img, pay,
    vh, vl, fh, fl, pre1, pdh, pdl, pre_d, rc, pre_c, ch, cl, pjh, pjl, cb, act_own, goh, gol,
    pgh, pgl, gdir, guh, gul, pch, pcl, gch, gcl, gdh, gdl,
    *, scale, size_x, size_y,
):
    px, py = pos[0], pos[1]

    z = lax.broadcasted_iota(jnp.int32, (256, 512), 0)
    col = lane_of((256, 512))
    pick = jnp.where(z == 2 * (col & 127) + (col >> 7) - 1, 1.0, 0.0).astype(BF16)
    pick_two = pick[:, 128:384]
    zt = lane_of((256, 256))
    rt = lax.broadcasted_iota(jnp.int32, (256, 256), 0)
    merge = jnp.where(zt == 2 * (rt & 127) + (rt >> 7), 1.0, 0.0).astype(BF16)

    for source, target in zip(split(fe[...].reshape(576, 256)), (vh, vl)):
        found = nn(source, pick).astype(BF16)
        for v in range(4):
            target[:, :, 16 * v : 16 * v + 16, :] = found[:, 128 * v : 128 * v + 128].reshape(18, 2, 16, 128)

    def first_rhs(ref, at, window):
        return rows([lanes([ref[2 * at + a + dx, window] for a in range(2)]) for dx in range(3)])

    base = b_first[...]
    w_first = stacked(rows([roll(base, yo + 16 * c) for yo in range(10) for c in range(2)])[:, :192])
    row_y = (lax.broadcasted_iota(jnp.int32, (160, 256), 0) >> 4) + 8 * py - 6
    lane_a = lane_of((1, 256)) >> 7
    for at in range(8):
        mask_x = inside(4 * px + 2 * (at - 3) + lane_a, size_x)
        for window in range(2):
            pre = mm3(w_first, first_rhs(vh, at, window), first_rhs(vl, at, window))
            act = pre * sigmoid(pre) * inside(row_y + 10 * window, size_y) * mask_x
            high, low = split(act)
            fh[at, 160 * window : 160 * window + 160] = high
            fl[at, 160 * window : 160 * window + 160] = low
            if at in (3, 4):
                pre1[at - 3, 160 * window : 160 * window + 160] = pre
            if 1 <= at <= 6:
                begin = 2 if window == 0 else 0
                part = act.reshape(10, 16, 256)[begin : begin + 8]
                for a in range(2):
                    high, low = split(four_depths(part[:, :, 128 * a : 128 * a + 128]))
                    pjh[at - 1, 8 * window : 8 * window + 8, 0:32, 128 * a : 128 * a + 128] = high
                    pjl[at - 1, 8 * window : 8 * window + 8, 0:32, 128 * a : 128 * a + 128] = low

    base = b_down[...]
    w_down = stacked(rows([roll(base, 32 * k) for k in range(4)]))
    row_64 = lax.broadcasted_iota(jnp.int32, (64, 256), 0) >> 4
    for pair in range(4):
        mask_x = inside(2 * px + 2 * pair + lane_a - 3, size_x // 2)
        for y0 in (0, 4, 6):
            def down_rhs(ref):
                return rows([
                    lanes([ref[2 * pair + j, 32 * y0 : 32 * y0 + 128, 128 * a : 128 * a + 128] for j in range(2)])
                    for a in range(2)
                ])
            pre = mm3(w_down, down_rhs(fh), down_rhs(fl))
            act = pre * sigmoid(pre) * inside(row_64 + y0 - 3 + 4 * py, size_y // 2) * mask_x
            for j in range(2):
                mine = slice(128 * j, 128 * j + 128)
                high, low = split(three_depths(act[:, mine].reshape(4, 16, 128)))
                pdh[2 * pair + j, y0 : y0 + 4] = high
                pdl[2 * pair + j, y0 : y0 + 4] = low
                if 2 * pair + j in (3, 4):
                    pre_d[2 * pair + j - 3, y0 : y0 + 4] = pre[:, mine].reshape(4, 16, 128)

    base = b_coarse[...]
    w_coarse = stacked(
        rows([roll(base[16 * dx : 16 * dx + 16], 48 * k) for dx in range(3) for k in range(2)])[:, :192]
    )
    for pair in range(4):
        for k in range(4):
            def coarse_rhs(ref):
                return lanes([ref[2 * pair + j, 2 * k : 2 * k + 4].reshape(192, 128) for j in range(2)])
            part = mm3(w_coarse, coarse_rhs(pdh), coarse_rhs(pdl))
            for j in range(2):
                rc[2 * pair + j, k] = part[:, 128 * j : 128 * j + 128]
    row_32 = lax.broadcasted_iota(jnp.int32, (32, 128), 0) >> 4
    for at in range(6):
        mask_x = inside(2 * px + at - 2, size_x // 2)
        for k in range(4):
            pre = rc[at, k, 0:32] + rc[at + 1, k, 32:64] + rc[at + 2, k, 64:96]
            act = pre * sigmoid(pre) * (inside(row_32 + 2 * k - 2 + 4 * py, size_y // 2) * mask_x)
            pre_c[at, 2 * k : 2 * k + 2] = pre.reshape(2, 16, 128)
            high, low = split(act)
            ch[at, 32 * k : 32 * k + 32] = high
            cl[at, 32 * k : 32 * k + 32] = low

    base = b_up[...]
    w_up_high, w_up_low = split(
        rows([roll(base[32 * a : 32 * a + 32], 16 * k) for a in range(2) for k in range(8)])
    )
    w_up_twice = lanes([w_up_high, w_up_high])
    for pair in range(3):
        high = lanes([ch[2 * pair], ch[2 * pair + 1]])
        low = lanes([cl[2 * pair], cl[2 * pair + 1]])
        part = nn(w_up_twice, rows([high, low])) + nn(w_up_low, high)
        for j in range(2):
            for a in range(2):
                mine = part[256 * a : 256 * a + 256, 128 * j : 128 * j + 128].reshape(16, 16, 128)
                high_part, low_part = split(four_depths(mine))
                pjh[2 * pair + j, :, 32:64, 128 * a : 128 * a + 128] = high_part
                pjl[2 * pair + j, :, 32:64, 128 * a : 128 * a + 128] = low_part

    cot = [nn(part, pick_two).astype(BF16).reshape(12, 16, 256) for part in split(ce[...].reshape(192, 256))]
    sel_row = lax.broadcasted_iota(jnp.int32, (224, 64), 0)
    sel_col = lane_of((224, 64)) & 31
    spread = jnp.where(sel_col == ((sel_row >> 3) & 1) * 16 + (sel_row >> 4), 1.0, 0.0).astype(BF16)
    for at in range(6):
        cb[at] = nn(
            spread,
            rows([
                lanes([part[2 * at + a, :, 128 * c : 128 * c + 128] for a in range(2)])
                for part in cot
                for c in range(2)
            ]),
        )

    base = b_joined[...]
    w_joined = stacked(
        rows([
            roll(base[8 * dx : 8 * dx + 8], 64 * b + 8 * c) for dx in range(3) for b in range(2) for c in range(2)
        ])
    )
    wf_rows = wf_col[...] * scale
    for kb in range(7):
        part = [
            mm3(
                w_joined,
                pjh[at, 2 * kb : 2 * kb + 4].reshape(256, 256),
                pjl[at, 2 * kb : 2 * kb + 4].reshape(256, 256),
            )
            for at in range(6)
        ]
        for plane in range(1, 11):
            at, a = plane // 2, plane % 2
            if a == 0:
                pre = part[at - 1][0:32, 128:256] + part[at][32:64, 0:128] + part[at][64:96, 128:256]
            else:
                pre = part[at][0:32, 0:128] + part[at][32:64, 128:256] + part[at + 1][64:96, 0:128]
            sig = sigmoid(pre)
            act = pre * sig
            grad = cb[at, 32 * kb : 32 * kb + 32, 128 * a : 128 * a + 128] * wf_rows * (sig + act * (1.0 - sig))
            high, low = split(four_depths(grad.reshape(2, 16, 128)))
            pgh[plane - 1, 2 * kb : 2 * kb + 2] = high
            pgl[plane - 1, 2 * kb : 2 * kb + 2] = low
            if at in (2, 3):
                act_own[at - 2, 32 * kb : 32 * kb + 32, 128 * a : 128 * a + 128] = act
                high, low = split(grad)
                goh[plane - 4, 32 * kb : 32 * kb + 32] = high
                gol[plane - 4, 32 * kb : 32 * kb + 32] = low

    f_row = lax.broadcasted_iota(jnp.int32, (16, 128), 0)
    f_col = lane_of((16, 128))
    w_final = stacked(
        jnp.where((f_row >> 3 == (f_col >> 3) & 1) & (f_row & 7 == f_col >> 4), wf_lanes[...], 0.0)
    )
    out_rows = []
    part_final = jnp.zeros((8, 256), F32)
    for at in range(2):
        act = act_own[at, 48:176]
        part_final = part_final + jnp.sum((act * cb[at + 2, 48:176]).reshape(16, 8, 256), axis=0)
        result = mm3(w_final, *split(act))
        for a in range(2):
            out_rows.append(lanes([result[8 * c : 8 * c + 8, 128 * a : 128 * a + 128] for c in range(2)]))
    whole = nn(stacked(rows(out_rows)), merge)
    img[...] = (whole[:32] + whole[32:]).reshape(4, 8, 256)
    part_final = jnp.sum(part_final, axis=1, keepdims=True) * scale

    nothing = jnp.zeros((32, 128), BF16)
    total = jnp.zeros((96, 256), F32)
    for at in range(1, 5):
        for k in range(4):
            def moved(ref):
                return rows([
                    lanes([
                        ref[xo, 32 * k + 48 : 32 * k + 80] if 0 <= xo < 4 else nothing
                        for xo in (2 * (at - 2) + a + 1 - dx for a in range(2))
                    ])
                    for dx in range(3)
                ])
            total = total + nt3(
                moved(goh),
                moved(gol),
                pjh[at, 2 * k + 3 : 2 * k + 7].reshape(256, 256),
                pjl[at, 2 * k + 3 : 2 * k + 7].reshape(256, 256),
            )
    part_joined = rows([
        sum(
            roll(total[32 * dx + 16 * b + 8 * c : 32 * dx + 16 * b + 8 * c + 8], -(64 * b + 8 * c))
            for b in range(2)
            for c in range(2)
        )
        for dx in range(3)
    ])

    base = b_joined_t[...]
    w_back = [
        stacked(
            rows([
                roll(base[8 * f : 8 * f + 8], 128 * a + 32 * b + 8 * c)
                for a in range(2)
                for b in range(2)
                for c in range(2)
            ])
        )
        for f in range(2)
    ]
    w_up_t = stacked(b_up_t[...][:, :64])
    for at in range(4):
        for pair in range(3):
            def back_rhs(ref):
                return rows([
                    lanes([
                        ref[2 * at + xw, 4 * pair + 2 * j : 4 * pair + 2 * j + 4].reshape(128, 128) for j in range(2)
                    ])
                    for xw in range(4)
                ])
            right_high, right_low = back_rhs(pgh), back_rhs(pgl)
            grad_up = mm3(w_back[0], right_high, right_low)
            if at in (1, 2):
                direct = mm3(w_back[1], right_high, right_low)
                for j in range(2):
                    if 1 <= 2 * pair + j <= 4:
                        gdir[at - 1, 2 * pair + j - 1] = direct[:, 128 * j : 128 * j + 128]
            high, low = split(grad_up)
            grad_act = mm3(w_up_t, high, low)
            for j in range(2):
                cell = 2 * pair + j
                mine = slice(128 * j, 128 * j + 128)
                guh[at, cell] = high[:, mine]
                gul[at, cell] = low[:, mine]
                mask = inside(2 * px + at - 1, size_x // 2) * inside(4 * py + cell - 1, size_y // 2)
                grad_pre = grad_act[:, mine] * slope(pre_c[at + 1, cell + 1]) * mask
                part_high, part_low = split(three_depths(grad_pre.reshape(1, 16, 128)))
                pch[at, cell] = part_high.reshape(48, 128)
                pcl[at, cell] = part_low.reshape(48, 128)
                if at in (1, 2) and 1 <= cell <= 4:
                    part_high, part_low = split(grad_pre)
                    gch[at - 1, cell - 1] = part_high
                    gcl[at - 1, cell - 1] = part_low

    cells = [(x, y) for x in range(2) for y in range(4)]

    def zeros(count, width):
        return jnp.zeros((count, width), BF16)

    def up_rhs(ref):
        return rows([zeros(48, 1024), lanes([ref[x + 1, y + 1] for x, y in cells]), zeros(16, 1024)])

    part_up = nt3(
        lanes([ch[x + 2, 16 * y + 32 : 16 * y + 48] for x, y in cells]),
        lanes([cl[x + 2, 16 * y + 32 : 16 * y + 48] for x, y in cells]),
        up_rhs(guh),
        up_rhs(gul),
    )

    part_coarse = jnp.zeros((16, 512), F32)
    for y in range(4):
        def around(ref):
            return rows(
                [lanes([ref[x + 2 + dx, y + 2 : y + 5].reshape(144, 128) for x in range(2)]) for dx in range(3)]
                + [zeros(80, 256)]
            )
        part_coarse = part_coarse + nt3(
            lanes([gch[x, y] for x in range(2)]), lanes([gcl[x, y] for x in range(2)]), around(pdh), around(pdl)
        )

    base = b_coarse_t[...]
    w_back_coarse = [
        stacked(rows([roll(base[:, 256 * dx : 256 * dx + 256], 48 * k) for k in range(2)])[:, :192])
        for dx in range(3)
    ]
    for k in range(2):
        grad_act = jnp.zeros((32, 256), F32)
        for dx in range(3):
            def shifted(ref):
                return lanes([ref[x + dx, 2 * k : 2 * k + 4].reshape(192, 128) for x in range(2)])
            grad_act = grad_act + mm3(w_back_coarse[dx], shifted(pch), shifted(pcl))
        for x in range(2):
            pre = pre_d[x, 2 * k + 3 : 2 * k + 5].reshape(32, 128)
            high, low = split(grad_act[:, 128 * x : 128 * x + 128] * slope(pre))
            gdh[x, 32 * k : 32 * k + 32] = high
            gdl[x, 32 * k : 32 * k + 32] = low

    def down_cells(ref):
        return lanes([ref[x, 16 * y : 16 * y + 16] for x, y in cells])

    def fine_cells(ref):
        return rows(
            [zeros(64, 1024)]
            + [
                lanes([ref[x + 3, 32 * y + 96 : 32 * y + 128, 128 * a : 128 * a + 128] for x, y in cells])
                for a in range(2)
            ]
        )

    part_down = nt3(down_cells(gdh), down_cells(gdl), fine_cells(fh), fine_cells(fl))

    base = b_down_t[...]
    right_high, right_low = lanes([gdh[0], gdh[1]]), lanes([gdl[0], gdl[1]])
    back = [
        mm3(
            stacked(rows([roll(base[32 * a : 32 * a + 32], 16 * k) for k in range(4)])[:, :64]),
            right_high,
            right_low,
        )
        for a in range(2)
    ]
    total = jnp.zeros((128, 256), F32)
    for x in range(2):
        grad = lanes([
            (rows([gdir[x, y, 32 * a : 32 * a + 32] for y in range(4)]) + back[a][:, 128 * x : 128 * x + 128])
            * slope(pre1[x, 96:224, 128 * a : 128 * a + 128])
            for a in range(2)
        ])
        high, low = split(grad)
        total = total + nt3(
            high,
            low,
            rows([first_rhs(vh, x + 3, 0), zeros(64, 256)]),
            rows([first_rhs(vl, x + 3, 0), zeros(64, 256)]),
        )
    part_first = sum(
        roll(total[16 * y + 8 * c : 16 * y + 8 * c + 8], -(6 + y + 16 * c)) for y in range(8) for c in range(2)
    )

    pay[0:16] = part_coarse[:, 0:128]
    pay[16:32] = part_coarse[:, 128:256]
    pay[32:48] = part_coarse[:, 256:384]
    pay[48:64] = part_coarse[:, 384:512] + part_up
    pay[64:88] = part_joined[:, 0:128]
    lane = lane_of((24, 128))
    pay[88:112] = jnp.where(lane < 64, part_joined[:, 128:256], 0.0) + rows([part_down, jnp.zeros((8, 128), F32)])
    pay[112:120] = part_first[:, 0:128]
    lane = lane_of((8, 128))
    pay[120:128] = jnp.where(lane == 127, part_final, jnp.where(lane < 64, part_first[:, 128:256], 0.0))


def run_kernel(args, scale, size_x, size_y):
    vmem = pl.BlockSpec(memory_space=pltpu.VMEM)

    def pair(*shape):
        return [pltpu.VMEM(shape, BF16)] * 2

    def plain(*shape):
        return [pltpu.VMEM(shape, F32)]

    scratch = (
        pair(18, 2, 64, 128)
        + pair(8, 320, 256)
        + plain(2, 320, 256)
        + pair(8, 10, 48, 128)
        + plain(2, 10, 16, 128)
        + plain(8, 4, 96, 128)
        + plain(6, 8, 16, 128)
        + pair(6, 128, 128)
        + pair(6, 16, 64, 256)
        + plain(6, 224, 256)
        + plain(2, 224, 256)
        + pair(4, 224, 128)
        + pair(10, 14, 32, 128)
        + plain(2, 4, 64, 128)
        + pair(4, 6, 64, 128)
        + pair(4, 6, 48, 128)
        + pair(2, 4, 16, 128)
        + pair(2, 64, 128)
    )

    def unet_tile(*refs):
        kernel(*refs, scale=scale, size_x=size_x, size_y=size_y)

    return pl.pallas_call(
        unet_tile,
        out_shape=(jax.ShapeDtypeStruct((4, 8, 256), F32), jax.ShapeDtypeStruct((128, 128), F32)),
        in_specs=[pl.BlockSpec(memory_space=pltpu.SMEM)] + [vmem] * (len(args) - 1),
        out_specs=(vmem, vmem),
        scratch_shapes=scratch,
        compiler_params=pltpu.CompilerParams(vmem_limit_bytes=48 * 1024 * 1024),
        cost_estimate=pl.CostEstimate(flops=3_000_000_000, bytes_accessed=2_000_000, transcendentals=2_000_000),
    )(*args)


def moved(block, axis, by):
    count = lax.axis_size(axis)
    return lax.ppermute(block, axis, [(i, i + by) for i in range(count) if 0 <= i + by < count])


def padded(block, *shape):
    return jnp.pad(block, [(0, want - have) for want, have in zip(shape, block.shape)])


def bases(w_first, w_down, w_coarse, w_up, w_joined, w_final):
    first = w_first.reshape(3, 3, 3, 8).transpose(3, 0, 2, 1)
    first = padded(first, 8, 4, 4, 16).reshape(8, 256)
    down = padded(w_down.transpose(0, 2, 3, 4, 1).reshape(16, 2, 32), 16, 2, 128).reshape(16, 256)
    down_t = padded(w_down.transpose(2, 3, 4, 1, 0).reshape(64, 16), 64, 128)
    coarse = w_coarse.reshape(3, 3, 3, 16, 16)
    coarse_out = padded(coarse.transpose(0, 3, 1, 2, 4).reshape(48, 144), 48, 256)
    coarse_t = coarse[::-1, ::-1, ::-1].transpose(4, 0, 1, 2, 3).reshape(16, 3, 144)
    coarse_t = padded(coarse_t, 16, 3, 256).reshape(16, 768)
    up = padded(w_up.transpose(2, 3, 4, 0, 1).reshape(64, 16), 64, 128)
    up_t = padded(w_up.transpose(1, 2, 3, 4, 0).reshape(16, 64), 16, 128)
    joined = w_joined.reshape(3, 3, 3, 8, 2, 8)
    joined_out = padded(joined.transpose(0, 3, 1, 4, 2, 5), 3, 8, 4, 2, 4, 8).reshape(24, 256)
    joined_t = joined[::-1, ::-1, ::-1, :, ::-1].transpose(4, 5, 0, 1, 2, 3)
    joined_t = padded(joined_t, 2, 8, 4, 4, 4, 8).reshape(16, 512)
    wf_lanes = jnp.tile(w_final, (1, 16))
    wf_col = jnp.tile(w_final.reshape(8, 1), (4, 1))
    return [first, down, down_t, coarse_out, coarse_t, up, up_t, joined_out, joined_t, wf_lanes, wf_col]


def shards(in_field, cotangent, w_first, w_down, w_coarse, w_up, w_joined, w_final):
    size_x, size_y = 4 * lax.axis_size("gx"), 8 * lax.axis_size("gy")
    field, cot = in_field[0], cotangent[0]
    both = jnp.concatenate([field, cot], axis=0)
    left, right = moved(both, "gx", 1), moved(both, "gx", -1)
    far_left, far_right = moved(field[1:], "gx", 2), moved(field[:3], "gx", -2)
    wide = jnp.concatenate([far_left, left[:4], field, right[:4], far_right], axis=0)
    wide_cot = jnp.concatenate([left[4:], cot, right[4:]], axis=0)

    def packed(part, part_cot):
        return jnp.concatenate([part.reshape(126, 256), part_cot.reshape(36, 256)], axis=0)

    before = moved(packed(wide[:, 1:], wide_cot[:, 5:]), "gy", 1)
    after = moved(packed(wide[:, :7], wide_cot[:, :3]), "gy", -1)
    fe = jnp.concatenate([before[:126].reshape(18, 7, 256), wide, after[:126].reshape(18, 7, 256)], axis=1)
    fe = jnp.pad(fe, ((0, 0), (0, 4), (0, 0)))
    fe = jnp.stack([fe[:, 0:16], fe[:, 10:26]], axis=1)
    ce = jnp.concatenate([before[126:].reshape(12, 3, 256), wide_cot, after[126:].reshape(12, 3, 256)], axis=1)
    ce = jnp.pad(ce, ((0, 0), (0, 2), (0, 0)))

    pos = jnp.stack([lax.axis_index("gx"), lax.axis_index("gy")]).astype(jnp.int32)
    scale = 1.0 / math.sqrt(size_x * size_y * in_field.shape[3])
    args = [pos, fe, ce] + bases(w_first, w_down, w_coarse, w_up, w_joined, w_final)
    imitated, pay = run_kernel(args, scale, size_x, size_y)

    count_x, count_y = lax.axis_size("gx"), lax.axis_size("gy")
    pay = pay.reshape(count_y, 128 // count_y, 128)
    pay = jnp.sum(lax.all_to_all(pay, "gy", 0, 0), axis=0)
    pay = jnp.broadcast_to(pay, (count_x,) + pay.shape)
    pay = jnp.sum(lax.all_to_all(pay, "gx", 0, 0), axis=0)
    pay = jnp.broadcast_to(pay, (count_y,) + pay.shape)
    pay = lax.all_to_all(pay, "gy", 0, 0).reshape(128, 128)

    block = jnp.concatenate([pay[0:16], pay[16:32], pay[32:48], pay[48:64]], axis=1)
    grad_coarse = block[:, :432].reshape(16, 27, 16).transpose(1, 0, 2)
    grad_up = block[:, 432:496].reshape(16, 2, 2, 2, 8).transpose(4, 0, 1, 2, 3)
    block = jnp.concatenate([pay[64:88], pay[88:112]], axis=1)
    grad_joined = block.reshape(3, 8, 4, 2, 4, 8)[:, :, :3, :, :3].transpose(0, 2, 4, 1, 3, 5).reshape(27, 8, 16)
    grad_down = block[:16, 192:].reshape(16, 2, 2, 2, 8).transpose(0, 4, 1, 2, 3)
    block = jnp.concatenate([pay[112:120], pay[120:128]], axis=1)
    grad_first = block.reshape(8, 4, 4, 16)[:, :3, :3, :3].transpose(1, 3, 2, 0).reshape(27, 8, 1)
    grad_final = block[:, 255].reshape(1, 8)
    return imitated[None], grad_first, grad_down, grad_coarse, grad_up, grad_joined, grad_final


def solution(mesh):
    in_specs = (P(None, "gx", "gy", None), P(None, "gx", "gy", None), P(), P(), P(), P(), P(), P())
    out_specs = (P(None, "gx", "gy", None), P(), P(), P(), P(), P(), P())
    return jax.shard_map(shards, mesh=mesh, in_specs=in_specs, out_specs=out_specs, check_vma=False)
```

```python
import math

import jax
import jax.numpy as jnp
from jax import lax
from jax.experimental import pallas as pl
from jax.experimental.pallas import tpu as pltpu
from jax.sharding import PartitionSpec as P

F32 = jnp.float32
BF16 = jnp.bfloat16


def nn(a, b):
    return lax.dot_general(a, b, (((1,), (0,)), ((), ())), preferred_element_type=F32)


def nt(a, b):
    return lax.dot_general(a, b, (((1,), (1,)), ((), ())), preferred_element_type=F32)


def split(x):
    high = x.astype(BF16)
    return high, (x - high.astype(F32)).astype(BF16)


def rows(parts):
    return jnp.concatenate(parts, axis=0)


def lanes(parts):
    return jnp.concatenate(parts, axis=1)


def stacked(weight):
    return rows(list(split(weight)))


def mm3(both, high, low):
    count = both.shape[0] // 2
    first = nn(both, high)
    return first[:count] + first[count:] + nn(both[:count], low)


def nt3(left_high, left_low, right_high, right_low):
    count = left_high.shape[0]
    first = nt(rows([left_high, left_low]), right_high)
    return first[:count] + first[count:] + nt(left_high, right_low)


def roll(x, shift):
    shift = shift % x.shape[1]
    return x if shift == 0 else pltpu.roll(x, shift, 1)


def sigmoid(x):
    return 1.0 / (1.0 + jnp.exp(-x))


def lane_of(shape):
    return lax.broadcasted_iota(jnp.int32, shape, len(shape) - 1)


def back_one(x):
    return jnp.where(lane_of(x.shape) == 0, 0.0, pltpu.roll(x, 1, 1))


def ahead_one(x):
    return jnp.where(lane_of(x.shape) == 127, 0.0, pltpu.roll(x, 127, 1))


def four_depths(field):
    count = field.shape[0]
    even, odd = field[:, :8], field[:, 8:]
    before = back_one(odd.reshape(count * 8, 128)).reshape(count, 8, 128)
    after = ahead_one(even.reshape(count * 8, 128)).reshape(count, 8, 128)
    return jnp.concatenate([before, even, odd, after], axis=1)


def three_depths(field):
    count = field.shape[0]
    flat = field.reshape(count * 16, 128)
    return jnp.concatenate(
        [back_one(flat).reshape(count, 16, 128), field, ahead_one(flat).reshape(count, 16, 128)],
        axis=1,
    )


def inside(at, extent):
    return jnp.where((at >= 0) & (at < extent), 1.0, 0.0).astype(F32)


def plane_of(field, near, far, even_x, even_far):
    def plane(x):
        if 5 <= x < 9:
            return field[x - 5]
        pair, even, at = (far, even_far, 0) if x in (0, 13) else (near, even_x, x - 1 if x < 5 else x - 9)
        below = x < 5
        return jnp.where(even, pair[1 if below else 0][at], pair[0 if below else 1][at])

    return plane


def strips(pos, field, near_0, near_1, far_0, far_1, out_0, out_1):
    px, py = pos[0], pos[1]
    even_y = (py & 1) == 0
    plane = plane_of(field, (near_0, near_1), (far_0, far_1), (px & 1) == 0, ((px >> 1) & 1) == 0)
    for x in range(14):
        own = plane(x)
        low, high = own[0:5], own[3:8]
        out_0[5 * x : 5 * x + 5] = jnp.where(even_y, high, low)
        out_1[5 * x : 5 * x + 5] = jnp.where(even_y, low, high)


def run_strips(args):
    vmem = pl.BlockSpec(memory_space=pltpu.VMEM)
    return pl.pallas_call(
        strips,
        out_shape=(jax.ShapeDtypeStruct((70, 256), F32),) * 2,
        in_specs=[pl.BlockSpec(memory_space=pltpu.SMEM)] + [vmem] * (len(args) - 1),
        out_specs=(vmem, vmem),
    )(*args)


def kernel(
    pos, field, near_0, near_1, far_0, far_1, beside_0, beside_1, cot,
    b_first, b_down, b_down_t, b_coarse, b_coarse_t, b_up, b_up_t, b_joined, b_joined_t, wf_lanes, wf_col,
    img, pay,
    fe, vh, vl, fh, fl, slope_f, pdh, pdl, slope_d, rc, slope_c, ch, cl, pjh, pjl, act_own, goh, gol,
    pgh, pgl, gdir, guh, gul, pch, pcl, gch, gcl, rd, gdh, gdl,
    *, scale, size_x, size_y,
):
    px, py = pos[0], pos[1]

    z = lax.broadcasted_iota(jnp.int32, (256, 512), 0)
    col = lane_of((256, 512))
    pick = jnp.where(z == 2 * (col & 127) + (col >> 7) - 1, 1.0, 0.0).astype(BF16)
    pick_two = pick[:, 128:384]
    zt = lane_of((256, 256))
    rt = lax.broadcasted_iota(jnp.int32, (256, 256), 0)
    merge = jnp.where(zt == 2 * (rt & 127) + (rt >> 7), 1.0, 0.0).astype(BF16)

    even_x, even_far, even_y = (px & 1) == 0, ((px >> 1) & 1) == 0, (py & 1) == 0
    plane = plane_of(field, (near_0, near_1), (far_0, far_1), even_x, even_far)
    has_head, has_tail = inside(8 * py - 1, size_y), inside(8 * py + 8, size_y)
    for x in range(14):
        own = plane(x)
        first, second = beside_0[5 * x : 5 * x + 5], beside_1[5 * x : 5 * x + 5]
        head, tail = jnp.where(even_y, second, first), jnp.where(even_y, first, second)
        there = inside(4 * px + x - 5, size_x)
        head, own, tail = head * (there * has_head), own * there, tail * (there * has_tail)
        fe[x, 0] = rows([head, own, tail[0:3]])
        fe[x, 1] = rows([own[3:8], tail, jnp.zeros((6, 256), F32)])
    for source, target in zip(split(fe[...].reshape(448, 256)), (vh, vl)):
        found = nn(source, pick).astype(BF16)
        for v in range(4):
            target[:, :, 16 * v : 16 * v + 16, :] = found[:, 128 * v : 128 * v + 128].reshape(14, 2, 16, 128)

    def first_rhs(ref, at, window):
        return rows([lanes([ref[2 * at + a + dx, window] for a in range(2)]) for dx in range(3)])

    base = b_first[...]
    w_first = stacked(rows([roll(base, yo + 16 * c) for yo in range(8) for c in range(2)])[:, :192])
    row_y = (lax.broadcasted_iota(jnp.int32, (128, 256), 0) >> 4) + 8 * py - 4
    lane_a = lane_of((1, 256)) >> 7
    for at in range(6):
        mask_x = inside(4 * px + 2 * (at - 2) + lane_a, size_x)
        for window in range(2):
            mine = slice(128 * window, 128 * window + 128)
            pre = mm3(w_first, first_rhs(vh, at, window), first_rhs(vl, at, window))
            mask = inside(row_y + 8 * window, size_y) * mask_x
            sig = sigmoid(pre)
            act = pre * sig
            slope_f[at, mine] = (sig + act * (1.0 - sig)) * mask
            act = act * mask
            high, low = split(act)
            fh[at, mine] = high
            fl[at, mine] = low
            part = act.reshape(8, 16, 256)[2:8] if window == 0 else act.reshape(8, 16, 256)[0:6]
            for a in range(2):
                plane = 2 * (at - 1) + a - 1
                if 0 <= plane < 6:
                    half = slice(128 * (plane % 2), 128 * (plane % 2) + 128)
                    high, low = split(four_depths(part[:, :, 128 * a : 128 * a + 128]))
                    pjh[plane // 2, 6 * window : 6 * window + 6, 0:32, half] = high
                    pjl[plane // 2, 6 * window : 6 * window + 6, 0:32, half] = low

    base = b_down[...]
    w_down = stacked(rows([roll(base, 32 * k) for k in range(4)]))
    row_64 = lax.broadcasted_iota(jnp.int32, (64, 256), 0) >> 4
    for pair in range(3):
        mask_x = inside(2 * px + 2 * pair + lane_a - 2, size_x // 2)
        for y0 in (0, 4):
            def down_rhs(ref):
                return rows([
                    lanes([ref[2 * pair + j, 32 * y0 : 32 * y0 + 128, 128 * a : 128 * a + 128] for j in range(2)])
                    for a in range(2)
                ])
            pre = mm3(w_down, down_rhs(fh), down_rhs(fl))
            mask = inside(row_64 + y0 - 2 + 4 * py, size_y // 2) * mask_x
            sig = sigmoid(pre)
            act = pre * sig
            sloped = (sig + act * (1.0 - sig)) * mask
            act = act * mask
            for j in range(2):
                mine = slice(128 * j, 128 * j + 128)
                high, low = split(three_depths(act[:, mine].reshape(4, 16, 128)))
                pdh[2 * pair + j, y0 : y0 + 4] = high
                pdl[2 * pair + j, y0 : y0 + 4] = low
                slope_d[2 * pair + j, 16 * y0 : 16 * y0 + 64] = sloped[:, mine]

    base = b_coarse[...]
    w_coarse = stacked(
        rows([roll(base[16 * dx : 16 * dx + 16], 48 * k) for dx in range(3) for k in range(2)])[:, :192]
    )
    for pair in range(3):
        for k in range(3):
            def coarse_rhs(ref):
                return lanes([ref[2 * pair + j, 2 * k : 2 * k + 4].reshape(192, 128) for j in range(2)])
            part = mm3(w_coarse, coarse_rhs(pdh), coarse_rhs(pdl))
            for j in range(2):
                rc[2 * pair + j, k] = part[:, 128 * j : 128 * j + 128]
    row_32 = lax.broadcasted_iota(jnp.int32, (32, 128), 0) >> 4
    for at in range(4):
        mask_x = inside(2 * px + at - 1, size_x // 2)
        for k in range(3):
            mine = slice(32 * k, 32 * k + 32)
            pre = rc[at, k, 0:32] + rc[at + 1, k, 32:64] + rc[at + 2, k, 64:96]
            mask = inside(row_32 + 2 * k - 1 + 4 * py, size_y // 2) * mask_x
            sig = sigmoid(pre)
            act = pre * sig
            slope_c[at, mine] = (sig + act * (1.0 - sig)) * mask
            high, low = split(act * mask)
            ch[at, mine] = high
            cl[at, mine] = low

    base = b_up[...]
    w_up_high, w_up_low = split(
        rows([roll(base[32 * a : 32 * a + 32], 16 * k) for a in range(2) for k in range(6)])[:, :96]
    )
    for pair in range(2):
        high = lanes([ch[2 * pair], ch[2 * pair + 1]])
        low = lanes([cl[2 * pair], cl[2 * pair + 1]])
        part = nn(w_up_high, high) + nn(w_up_low, high) + nn(w_up_high, low)
        for j in range(2):
            for a in range(2):
                plane = 2 * (2 * pair + j) + a - 1
                if 0 <= plane < 6:
                    half = slice(128 * (plane % 2), 128 * (plane % 2) + 128)
                    mine = part[192 * a : 192 * a + 192, 128 * j : 128 * j + 128].reshape(12, 16, 128)
                    high_part, low_part = split(four_depths(mine))
                    pjh[plane // 2, :, 32:64, half] = high_part
                    pjl[plane // 2, :, 32:64, half] = low_part

    found = nn(rows(list(split(cot[...].reshape(32, 256)))), pick_two)
    sel_row = lax.broadcasted_iota(jnp.int32, (128, 32), 0)
    sel_col = lane_of((128, 32)) & 15
    spread = jnp.where(sel_col == ((sel_row >> 3) & 1) * 8 + (sel_row >> 4), 1.0, 0.0).astype(BF16)
    cb = [
        nn(
            spread,
            rows([
                lanes([
                    found[32 * s + 16 * at + 8 * a : 32 * s + 16 * at + 8 * a + 8, 128 * c : 128 * c + 128]
                    for a in range(2)
                ])
                for s in range(2)
                for c in range(2)
            ]).astype(BF16),
        )
        for at in range(2)
    ]

    base = b_joined[...]
    w_joined = stacked(
        rows([
            roll(base[8 * dx : 8 * dx + 8], 64 * b + 8 * c) for dx in range(3) for b in range(2) for c in range(2)
        ])
    )
    wf_rows = wf_col[...] * scale
    for x in range(4):
        for ref in (pgh, pgl):
            ref[x, 0:3] = jnp.zeros((3, 32, 128), BF16)
            ref[x, 11:14] = jnp.zeros((3, 32, 128), BF16)

    def around_pair(ref, pair, k):
        return ref[pair, 2 * k + 1 : 2 * k + 5].reshape(256, 256)

    for k in range(4):
        part = [mm3(w_joined, around_pair(pjh, pair, k), around_pair(pjl, pair, k)) for pair in range(3)]
        for x in range(4):
            pre = sum(
                part[(x + dx) // 2][32 * dx : 32 * dx + 32, 128 * ((x + dx) % 2) : 128 * ((x + dx) % 2) + 128]
                for dx in range(3)
            )
            at, half = x // 2, slice(128 * (x % 2), 128 * (x % 2) + 128)
            mine = slice(32 * k, 32 * k + 32)
            sig = sigmoid(pre)
            act = pre * sig
            grad = cb[at][mine, half] * wf_rows * (sig + act * (1.0 - sig))
            high, low = split(four_depths(grad.reshape(2, 16, 128)))
            pgh[x, 2 * k + 3 : 2 * k + 5] = high
            pgl[x, 2 * k + 3 : 2 * k + 5] = low
            act_own[at, mine, half] = act
            high, low = split(grad)
            goh[x, mine] = high
            gol[x, mine] = low

    f_row = lax.broadcasted_iota(jnp.int32, (16, 128), 0)
    f_col = lane_of((16, 128))
    w_final = stacked(
        jnp.where((f_row >> 3 == (f_col >> 3) & 1) & (f_row & 7 == f_col >> 4), wf_lanes[...], 0.0)
    )
    out_rows = []
    part_final = jnp.zeros((8, 256), F32)
    for at in range(2):
        act = act_own[at]
        part_final = part_final + jnp.sum((act * cb[at]).reshape(16, 8, 256), axis=0)
        result = mm3(w_final, *split(act))
        for a in range(2):
            out_rows.append(lanes([result[8 * c : 8 * c + 8, 128 * a : 128 * a + 128] for c in range(2)]))
    whole = nn(stacked(rows(out_rows)), merge)
    img[...] = (whole[:32] + whole[32:]).reshape(4, 8, 256)
    part_final = jnp.sum(part_final, axis=1, keepdims=True) * scale

    nothing = jnp.zeros((32, 128), BF16)
    total = jnp.zeros((96, 256), F32)
    for pair in range(3):
        for k in range(4):
            def moved_rows(ref):
                return rows([
                    lanes([
                        ref[2 * pair + j - dx, 32 * k : 32 * k + 32] if 0 <= 2 * pair + j - dx < 4 else nothing
                        for j in range(2)
                    ])
                    for dx in range(3)
                ])
            total = total + nt3(
                moved_rows(goh), moved_rows(gol), around_pair(pjh, pair, k), around_pair(pjl, pair, k)
            )
    part_joined = rows([
        sum(
            roll(total[32 * dx + 16 * b + 8 * c : 32 * dx + 16 * b + 8 * c + 8], -(64 * b + 8 * c))
            for b in range(2)
            for c in range(2)
        )
        for dx in range(3)
    ])

    base = b_joined_t[...]
    w_back = stacked(
        rows([
            roll(base[8 * f : 8 * f + 8], 128 * a + 32 * b + 8 * c)
            for f in range(2)
            for a in range(2)
            for b in range(2)
            for c in range(2)
        ])
    )
    w_up_t = stacked(b_up_t[...][:, :64])
    for ref in (pch, pcl):
        for at in range(4):
            ref[at, 0:2] = jnp.zeros((2, 48, 128), BF16)
            ref[at, 8:10] = jnp.zeros((2, 48, 128), BF16)
    for at in range(4):
        planes = [(2 * at - 3 + xw, xw) for xw in range(4) if 0 <= 2 * at - 3 + xw < 4]
        weight = w_back[:, 128 * planes[0][1] : 128 * planes[-1][1] + 128]
        for pair in range(3):
            def back_rhs(ref):
                return rows([
                    lanes([ref[x, 4 * pair + 2 * j : 4 * pair + 2 * j + 4].reshape(128, 128) for j in range(2)])
                    for x, _ in planes
                ])
            result = mm3(weight, back_rhs(pgh), back_rhs(pgl))
            high, low = split(result[:64])
            grad_act = mm3(w_up_t, high, low)
            for j in range(2):
                cell = 2 * pair + j
                mine = slice(128 * j, 128 * j + 128)
                gdir[at, cell] = result[64:, mine]
                guh[at, 64 * cell : 64 * cell + 64] = high[:, mine]
                gul[at, 64 * cell : 64 * cell + 64] = low[:, mine]
                grad_pre = grad_act[:, mine] * slope_c[at, 16 * cell : 16 * cell + 16]
                part_high, part_low = split(three_depths(grad_pre.reshape(1, 16, 128)))
                pch[at, cell + 2] = part_high.reshape(48, 128)
                pcl[at, cell + 2] = part_low.reshape(48, 128)
                part_high, part_low = split(grad_pre)
                gch[at, 16 * cell : 16 * cell + 16] = part_high
                gcl[at, 16 * cell : 16 * cell + 16] = part_low

    total = jnp.zeros((384, 96), F32)
    for pair in range(2):
        def two(ref):
            return lanes([ref[2 * pair], ref[2 * pair + 1]])
        total = total + nt3(two(guh), two(gul), two(ch), two(cl))
    total = lanes([total, jnp.zeros((384, 32), F32)])
    part_up = sum(roll(total[64 * y : 64 * y + 64], -16 * y) for y in range(6))

    nothing = jnp.zeros((96, 128), BF16)
    total = jnp.zeros((288, 384), F32)
    for pair in range(3):
        def moved_cells(ref):
            return rows([
                lanes([ref[2 * pair + j - dx] if 0 <= 2 * pair + j - dx < 4 else nothing for j in range(2)])
                for dx in range(3)
            ])
        def plane_pair(ref):
            return lanes([ref[2 * pair + j].reshape(384, 128) for j in range(2)])
        total = total + nt3(moved_cells(gch), moved_cells(gcl), plane_pair(pdh), plane_pair(pdl))
    lane_512 = lane_of((1, 512))
    tap, chan = lane_512 & 31, lane_512 >> 5
    tap_y = (tap * 11) >> 5
    row_256 = lax.broadcasted_iota(jnp.int32, (256, 512), 0)
    to_taps = jnp.where(row_256 == jnp.where(tap < 9, 16 * tap + chan, -1), 1.0, 0.0).astype(BF16)
    parts = [
        sum(roll(total[96 * dx + 16 * y : 96 * dx + 16 * y + 16], -48 * y) for y in range(6))[:, 0:256]
        for dx in range(3)
    ]
    part_coarse = by_tap(parts, to_taps)
    key = 64 * tap_y + 32 * (chan >> 3) + 8 * (tap - 3 * tap_y) + (chan & 7)
    to_taps = jnp.where(row_256 == jnp.where(tap < 9, key, -1), 1.0, 0.0).astype(BF16)
    part_joined = by_tap([part_joined[8 * dx : 8 * dx + 8] for dx in range(3)], to_taps)

    base = b_coarse_t[...]
    w_back_coarse = stacked(
        rows([
            roll(base[:, 256 * dx : 256 * dx + 256], 48 * k) for dx in range(3) for k in range(2)
        ])[:, :192]
    )
    for pair in range(2):
        for k in range(4):
            def shifted(ref):
                return lanes([ref[2 * pair + j, 2 * k : 2 * k + 4].reshape(192, 128) for j in range(2)])
            part = mm3(w_back_coarse, shifted(pch), shifted(pcl))
            for j in range(2):
                rd[2 * pair + j, k] = part[:, 128 * j : 128 * j + 128]
    for at in range(6):
        for k in range(4):
            mine = slice(32 * k, 32 * k + 32)
            grad = sum(rd[at - 2 + dx, k, 32 * dx : 32 * dx + 32] for dx in range(3) if 0 <= at - 2 + dx < 4)
            high, low = split(grad * slope_d[at, mine])
            gdh[at, mine] = high
            gdl[at, mine] = low

    total = jnp.zeros((512, 128), F32)
    for pair in range(3):
        def cells(ref):
            return lanes([ref[2 * pair], ref[2 * pair + 1]])
        def fine(ref):
            return rows([lanes([ref[2 * pair + j, :, 128 * a : 128 * a + 128] for j in range(2)]) for a in range(2)])
        total = total + nt3(fine(fh), fine(fl), cells(gdh), cells(gdl))
    part_down = rows([
        sum(roll(total[256 * a + 32 * y : 256 * a + 32 * y + 32], -16 * y) for y in range(8)) for a in range(2)
    ])

    base = b_down_t[...]
    w_back_down = stacked(
        rows([roll(base[32 * a : 32 * a + 32], 16 * k) for a in range(2) for k in range(4)])[:, :64]
    )
    total = jnp.zeros((128, 256), F32)
    for pair in range(3):
        for window in range(2):
            mine = slice(64 * window, 64 * window + 64)
            back = mm3(
                w_back_down,
                lanes([gdh[2 * pair, mine], gdh[2 * pair + 1, mine]]),
                lanes([gdl[2 * pair, mine], gdl[2 * pair + 1, mine]]),
            )
            for j in range(2):
                at = 2 * pair + j
                halves = []
                for a in range(2):
                    half = back[128 * a : 128 * a + 128, 128 * j : 128 * j + 128]
                    if 1 <= at <= 4:
                        blocks = [
                            gdir[at - 1, y - 1, 32 * a : 32 * a + 32] if 1 <= y <= 6 else jnp.zeros((32, 128), F32)
                            for y in range(4 * window, 4 * window + 4)
                        ]
                        half = half + rows(blocks)
                    halves.append(half)
                high, low = split(lanes(halves) * slope_f[at, 128 * window : 128 * window + 128])
                pad = jnp.zeros((64, 256), BF16)
                total = total + nt3(
                    high, low, rows([first_rhs(vh, at, window), pad]), rows([first_rhs(vl, at, window), pad])
                )
    part_first = sum(
        roll(total[16 * y + 8 * c : 16 * y + 8 * c + 8], -(y + 16 * c)) for y in range(8) for c in range(2)
    )

    tap = lane_of((1, 128))
    tap_x = (tap * 57) >> 9
    tap_y = ((tap - 9 * tap_x) * 11) >> 5
    key = jnp.where(tap < 27, 64 * tap_x + 16 * (tap - 9 * tap_x - 3 * tap_y) + tap_y, -1)
    row_256 = lax.broadcasted_iota(jnp.int32, (256, 128), 0)
    part_first = exact(part_first, jnp.where(row_256 == key, 1.0, 0.0).astype(BF16))
    for m in range(4):
        pay[16 * m : 16 * m + 16] = part_coarse[:, 128 * m : 128 * m + 128]
        pay[64 + 8 * m : 72 + 8 * m] = part_joined[:, 128 * m : 128 * m + 128]
    lane = lane_of((16, 128))
    pay[96:112] = sum(
        roll(jnp.where(lane < 16, part[16 * m : 16 * m + 16], 0.0), 32 * m + at)
        for m in range(4)
        for part, at in ((part_down, 0), (part_up, 16))
    )
    lane, row = lane_of((8, 128)), lax.broadcasted_iota(jnp.int32, (8, 128), 0)
    pay[112:120] = part_first + jnp.where(lane == 64 + row, part_final, 0.0)


def exact(block, choice):
    high, low = split(block)
    rest = (block - high.astype(F32) - low.astype(F32)).astype(BF16)
    count = block.shape[0]
    found = nn(jnp.concatenate([high.astype(F32), low.astype(F32), rest.astype(F32)], axis=0).astype(BF16), choice)
    return found[:count] + found[count : 2 * count] + found[2 * count :]


def by_tap(parts, choice):
    return sum(roll(exact(part, choice), 9 * dx) for dx, part in enumerate(parts))


def outputs(*refs):
    blocks, (coarse, joined, first, down, up, final) = refs[:-6], refs[-6:]
    total = [ref[...] for ref in blocks]
    while len(total) > 1:
        total = [total[i] + total[i + 1] for i in range(0, len(total), 2)]
    total = total[0]

    def slot(start, count, at, width):
        block = total[start : start + count]
        return roll(block, -at)[:, :width]

    for i in range(16):
        coarse[:, i, :] = slot(16 * (i // 4), 16, 32 * (i % 4), 27)
        joined[:, i, :] = slot(64 + 8 * (i // 4), 8, 32 * (i % 4), 27)
    for k in range(8):
        down[:, k // 2, k % 2, :] = slot(96 + 8 * (k % 2), 8, 32 * (k // 2), 16)
        up[:, k // 2, k % 2, :] = slot(96 + 8 * (k % 2), 8, 32 * (k // 2) + 16, 16)
    first[:, 0, :] = total[112:120, :27]
    lane, row = lane_of((8, 128)), lax.broadcasted_iota(jnp.int32, (8, 128), 0)
    row_sum = jnp.sum(jnp.where(lane == 64 + row, total[112:120], 0.0), axis=0, keepdims=True)
    final[...] = roll(row_sum, -64)[:, :8]


def run_outputs(blocks):
    vmem = pl.BlockSpec(memory_space=pltpu.VMEM)
    shapes = ((16, 16, 27), (8, 16, 27), (8, 1, 27), (8, 4, 2, 16), (8, 4, 2, 16), (1, 8))
    return pl.pallas_call(
        outputs,
        out_shape=tuple(jax.ShapeDtypeStruct(shape, F32) for shape in shapes),
        in_specs=[vmem] * len(blocks),
        out_specs=(vmem,) * len(shapes),
    )(*blocks)


def run_kernel(args, scale, size_x, size_y):
    vmem = pl.BlockSpec(memory_space=pltpu.VMEM)

    def pair(*shape):
        return [pltpu.VMEM(shape, BF16)] * 2

    def plain(*shape):
        return [pltpu.VMEM(shape, F32)]

    scratch = (
        plain(14, 2, 16, 256)
        + pair(14, 2, 64, 128)
        + pair(6, 256, 256)
        + plain(6, 256, 256)
        + pair(6, 8, 48, 128)
        + plain(6, 128, 128)
        + plain(6, 3, 96, 128)
        + plain(4, 96, 128)
        + pair(4, 96, 128)
        + pair(3, 12, 64, 256)
        + plain(2, 128, 256)
        + pair(4, 128, 128)
        + pair(4, 14, 32, 128)
        + plain(4, 6, 64, 128)
        + pair(4, 384, 128)
        + pair(4, 10, 48, 128)
        + pair(4, 96, 128)
        + plain(4, 4, 96, 128)
        + pair(6, 128, 128)
    )

    def unet_tile(*refs):
        kernel(*refs, scale=scale, size_x=size_x, size_y=size_y)

    return pl.pallas_call(
        unet_tile,
        out_shape=(jax.ShapeDtypeStruct((4, 8, 256), F32), jax.ShapeDtypeStruct((120, 128), F32)),
        in_specs=[pl.BlockSpec(memory_space=pltpu.SMEM)] + [vmem] * (len(args) - 1),
        out_specs=(vmem, vmem),
        scratch_shapes=scratch,
        compiler_params=pltpu.CompilerParams(vmem_limit_bytes=48 * 1024 * 1024),
        cost_estimate=pl.CostEstimate(flops=3_000_000_000, bytes_accessed=2_000_000, transcendentals=2_000_000),
    )(*args)


def swap(first, second, axis, by):
    count = lax.axis_size(axis)

    def pairs(parity):
        return [(i, (i + (by if (i // by) % 2 == parity else -by)) % count) for i in range(count)]

    return lax.ppermute(first, axis, pairs(0)), lax.ppermute(second, axis, pairs(1))


def rounds(count):
    return [[k * by for k in (1, 2, 3) if k * by < count] for by in (1, 4, 16, 64) if by < count]


def padded(block, *shape):
    return jnp.pad(block, [(0, want - have) for want, have in zip(shape, block.shape)])


def bases(w_first, w_down, w_coarse, w_up, w_joined, w_final):
    first = w_first.reshape(3, 3, 3, 8).transpose(3, 0, 2, 1)
    first = padded(first, 8, 4, 4, 16).reshape(8, 256)
    down = padded(w_down.transpose(0, 2, 3, 4, 1).reshape(16, 2, 32), 16, 2, 128).reshape(16, 256)
    down_t = padded(w_down.transpose(2, 3, 4, 1, 0).reshape(64, 16), 64, 128)
    coarse = w_coarse.reshape(3, 3, 3, 16, 16)
    coarse_out = padded(coarse.transpose(0, 3, 1, 2, 4).reshape(48, 144), 48, 256)
    coarse_t = coarse[::-1, ::-1, ::-1].transpose(4, 0, 1, 2, 3).reshape(16, 3, 144)
    coarse_t = padded(coarse_t, 16, 3, 256).reshape(16, 768)
    up = padded(w_up.transpose(2, 3, 4, 0, 1).reshape(64, 16), 64, 128)
    up_t = padded(w_up.transpose(1, 2, 3, 4, 0).reshape(16, 64), 16, 128)
    joined = w_joined.reshape(3, 3, 3, 8, 2, 8)
    joined_out = padded(joined.transpose(0, 3, 1, 4, 2, 5), 3, 8, 4, 2, 4, 8).reshape(24, 256)
    joined_t = joined[::-1, ::-1, ::-1, :, ::-1].transpose(4, 5, 0, 1, 2, 3)
    joined_t = padded(joined_t, 2, 8, 4, 4, 4, 8).reshape(16, 512)
    wf_lanes = jnp.tile(w_final, (1, 16))
    wf_col = jnp.tile(w_final.reshape(8, 1), (4, 1))
    return [first, down, down_t, coarse_out, coarse_t, up, up_t, joined_out, joined_t, wf_lanes, wf_col]


def shards(in_field, cotangent, w_first, w_down, w_coarse, w_up, w_joined, w_final):
    size_x, size_y = 4 * lax.axis_size("gx"), 8 * lax.axis_size("gy")
    field, cot = in_field[0], cotangent[0]
    weights = bases(w_first, w_down, w_coarse, w_up, w_joined, w_final)
    pos = jnp.stack([lax.axis_index("gx"), lax.axis_index("gy")]).astype(jnp.int32)
    even = ((lax.axis_index("gx") >> 1) & 1) == 0
    low, high = field[:1], field[3:]
    far = swap(jnp.where(even, high, low), jnp.where(even, low, high), "gx", 2)
    near = swap(field, field, "gx", 1)
    near, far, weights, pos = lax.optimization_barrier((near, far, weights, pos))
    args = [pos, field, *near, *far]
    beside = swap(*run_strips(args), "gy", 1)

    scale = 1.0 / math.sqrt(size_x * size_y * in_field.shape[3])
    imitated, pay = run_kernel([*args, *beside, cot, *weights], scale, size_x, size_y)

    blocks = [pay]
    for axis in ("gy", "gx"):
        count = lax.axis_size(axis)
        for partners in rounds(count):
            while len(blocks) > 1:
                blocks = [blocks[i] + blocks[i + 1] for i in range(0, len(blocks), 2)]
            mine = blocks[0]
            blocks = [mine] + [lax.ppermute(mine, axis, [(i, i ^ k) for i in range(count)]) for k in partners]
    coarse, joined, first, down, up, final = run_outputs(blocks)
    return (
        imitated[None],
        first.transpose(2, 0, 1),
        down.reshape(8, 2, 2, 2, 16).transpose(4, 0, 1, 2, 3),
        coarse.transpose(2, 0, 1),
        up.reshape(8, 2, 2, 2, 16).transpose(0, 4, 1, 2, 3),
        joined.transpose(2, 0, 1),
        final,
    )


def solution(mesh):
    in_specs = (P(None, "gx", "gy", None), P(None, "gx", "gy", None), P(), P(), P(), P(), P(), P())
    out_specs = (P(None, "gx", "gy", None), P(), P(), P(), P(), P(), P())
    return jax.shard_map(shards, mesh=mesh, in_specs=in_specs, out_specs=out_specs, check_vma=False)
```

```python
import math

import jax
import jax.numpy as jnp
from jax import lax
from jax.experimental import pallas as pl
from jax.experimental.pallas import tpu as pltpu
from jax.sharding import PartitionSpec as P

F32 = jnp.float32
BF16 = jnp.bfloat16


def nn(a, b):
    return lax.dot_general(a, b, (((1,), (0,)), ((), ())), preferred_element_type=F32)


def nt(a, b):
    return lax.dot_general(a, b, (((1,), (1,)), ((), ())), preferred_element_type=F32)


def split(x):
    high = x.astype(BF16)
    return high, (x - high.astype(F32)).astype(BF16)


def rows(parts):
    return jnp.concatenate(parts, axis=0)


def lanes(parts):
    return jnp.concatenate(parts, axis=1)


def stacked(weight):
    return rows(list(split(weight)))


def mm3(both, high, low):
    count = both.shape[0] // 2
    first = nn(both, high)
    return first[:count] + first[count:] + nn(both[:count], low)


def nt3(left_high, left_low, right_high, right_low):
    count = left_high.shape[0]
    first = nt(rows([left_high, left_low]), right_high)
    return first[:count] + first[count:] + nt(left_high, right_low)


def roll(x, shift):
    shift = shift % x.shape[1]
    return x if shift == 0 else pltpu.roll(x, shift, 1)


def sigmoid(x):
    return 1.0 / (1.0 + jnp.exp(-x))


def lane_of(shape):
    return lax.broadcasted_iota(jnp.int32, shape, len(shape) - 1)


def back_one(x):
    return jnp.where(lane_of(x.shape) == 0, 0.0, pltpu.roll(x, 1, 1))


def ahead_one(x):
    return jnp.where(lane_of(x.shape) == 127, 0.0, pltpu.roll(x, 127, 1))


def four_depths(field):
    count = field.shape[0]
    even, odd = field[:, :8], field[:, 8:]
    before = back_one(odd.reshape(count * 8, 128)).reshape(count, 8, 128)
    after = ahead_one(even.reshape(count * 8, 128)).reshape(count, 8, 128)
    return jnp.concatenate([before, even, odd, after], axis=1)


def three_depths(field):
    count = field.shape[0]
    flat = field.reshape(count * 16, 128)
    return jnp.concatenate(
        [back_one(flat).reshape(count, 16, 128), field, ahead_one(flat).reshape(count, 16, 128)],
        axis=1,
    )


def inside(at, extent):
    return jnp.where((at >= 0) & (at < extent), 1.0, 0.0).astype(F32)


def plane_of(field, near, far, even_x, even_far):
    def plane(x):
        if 5 <= x < 9:
            return field[x - 5]
        pair, even, at = (far, even_far, 0) if x in (0, 13) else (near, even_x, x - 1 if x < 5 else x - 9)
        below = x < 5
        return jnp.where(even, pair[1 if below else 0][at], pair[0 if below else 1][at])

    return plane


def strips(pos, field, near_0, near_1, far_0, far_1, wide, out_0, out_1):
    px, py = pos[0], pos[1]
    even_y = (py & 1) == 0
    plane = plane_of(field, (near_0, near_1), (far_0, far_1), (px & 1) == 0, ((px >> 1) & 1) == 0)
    for x in range(14):
        own = plane(x)
        wide[x] = own
        low, high = own[0:5], own[3:8]
        out_0[5 * x : 5 * x + 5] = jnp.where(even_y, high, low)
        out_1[5 * x : 5 * x + 5] = jnp.where(even_y, low, high)


def run_strips(args):
    vmem = pl.BlockSpec(memory_space=pltpu.VMEM)
    return pl.pallas_call(
        strips,
        out_shape=tuple(jax.ShapeDtypeStruct(shape, F32) for shape in ((14, 8, 256), (70, 256), (70, 256))),
        in_specs=[pl.BlockSpec(memory_space=pltpu.SMEM)] + [vmem] * (len(args) - 1),
        out_specs=(vmem,) * 3,
        compiler_params=pltpu.CompilerParams(vmem_limit_bytes=4 * 1024 * 1024),
    )(*args)


def kernel(
    pos, wide, beside_0, beside_1, cot,
    b_first, b_down, b_down_t, b_coarse, b_coarse_t, b_up, b_up_t, b_joined, b_joined_t, wf_lanes, wf_col,
    img, pay,
    fe, vh, vl, fh, fl, slope_f, pdh, pdl, slope_d, rc, slope_c, ch, cl, pjh, pjl, act_own, goh, gol,
    pgh, pgl, gdir, guh, gul, pch, pcl, gch, gcl, rd, gdh, gdl,
    *, scale, size_x, size_y,
):
    px, py = pos[0], pos[1]

    z = lax.broadcasted_iota(jnp.int32, (256, 512), 0)
    col = lane_of((256, 512))
    pick = jnp.where(z == 2 * (col & 127) + (col >> 7) - 1, 1.0, 0.0).astype(BF16)
    pick_two = pick[:, 128:384]
    zt = lane_of((256, 256))
    rt = lax.broadcasted_iota(jnp.int32, (256, 256), 0)
    merge = jnp.where(zt == 2 * (rt & 127) + (rt >> 7), 1.0, 0.0).astype(BF16)

    even_y = (py & 1) == 0
    has_head, has_tail = inside(8 * py - 1, size_y), inside(8 * py + 8, size_y)
    for x in range(14):
        own = wide[x]
        first, second = beside_0[5 * x : 5 * x + 5], beside_1[5 * x : 5 * x + 5]
        head, tail = jnp.where(even_y, second, first), jnp.where(even_y, first, second)
        there = inside(4 * px + x - 5, size_x)
        head, own, tail = head * (there * has_head), own * there, tail * (there * has_tail)
        fe[x, 0] = rows([head, own, tail[0:3]])
        fe[x, 1] = rows([own[3:8], tail, jnp.zeros((6, 256), F32)])
    for source, target in zip(split(fe[...].reshape(448, 256)), (vh, vl)):
        found = nn(source, pick).astype(BF16)
        for v in range(4):
            target[:, :, 16 * v : 16 * v + 16, :] = found[:, 128 * v : 128 * v + 128].reshape(14, 2, 16, 128)

    def first_rhs(ref, at, window):
        return rows([lanes([ref[2 * at + a + dx, window] for a in range(2)]) for dx in range(3)])

    base = b_first[...]
    w_first = stacked(rows([roll(base, yo + 16 * c) for yo in range(8) for c in range(2)])[:, :192])
    row_y = (lax.broadcasted_iota(jnp.int32, (128, 256), 0) >> 4) + 8 * py - 4
    lane_a = lane_of((1, 256)) >> 7
    for at in range(6):
        mask_x = inside(4 * px + 2 * (at - 2) + lane_a, size_x)
        for window in range(2):
            mine = slice(128 * window, 128 * window + 128)
            pre = mm3(w_first, first_rhs(vh, at, window), first_rhs(vl, at, window))
            mask = inside(row_y + 8 * window, size_y) * mask_x
            sig = sigmoid(pre)
            act = pre * sig
            slope_f[at, mine] = (sig + act * (1.0 - sig)) * mask
            act = act * mask
            high, low = split(act)
            fh[at, mine] = high
            fl[at, mine] = low
            part = act.reshape(8, 16, 256)[2:8] if window == 0 else act.reshape(8, 16, 256)[0:6]
            for a in range(2):
                plane = 2 * (at - 1) + a - 1
                if 0 <= plane < 6:
                    half = slice(128 * (plane % 2), 128 * (plane % 2) + 128)
                    high, low = split(four_depths(part[:, :, 128 * a : 128 * a + 128]))
                    pjh[plane // 2, 6 * window : 6 * window + 6, 0:32, half] = high
                    pjl[plane // 2, 6 * window : 6 * window + 6, 0:32, half] = low

    base = b_down[...]
    w_down = stacked(rows([roll(base, 32 * k) for k in range(4)]))
    row_64 = lax.broadcasted_iota(jnp.int32, (64, 256), 0) >> 4
    for pair in range(3):
        mask_x = inside(2 * px + 2 * pair + lane_a - 2, size_x // 2)
        for y0 in (0, 4):
            def down_rhs(ref):
                return rows([
                    lanes([ref[2 * pair + j, 32 * y0 : 32 * y0 + 128, 128 * a : 128 * a + 128] for j in range(2)])
                    for a in range(2)
                ])
            pre = mm3(w_down, down_rhs(fh), down_rhs(fl))
            mask = inside(row_64 + y0 - 2 + 4 * py, size_y // 2) * mask_x
            sig = sigmoid(pre)
            act = pre * sig
            sloped = (sig + act * (1.0 - sig)) * mask
            act = act * mask
            for j in range(2):
                mine = slice(128 * j, 128 * j + 128)
                high, low = split(three_depths(act[:, mine].reshape(4, 16, 128)))
                pdh[2 * pair + j, y0 : y0 + 4] = high
                pdl[2 * pair + j, y0 : y0 + 4] = low
                slope_d[2 * pair + j, 16 * y0 : 16 * y0 + 64] = sloped[:, mine]

    base = b_coarse[...]
    w_coarse = stacked(
        rows([roll(base[16 * dx : 16 * dx + 16], 48 * k) for dx in range(3) for k in range(2)])[:, :192]
    )
    for pair in range(3):
        for k in range(3):
            def coarse_rhs(ref):
                return lanes([ref[2 * pair + j, 2 * k : 2 * k + 4].reshape(192, 128) for j in range(2)])
            part = mm3(w_coarse, coarse_rhs(pdh), coarse_rhs(pdl))
            for j in range(2):
                rc[2 * pair + j, k] = part[:, 128 * j : 128 * j + 128]
    row_32 = lax.broadcasted_iota(jnp.int32, (32, 128), 0) >> 4
    for at in range(4):
        mask_x = inside(2 * px + at - 1, size_x // 2)
        for k in range(3):
            mine = slice(32 * k, 32 * k + 32)
            pre = rc[at, k, 0:32] + rc[at + 1, k, 32:64] + rc[at + 2, k, 64:96]
            mask = inside(row_32 + 2 * k - 1 + 4 * py, size_y // 2) * mask_x
            sig = sigmoid(pre)
            act = pre * sig
            slope_c[at, mine] = (sig + act * (1.0 - sig)) * mask
            high, low = split(act * mask)
            ch[at, mine] = high
            cl[at, mine] = low

    base = b_up[...]
    w_up_high, w_up_low = split(
        rows([roll(base[32 * a : 32 * a + 32], 16 * k) for a in range(2) for k in range(6)])[:, :96]
    )
    for pair in range(2):
        high = lanes([ch[2 * pair], ch[2 * pair + 1]])
        low = lanes([cl[2 * pair], cl[2 * pair + 1]])
        part = nn(w_up_high, high) + nn(w_up_low, high) + nn(w_up_high, low)
        for j in range(2):
            for a in range(2):
                plane = 2 * (2 * pair + j) + a - 1
                if 0 <= plane < 6:
                    half = slice(128 * (plane % 2), 128 * (plane % 2) + 128)
                    mine = part[192 * a : 192 * a + 192, 128 * j : 128 * j + 128].reshape(12, 16, 128)
                    high_part, low_part = split(four_depths(mine))
                    pjh[plane // 2, :, 32:64, half] = high_part
                    pjl[plane // 2, :, 32:64, half] = low_part

    found = nn(rows(list(split(cot[...].reshape(32, 256)))), pick_two)
    sel_row = lax.broadcasted_iota(jnp.int32, (128, 32), 0)
    sel_col = lane_of((128, 32)) & 15
    spread = jnp.where(sel_col == ((sel_row >> 3) & 1) * 8 + (sel_row >> 4), 1.0, 0.0).astype(BF16)
    cb = [
        nn(
            spread,
            rows([
                lanes([
                    found[32 * s + 16 * at + 8 * a : 32 * s + 16 * at + 8 * a + 8, 128 * c : 128 * c + 128]
                    for a in range(2)
                ])
                for s in range(2)
                for c in range(2)
            ]).astype(BF16),
        )
        for at in range(2)
    ]

    base = b_joined[...]
    w_joined = stacked(
        rows([
            roll(base[8 * dx : 8 * dx + 8], 64 * b + 8 * c) for dx in range(3) for b in range(2) for c in range(2)
        ])
    )
    wf_rows = wf_col[...] * scale
    for x in range(4):
        for ref in (pgh, pgl):
            ref[x, 0:3] = jnp.zeros((3, 32, 128), BF16)
            ref[x, 11:14] = jnp.zeros((3, 32, 128), BF16)

    def around_pair(ref, pair, k):
        return ref[pair, 2 * k + 1 : 2 * k + 5].reshape(256, 256)

    for k in range(4):
        part = [mm3(w_joined, around_pair(pjh, pair, k), around_pair(pjl, pair, k)) for pair in range(3)]
        for x in range(4):
            pre = sum(
                part[(x + dx) // 2][32 * dx : 32 * dx + 32, 128 * ((x + dx) % 2) : 128 * ((x + dx) % 2) + 128]
                for dx in range(3)
            )
            at, half = x // 2, slice(128 * (x % 2), 128 * (x % 2) + 128)
            mine = slice(32 * k, 32 * k + 32)
            sig = sigmoid(pre)
            act = pre * sig
            grad = cb[at][mine, half] * wf_rows * (sig + act * (1.0 - sig))
            high, low = split(four_depths(grad.reshape(2, 16, 128)))
            pgh[x, 2 * k + 3 : 2 * k + 5] = high
            pgl[x, 2 * k + 3 : 2 * k + 5] = low
            act_own[at, mine, half] = act
            high, low = split(grad)
            goh[x, mine] = high
            gol[x, mine] = low

    f_row = lax.broadcasted_iota(jnp.int32, (16, 128), 0)
    f_col = lane_of((16, 128))
    w_final = stacked(
        jnp.where((f_row >> 3 == (f_col >> 3) & 1) & (f_row & 7 == f_col >> 4), wf_lanes[...], 0.0)
    )
    out_rows = []
    part_final = jnp.zeros((8, 256), F32)
    for at in range(2):
        act = act_own[at]
        part_final = part_final + jnp.sum((act * cb[at]).reshape(16, 8, 256), axis=0)
        result = mm3(w_final, *split(act))
        for a in range(2):
            out_rows.append(lanes([result[8 * c : 8 * c + 8, 128 * a : 128 * a + 128] for c in range(2)]))
    whole = nn(stacked(rows(out_rows)), merge)
    img[...] = (whole[:32] + whole[32:]).reshape(4, 8, 256)
    part_final = jnp.sum(part_final, axis=1, keepdims=True) * scale

    nothing = jnp.zeros((32, 128), BF16)
    total = jnp.zeros((96, 256), F32)
    for pair in range(3):
        for k in range(4):
            def moved_rows(ref):
                return rows([
                    lanes([
                        ref[2 * pair + j - dx, 32 * k : 32 * k + 32] if 0 <= 2 * pair + j - dx < 4 else nothing
                        for j in range(2)
                    ])
                    for dx in range(3)
                ])
            total = total + nt3(
                moved_rows(goh), moved_rows(gol), around_pair(pjh, pair, k), around_pair(pjl, pair, k)
            )
    part_joined = rows([
        sum(
            roll(total[32 * dx + 16 * b + 8 * c : 32 * dx + 16 * b + 8 * c + 8], -(64 * b + 8 * c))
            for b in range(2)
            for c in range(2)
        )
        for dx in range(3)
    ])

    base = b_joined_t[...]
    w_back = stacked(
        rows([
            roll(base[8 * f : 8 * f + 8], 128 * a + 32 * b + 8 * c)
            for f in range(2)
            for a in range(2)
            for b in range(2)
            for c in range(2)
        ])
    )
    w_up_t = stacked(b_up_t[...][:, :64])
    for ref in (pch, pcl):
        for at in range(4):
            ref[at, 0:2] = jnp.zeros((2, 48, 128), BF16)
            ref[at, 8:10] = jnp.zeros((2, 48, 128), BF16)
    for at in range(4):
        planes = [(2 * at - 3 + xw, xw) for xw in range(4) if 0 <= 2 * at - 3 + xw < 4]
        weight = w_back[:, 128 * planes[0][1] : 128 * planes[-1][1] + 128]
        for pair in range(3):
            def back_rhs(ref):
                return rows([
                    lanes([ref[x, 4 * pair + 2 * j : 4 * pair + 2 * j + 4].reshape(128, 128) for j in range(2)])
                    for x, _ in planes
                ])
            result = mm3(weight, back_rhs(pgh), back_rhs(pgl))
            high, low = split(result[:64])
            grad_act = mm3(w_up_t, high, low)
            for j in range(2):
                cell = 2 * pair + j
                mine = slice(128 * j, 128 * j + 128)
                gdir[at, cell] = result[64:, mine]
                guh[at, 64 * cell : 64 * cell + 64] = high[:, mine]
                gul[at, 64 * cell : 64 * cell + 64] = low[:, mine]
                grad_pre = grad_act[:, mine] * slope_c[at, 16 * cell : 16 * cell + 16]
                part_high, part_low = split(three_depths(grad_pre.reshape(1, 16, 128)))
                pch[at, cell + 2] = part_high.reshape(48, 128)
                pcl[at, cell + 2] = part_low.reshape(48, 128)
                part_high, part_low = split(grad_pre)
                gch[at, 16 * cell : 16 * cell + 16] = part_high
                gcl[at, 16 * cell : 16 * cell + 16] = part_low

    total = jnp.zeros((384, 96), F32)
    for pair in range(2):
        def two(ref):
            return lanes([ref[2 * pair], ref[2 * pair + 1]])
        total = total + nt3(two(guh), two(gul), two(ch), two(cl))
    total = lanes([total, jnp.zeros((384, 32), F32)])
    part_up = sum(roll(total[64 * y : 64 * y + 64], -16 * y) for y in range(6))

    nothing = jnp.zeros((96, 128), BF16)
    total = jnp.zeros((288, 384), F32)
    for pair in range(3):
        def moved_cells(ref):
            return rows([
                lanes([ref[2 * pair + j - dx] if 0 <= 2 * pair + j - dx < 4 else nothing for j in range(2)])
                for dx in range(3)
            ])
        def plane_pair(ref):
            return lanes([ref[2 * pair + j].reshape(384, 128) for j in range(2)])
        total = total + nt3(moved_cells(gch), moved_cells(gcl), plane_pair(pdh), plane_pair(pdl))
    lane_512 = lane_of((1, 512))
    tap, chan = lane_512 & 31, lane_512 >> 5
    tap_y = (tap * 11) >> 5
    row_256 = lax.broadcasted_iota(jnp.int32, (256, 512), 0)
    to_taps = jnp.where(row_256 == jnp.where(tap < 9, 16 * tap + chan, -1), 1.0, 0.0).astype(BF16)
    parts = [
        sum(roll(total[96 * dx + 16 * y : 96 * dx + 16 * y + 16], -48 * y) for y in range(6))[:, 0:256]
        for dx in range(3)
    ]
    part_coarse = by_tap(parts, to_taps)
    key = 64 * tap_y + 32 * (chan >> 3) + 8 * (tap - 3 * tap_y) + (chan & 7)
    to_taps = jnp.where(row_256 == jnp.where(tap < 9, key, -1), 1.0, 0.0).astype(BF16)
    part_joined = by_tap([part_joined[8 * dx : 8 * dx + 8] for dx in range(3)], to_taps)

    base = b_coarse_t[...]
    w_back_coarse = stacked(
        rows([
            roll(base[:, 256 * dx : 256 * dx + 256], 48 * k) for dx in range(3) for k in range(2)
        ])[:, :192]
    )
    for pair in range(2):
        for k in range(4):
            def shifted(ref):
                return lanes([ref[2 * pair + j, 2 * k : 2 * k + 4].reshape(192, 128) for j in range(2)])
            part = mm3(w_back_coarse, shifted(pch), shifted(pcl))
            for j in range(2):
                rd[2 * pair + j, k] = part[:, 128 * j : 128 * j + 128]
    for at in range(6):
        for k in range(4):
            mine = slice(32 * k, 32 * k + 32)
            grad = sum(rd[at - 2 + dx, k, 32 * dx : 32 * dx + 32] for dx in range(3) if 0 <= at - 2 + dx < 4)
            high, low = split(grad * slope_d[at, mine])
            gdh[at, mine] = high
            gdl[at, mine] = low

    total = jnp.zeros((512, 128), F32)
    for pair in range(3):
        def cells(ref):
            return lanes([ref[2 * pair], ref[2 * pair + 1]])
        def fine(ref):
            return rows([lanes([ref[2 * pair + j, :, 128 * a : 128 * a + 128] for j in range(2)]) for a in range(2)])
        total = total + nt3(fine(fh), fine(fl), cells(gdh), cells(gdl))
    part_down = rows([
        sum(roll(total[256 * a + 32 * y : 256 * a + 32 * y + 32], -16 * y) for y in range(8)) for a in range(2)
    ])

    base = b_down_t[...]
    w_back_down = stacked(
        rows([roll(base[32 * a : 32 * a + 32], 16 * k) for a in range(2) for k in range(4)])[:, :64]
    )
    total = jnp.zeros((128, 256), F32)
    for pair in range(3):
        for window in range(2):
            mine = slice(64 * window, 64 * window + 64)
            back = mm3(
                w_back_down,
                lanes([gdh[2 * pair, mine], gdh[2 * pair + 1, mine]]),
                lanes([gdl[2 * pair, mine], gdl[2 * pair + 1, mine]]),
            )
            for j in range(2):
                at = 2 * pair + j
                halves = []
                for a in range(2):
                    half = back[128 * a : 128 * a + 128, 128 * j : 128 * j + 128]
                    if 1 <= at <= 4:
                        blocks = [
                            gdir[at - 1, y - 1, 32 * a : 32 * a + 32] if 1 <= y <= 6 else jnp.zeros((32, 128), F32)
                            for y in range(4 * window, 4 * window + 4)
                        ]
                        half = half + rows(blocks)
                    halves.append(half)
                high, low = split(lanes(halves) * slope_f[at, 128 * window : 128 * window + 128])
                pad = jnp.zeros((64, 256), BF16)
                total = total + nt3(
                    high, low, rows([first_rhs(vh, at, window), pad]), rows([first_rhs(vl, at, window), pad])
                )
    part_first = sum(
        roll(total[16 * y + 8 * c : 16 * y + 8 * c + 8], -(y + 16 * c)) for y in range(8) for c in range(2)
    )

    tap = lane_of((1, 128))
    tap_x = (tap * 57) >> 9
    tap_y = ((tap - 9 * tap_x) * 11) >> 5
    key = jnp.where(tap < 27, 64 * tap_x + 16 * (tap - 9 * tap_x - 3 * tap_y) + tap_y, -1)
    row_256 = lax.broadcasted_iota(jnp.int32, (256, 128), 0)
    part_first = exact(part_first, jnp.where(row_256 == key, 1.0, 0.0).astype(BF16))
    for m in range(4):
        pay[16 * m : 16 * m + 16] = part_coarse[:, 128 * m : 128 * m + 128]
        pay[64 + 8 * m : 72 + 8 * m] = part_joined[:, 128 * m : 128 * m + 128]
    lane = lane_of((16, 128))
    pay[96:112] = sum(
        roll(jnp.where(lane < 16, part[16 * m : 16 * m + 16], 0.0), 32 * m + at)
        for m in range(4)
        for part, at in ((part_down, 0), (part_up, 16))
    )
    lane, row = lane_of((8, 128)), lax.broadcasted_iota(jnp.int32, (8, 128), 0)
    pay[112:120] = part_first + jnp.where(lane == 64 + row, part_final, 0.0)


def exact(block, choice):
    high, low = split(block)
    rest = (block - high.astype(F32) - low.astype(F32)).astype(BF16)
    count = block.shape[0]
    found = nn(jnp.concatenate([high.astype(F32), low.astype(F32), rest.astype(F32)], axis=0).astype(BF16), choice)
    return found[:count] + found[count : 2 * count] + found[2 * count :]


def by_tap(parts, choice):
    return sum(roll(exact(part, choice), 9 * dx) for dx, part in enumerate(parts))


def outputs(*refs):
    blocks, (coarse, joined, first, down, up, final) = refs[:-6], refs[-6:]
    total = [ref[...] for ref in blocks]
    while len(total) > 1:
        total = [total[i] + total[i + 1] for i in range(0, len(total), 2)]
    total = total[0]

    def slot(start, count, at, width):
        block = total[start : start + count]
        return roll(block, -at)[:, :width]

    for i in range(16):
        coarse[:, i, :] = slot(16 * (i // 4), 16, 32 * (i % 4), 27)
        joined[:, i, :] = slot(64 + 8 * (i // 4), 8, 32 * (i % 4), 27)
    for k in range(8):
        down[:, k // 2, k % 2, :] = slot(96 + 8 * (k % 2), 8, 32 * (k // 2), 16)
        up[:, k // 2, k % 2, :] = slot(96 + 8 * (k % 2), 8, 32 * (k // 2) + 16, 16)
    first[:, 0, :] = total[112:120, :27]
    lane, row = lane_of((8, 128)), lax.broadcasted_iota(jnp.int32, (8, 128), 0)
    row_sum = jnp.sum(jnp.where(lane == 64 + row, total[112:120], 0.0), axis=0, keepdims=True)
    final[...] = roll(row_sum, -64)[:, :8]


def run_outputs(blocks):
    vmem = pl.BlockSpec(memory_space=pltpu.VMEM)
    shapes = ((16, 16, 27), (8, 16, 27), (8, 1, 27), (8, 4, 2, 16), (8, 4, 2, 16), (1, 8))
    return pl.pallas_call(
        outputs,
        out_shape=tuple(jax.ShapeDtypeStruct(shape, F32) for shape in shapes),
        in_specs=[vmem] * len(blocks),
        out_specs=(vmem,) * len(shapes),
        compiler_params=pltpu.CompilerParams(vmem_limit_bytes=4 * 1024 * 1024),
    )(*blocks)


def run_kernel(args, scale, size_x, size_y):
    vmem = pl.BlockSpec(memory_space=pltpu.VMEM)

    def pair(*shape):
        return [pltpu.VMEM(shape, BF16)] * 2

    def plain(*shape):
        return [pltpu.VMEM(shape, F32)]

    scratch = (
        plain(14, 2, 16, 256)
        + pair(14, 2, 64, 128)
        + pair(6, 256, 256)
        + plain(6, 256, 256)
        + pair(6, 8, 48, 128)
        + plain(6, 128, 128)
        + plain(6, 3, 96, 128)
        + plain(4, 96, 128)
        + pair(4, 96, 128)
        + pair(3, 12, 64, 256)
        + plain(2, 128, 256)
        + pair(4, 128, 128)
        + pair(4, 14, 32, 128)
        + plain(4, 6, 64, 128)
        + pair(4, 384, 128)
        + pair(4, 10, 48, 128)
        + pair(4, 96, 128)
        + plain(4, 4, 96, 128)
        + pair(6, 128, 128)
    )

    def unet_tile(*refs):
        kernel(*refs, scale=scale, size_x=size_x, size_y=size_y)

    return pl.pallas_call(
        unet_tile,
        out_shape=(jax.ShapeDtypeStruct((4, 8, 256), F32), jax.ShapeDtypeStruct((120, 128), F32)),
        in_specs=[pl.BlockSpec(memory_space=pltpu.SMEM)] + [vmem] * (len(args) - 1),
        out_specs=(vmem, vmem),
        scratch_shapes=scratch,
        compiler_params=pltpu.CompilerParams(vmem_limit_bytes=48 * 1024 * 1024),
        cost_estimate=pl.CostEstimate(flops=3_000_000_000, bytes_accessed=2_000_000, transcendentals=2_000_000),
    )(*args)


def swap(first, second, axis, by):
    count = lax.axis_size(axis)

    def pairs(parity):
        return [(i, (i + (by if (i // by) % 2 == parity else -by)) % count) for i in range(count)]

    return lax.ppermute(first, axis, pairs(0)), lax.ppermute(second, axis, pairs(1))


def rounds(count, apart):
    groups = [[k * by for k in (1, 2, 3) if k * by < count] for by in (1, 4, 16, 64) if by < count]
    if apart and len(groups[0]) == 3:
        groups = [[1], [3]] + groups[1:]
    return groups


def padded(block, *shape):
    return jnp.pad(block, [(0, want - have) for want, have in zip(shape, block.shape)])


def bases_now(w_first, w_joined, w_final):
    first = w_first.reshape(3, 3, 3, 8).transpose(3, 0, 2, 1)
    first = padded(first, 8, 4, 4, 16).reshape(8, 256)
    joined = w_joined.reshape(3, 3, 3, 8, 2, 8)
    joined_out = padded(joined.transpose(0, 3, 1, 4, 2, 5), 3, 8, 4, 2, 4, 8).reshape(24, 256)
    joined_t = joined[::-1, ::-1, ::-1, :, ::-1].transpose(4, 5, 0, 1, 2, 3)
    joined_t = padded(joined_t, 2, 8, 4, 4, 4, 8).reshape(16, 512)
    wf_lanes = jnp.tile(w_final, (1, 16))
    wf_col = jnp.tile(w_final.reshape(8, 1), (4, 1))
    return first, joined_out, joined_t, wf_lanes, wf_col


def bases_later(w_down, w_coarse, w_up):
    down = padded(w_down.transpose(0, 2, 3, 4, 1).reshape(16, 2, 32), 16, 2, 128).reshape(16, 256)
    down_t = padded(w_down.transpose(2, 3, 4, 1, 0).reshape(64, 16), 64, 128)
    coarse = w_coarse.reshape(3, 3, 3, 16, 16)
    coarse_out = padded(coarse.transpose(0, 3, 1, 2, 4).reshape(48, 144), 48, 256)
    coarse_t = coarse[::-1, ::-1, ::-1].transpose(4, 0, 1, 2, 3).reshape(16, 3, 144)
    coarse_t = padded(coarse_t, 16, 3, 256).reshape(16, 768)
    up = padded(w_up.transpose(2, 3, 4, 0, 1).reshape(64, 16), 64, 128)
    up_t = padded(w_up.transpose(1, 2, 3, 4, 0).reshape(16, 64), 16, 128)
    return down, down_t, coarse_out, coarse_t, up, up_t


def shards(in_field, cotangent, w_first, w_down, w_coarse, w_up, w_joined, w_final):
    size_x, size_y = 4 * lax.axis_size("gx"), 8 * lax.axis_size("gy")
    field, cot = in_field[0], cotangent[0]
    now = bases_now(w_first, w_joined, w_final)
    pos = jnp.stack([lax.axis_index("gx"), lax.axis_index("gy")]).astype(jnp.int32)
    even = ((lax.axis_index("gx") >> 1) & 1) == 0
    low, high = field[:1], field[3:]
    far = swap(jnp.where(even, high, low), jnp.where(even, low, high), "gx", 2)
    near = swap(field, field, "gx", 1)
    near, far, now, pos, (w_down, w_coarse, w_up) = lax.optimization_barrier(
        (near, far, now, pos, (w_down, w_coarse, w_up))
    )
    wide, *sent = run_strips([pos, field, *near, *far])
    beside = swap(*sent, "gy", 1)
    first, joined_out, joined_t, wf_lanes, wf_col = now
    later = bases_later(w_down, w_coarse, w_up)
    weights = [first, *later, joined_out, joined_t, wf_lanes, wf_col]

    scale = 1.0 / math.sqrt(size_x * size_y * in_field.shape[3])
    imitated, pay = run_kernel([pos, wide, *beside, cot, *weights], scale, size_x, size_y)

    blocks = [pay]
    for axis in ("gy", "gx"):
        count = lax.axis_size(axis)
        for partners in rounds(count, axis == "gx"):
            while len(blocks) > 1:
                blocks = [blocks[i] + blocks[i + 1] for i in range(0, len(blocks), 2)]
            mine = blocks[0]
            blocks = [mine] + [lax.ppermute(mine, axis, [(i, i ^ k) for i in range(count)]) for k in partners]
    coarse, joined, first, down, up, final = run_outputs(blocks)
    return (
        imitated[None],
        first.transpose(2, 0, 1),
        down.reshape(8, 2, 2, 2, 16).transpose(4, 0, 1, 2, 3),
        coarse.transpose(2, 0, 1),
        up.reshape(8, 2, 2, 2, 16).transpose(0, 4, 1, 2, 3),
        joined.transpose(2, 0, 1),
        final,
    )


def solution(mesh):
    in_specs = (P(None, "gx", "gy", None), P(None, "gx", "gy", None), P(), P(), P(), P(), P(), P())
    out_specs = (P(None, "gx", "gy", None), P(), P(), P(), P(), P(), P())
    return jax.shard_map(shards, mesh=mesh, in_specs=in_specs, out_specs=out_specs, check_vma=False)
```

```python
import math

import jax
import jax.numpy as jnp
from jax import lax
from jax.experimental import pallas as pl
from jax.experimental.pallas import tpu as pltpu
from jax.sharding import PartitionSpec as P

F32 = jnp.float32
BF16 = jnp.bfloat16


def nn(a, b):
    return lax.dot_general(a, b, (((1,), (0,)), ((), ())), preferred_element_type=F32)


def nt(a, b):
    return lax.dot_general(a, b, (((1,), (1,)), ((), ())), preferred_element_type=F32)


def split(x):
    high = x.astype(BF16)
    return high, (x - high.astype(F32)).astype(BF16)


def rows(parts):
    return jnp.concatenate(parts, axis=0)


def lanes(parts):
    return jnp.concatenate(parts, axis=1)


def stacked(weight):
    return rows(list(split(weight)))


def mm3(both, high, low):
    count = both.shape[0] // 2
    first = nn(both, high)
    return first[:count] + first[count:] + nn(both[:count], low)


def nt3(left_high, left_low, right_high, right_low):
    count = left_high.shape[0]
    first = nt(rows([left_high, left_low]), right_high)
    return first[:count] + first[count:] + nt(left_high, right_low)


def thrice(base, depth):
    high, low = split(base)
    high = high.astype(F32)
    return high + roll(high, depth) + roll(low.astype(F32), 2 * depth)


def wider(base):
    return lanes([base, jnp.zeros((base.shape[0], 256 - base.shape[1]), F32)])


def roll(x, shift):
    shift = shift % x.shape[1]
    return x if shift == 0 else pltpu.roll(x, shift, 1)


def sigmoid(x):
    return 1.0 / (1.0 + jnp.exp(-x))


def lane_of(shape):
    return lax.broadcasted_iota(jnp.int32, shape, len(shape) - 1)


def back_one(x):
    return jnp.where(lane_of(x.shape) == 0, 0.0, pltpu.roll(x, 1, 1))


def ahead_one(x):
    return jnp.where(lane_of(x.shape) == 127, 0.0, pltpu.roll(x, 127, 1))


def four_depths(field):
    count = field.shape[0]
    even, odd = field[:, :8], field[:, 8:]
    before = back_one(odd.reshape(count * 8, 128)).reshape(count, 8, 128)
    after = ahead_one(even.reshape(count * 8, 128)).reshape(count, 8, 128)
    return jnp.concatenate([before, even, odd, after], axis=1)


def three_depths(field):
    count = field.shape[0]
    flat = field.reshape(count * 16, 128)
    return jnp.concatenate(
        [back_one(flat).reshape(count, 16, 128), field, ahead_one(flat).reshape(count, 16, 128)],
        axis=1,
    )


def inside(at, extent):
    return jnp.where((at >= 0) & (at < extent), 1.0, 0.0).astype(F32)


def plane_of(field, near, far, even_x, even_far):
    def plane(x):
        if 5 <= x < 9:
            return field[x - 5]
        pair, even, at = (far, even_far, 0) if x in (0, 13) else (near, even_x, x - 1 if x < 5 else x - 9)
        below = x < 5
        return jnp.where(even, pair[1 if below else 0][at], pair[0 if below else 1][at])

    return plane


def strips(pos, field, near_0, near_1, far_0, far_1, wide, out_0, out_1):
    px, py = pos[0], pos[1]
    even_y = (py & 1) == 0
    plane = plane_of(field, (near_0, near_1), (far_0, far_1), (px & 1) == 0, ((px >> 1) & 1) == 0)
    for x in range(14):
        own = plane(x)
        wide[x] = own
        low, high = own[0:5], own[3:8]
        out_0[5 * x : 5 * x + 5] = jnp.where(even_y, high, low)
        out_1[5 * x : 5 * x + 5] = jnp.where(even_y, low, high)


def run_strips(args):
    vmem = pl.BlockSpec(memory_space=pltpu.VMEM)
    return pl.pallas_call(
        strips,
        out_shape=tuple(jax.ShapeDtypeStruct(shape, F32) for shape in ((14, 8, 256), (70, 256), (70, 256))),
        in_specs=[pl.BlockSpec(memory_space=pltpu.SMEM)] + [vmem] * (len(args) - 1),
        out_specs=(vmem,) * 3,
        compiler_params=pltpu.CompilerParams(vmem_limit_bytes=4 * 1024 * 1024),
    )(*args)


def kernel(
    pos, wide, beside_0, beside_1, cot,
    b_first, b_down, b_down_t, b_coarse, b_coarse_t, b_up, b_up_t, b_joined, b_joined_t, wf_col,
    act_own, pay,
    fe, vh, vl, fh, fl, slope_f, pdh, pdl, slope_d, rc, slope_c, ch, cl, pjh, pjl, goh, gol,
    pgh, pgl, gdir, guh, gul, pch, pcl, gch, gcl, rd, gdh, gdl,
    *, scale, size_x, size_y,
):
    px, py = pos[0], pos[1]

    z = lax.broadcasted_iota(jnp.int32, (256, 512), 0)
    col = lane_of((256, 512))
    pick = jnp.where(z == 2 * (col & 127) + (col >> 7) - 1, 1.0, 0.0).astype(BF16)
    pick_two = pick[:, 128:384]

    even_y = (py & 1) == 0
    has_head, has_tail = inside(8 * py - 1, size_y), inside(8 * py + 8, size_y)
    for x in range(14):
        own = wide[x]
        first, second = beside_0[5 * x : 5 * x + 5], beside_1[5 * x : 5 * x + 5]
        head, tail = jnp.where(even_y, second, first), jnp.where(even_y, first, second)
        there = inside(4 * px + x - 5, size_x)
        head, own, tail = head * (there * has_head), own * there, tail * (there * has_tail)
        fe[x, 0] = rows([head, own, tail[0:3]])
        fe[x, 1] = rows([own[3:8], tail, jnp.zeros((6, 256), F32)])
    for source, target in zip(split(fe[...].reshape(448, 256)), (vh, vl)):
        found = nn(source, pick).astype(BF16)
        for v in range(4):
            target[:, :, 16 * v : 16 * v + 16, :] = found[:, 128 * v : 128 * v + 128].reshape(14, 2, 16, 128)

    def first_rhs(ref, at, window):
        return rows([lanes([ref[2 * at + a + dx, window] for a in range(2)]) for dx in range(3)])

    base = b_first[...]
    w_first = stacked(rows([roll(base, yo + 16 * c) for yo in range(8) for c in range(2)])[:, :192])
    row_y = (lax.broadcasted_iota(jnp.int32, (128, 256), 0) >> 4) + 8 * py - 4
    lane_a = lane_of((1, 256)) >> 7
    for at in range(6):
        mask_x = inside(4 * px + 2 * (at - 2) + lane_a, size_x)
        for window in range(2):
            mine = slice(128 * window, 128 * window + 128)
            pre = mm3(w_first, first_rhs(vh, at, window), first_rhs(vl, at, window))
            mask = inside(row_y + 8 * window, size_y) * mask_x
            sig = sigmoid(pre)
            act = pre * sig
            slope_f[at, mine] = (sig + act * (1.0 - sig)) * mask
            act = act * mask
            high, low = split(act)
            fh[at, mine] = high
            fl[at, mine] = low
            part = act.reshape(8, 16, 256)[2:8] if window == 0 else act.reshape(8, 16, 256)[0:6]
            for a in range(2):
                plane = 2 * (at - 1) + a - 1
                if 0 <= plane < 6:
                    half = slice(128 * (plane % 2), 128 * (plane % 2) + 128)
                    high, low = split(four_depths(part[:, :, 128 * a : 128 * a + 128]))
                    pjh[plane // 2, 6 * window : 6 * window + 6, 0:32, half] = high
                    pjl[plane // 2, 6 * window : 6 * window + 6, 0:32, half] = low

    base = b_down[...]
    w_down = stacked(rows([roll(base, 32 * k) for k in range(4)]))
    row_64 = lax.broadcasted_iota(jnp.int32, (64, 256), 0) >> 4
    for pair in range(3):
        mask_x = inside(2 * px + 2 * pair + lane_a - 2, size_x // 2)
        for y0 in (0, 4):
            def down_rhs(ref):
                return rows([
                    lanes([ref[2 * pair + j, 32 * y0 : 32 * y0 + 128, 128 * a : 128 * a + 128] for j in range(2)])
                    for a in range(2)
                ])
            pre = mm3(w_down, down_rhs(fh), down_rhs(fl))
            mask = inside(row_64 + y0 - 2 + 4 * py, size_y // 2) * mask_x
            sig = sigmoid(pre)
            act = pre * sig
            sloped = (sig + act * (1.0 - sig)) * mask
            act = act * mask
            for j in range(2):
                mine = slice(128 * j, 128 * j + 128)
                high, low = split(three_depths(act[:, mine].reshape(4, 16, 128)))
                pdh[2 * pair + j, y0 : y0 + 4] = high
                pdl[2 * pair + j, y0 : y0 + 4] = low
                slope_d[2 * pair + j, 16 * y0 : 16 * y0 + 64] = sloped[:, mine]

    base = b_coarse[...]
    w_coarse = stacked(
        rows([roll(base[16 * dx : 16 * dx + 16], 48 * k) for dx in range(3) for k in range(2)])[:, :192]
    )
    for pair in range(3):
        for k in range(3):
            def coarse_rhs(ref):
                return lanes([ref[2 * pair + j, 2 * k : 2 * k + 4].reshape(192, 128) for j in range(2)])
            part = mm3(w_coarse, coarse_rhs(pdh), coarse_rhs(pdl))
            for j in range(2):
                rc[2 * pair + j, k] = part[:, 128 * j : 128 * j + 128]
    row_32 = lax.broadcasted_iota(jnp.int32, (32, 128), 0) >> 4
    for at in range(4):
        mask_x = inside(2 * px + at - 1, size_x // 2)
        for k in range(3):
            mine = slice(32 * k, 32 * k + 32)
            pre = rc[at, k, 0:32] + rc[at + 1, k, 32:64] + rc[at + 2, k, 64:96]
            mask = inside(row_32 + 2 * k - 1 + 4 * py, size_y // 2) * mask_x
            sig = sigmoid(pre)
            act = pre * sig
            slope_c[at, mine] = (sig + act * (1.0 - sig)) * mask
            high, low = split(act * mask)
            ch[at, mine] = high
            cl[at, mine] = low

    base = b_up[...]
    base = thrice(wider(base), 48)
    w_up = rows([roll(base[32 * a : 32 * a + 32], 16 * k) for a in range(2) for k in range(3)])[:, :144].astype(BF16)
    for pair in range(2):
        for block in range(2):
            mine = slice(48 * block, 48 * block + 48)
            high = lanes([ch[2 * pair, mine], ch[2 * pair + 1, mine]])
            low = lanes([cl[2 * pair, mine], cl[2 * pair + 1, mine]])
            part = nn(w_up, rows([high, low, high]))
            for j in range(2):
                for a in range(2):
                    plane = 2 * (2 * pair + j) + a - 1
                    if 0 <= plane < 6:
                        half = slice(128 * (plane % 2), 128 * (plane % 2) + 128)
                        cells = part[96 * a : 96 * a + 96, 128 * j : 128 * j + 128].reshape(6, 16, 128)
                        high_part, low_part = split(four_depths(cells))
                        pjh[plane // 2, 6 * block : 6 * block + 6, 32:64, half] = high_part
                        pjl[plane // 2, 6 * block : 6 * block + 6, 32:64, half] = low_part

    found = nn(rows(list(split(cot[...].reshape(32, 256)))), pick_two)
    sel_row = lax.broadcasted_iota(jnp.int32, (128, 32), 0)
    sel_col = lane_of((128, 32)) & 15
    spread = jnp.where(sel_col == ((sel_row >> 3) & 1) * 8 + (sel_row >> 4), 1.0, 0.0).astype(BF16)
    cb = [
        nn(
            spread,
            rows([
                lanes([
                    found[32 * s + 16 * at + 8 * a : 32 * s + 16 * at + 8 * a + 8, 128 * c : 128 * c + 128]
                    for a in range(2)
                ])
                for s in range(2)
                for c in range(2)
            ]).astype(BF16),
        )
        for at in range(2)
    ]

    base = b_joined[...]
    w_joined = stacked(
        rows([
            roll(base[8 * dx : 8 * dx + 8], 64 * b + 8 * c) for dx in range(3) for b in range(2) for c in range(2)
        ])
    )
    wf_rows = wf_col[...] * scale
    for x in range(4):
        for ref in (pgh, pgl):
            ref[x, 0:3] = jnp.zeros((3, 32, 128), BF16)
            ref[x, 11:14] = jnp.zeros((3, 32, 128), BF16)

    def around_pair(ref, pair, k):
        return ref[pair, 2 * k + 1 : 2 * k + 5].reshape(256, 256)

    for k in range(4):
        part = [mm3(w_joined, around_pair(pjh, pair, k), around_pair(pjl, pair, k)) for pair in range(3)]
        for x in range(4):
            pre = sum(
                part[(x + dx) // 2][32 * dx : 32 * dx + 32, 128 * ((x + dx) % 2) : 128 * ((x + dx) % 2) + 128]
                for dx in range(3)
            )
            at, half = x // 2, slice(128 * (x % 2), 128 * (x % 2) + 128)
            mine = slice(32 * k, 32 * k + 32)
            sig = sigmoid(pre)
            act = pre * sig
            grad = cb[at][mine, half] * wf_rows * (sig + act * (1.0 - sig))
            high, low = split(four_depths(grad.reshape(2, 16, 128)))
            pgh[x, 2 * k + 3 : 2 * k + 5] = high
            pgl[x, 2 * k + 3 : 2 * k + 5] = low
            act_own[at, mine, half] = act
            high, low = split(grad)
            goh[x, mine] = high
            gol[x, mine] = low

    part_final = sum(jnp.sum((act_own[at] * cb[at]).reshape(16, 8, 256), axis=0) for at in range(2))
    part_final = jnp.sum(part_final, axis=1, keepdims=True) * scale

    nothing = jnp.zeros((32, 128), BF16)
    total = jnp.zeros((96, 256), F32)
    for pair in range(3):
        for k in range(4):
            def moved_rows(ref):
                return rows([
                    lanes([
                        ref[2 * pair + j - dx, 32 * k : 32 * k + 32] if 0 <= 2 * pair + j - dx < 4 else nothing
                        for j in range(2)
                    ])
                    for dx in range(3)
                ])
            total = total + nt3(
                moved_rows(goh), moved_rows(gol), around_pair(pjh, pair, k), around_pair(pjl, pair, k)
            )
    part_joined = rows([
        sum(
            roll(total[32 * dx + 16 * b + 8 * c : 32 * dx + 16 * b + 8 * c + 8], -(64 * b + 8 * c))
            for b in range(2)
            for c in range(2)
        )
        for dx in range(3)
    ])

    base = b_joined_t[...]
    w_back = stacked(
        rows([
            roll(base[8 * f : 8 * f + 8], 128 * a + 32 * b + 8 * c)
            for f in range(2)
            for a in range(2)
            for b in range(2)
            for c in range(2)
        ])
    )
    w_up_t = stacked(b_up_t[...][:, :64])
    for ref in (pch, pcl):
        for at in range(4):
            ref[at, 0:2] = jnp.zeros((2, 48, 128), BF16)
            ref[at, 8:10] = jnp.zeros((2, 48, 128), BF16)
    for at in range(4):
        planes = [(2 * at - 3 + xw, xw) for xw in range(4) if 0 <= 2 * at - 3 + xw < 4]
        weight = w_back[:, 128 * planes[0][1] : 128 * planes[-1][1] + 128]
        for pair in range(3):
            def back_rhs(ref):
                return rows([
                    lanes([ref[x, 4 * pair + 2 * j : 4 * pair + 2 * j + 4].reshape(128, 128) for j in range(2)])
                    for x, _ in planes
                ])
            result = mm3(weight, back_rhs(pgh), back_rhs(pgl))
            high, low = split(result[:64])
            grad_act = mm3(w_up_t, high, low)
            for j in range(2):
                cell = 2 * pair + j
                mine = slice(128 * j, 128 * j + 128)
                gdir[at, cell] = result[64:, mine]
                guh[at, 64 * cell : 64 * cell + 64] = high[:, mine]
                gul[at, 64 * cell : 64 * cell + 64] = low[:, mine]
                grad_pre = grad_act[:, mine] * slope_c[at, 16 * cell : 16 * cell + 16]
                part_high, part_low = split(three_depths(grad_pre.reshape(1, 16, 128)))
                pch[at, cell + 2] = part_high.reshape(48, 128)
                pcl[at, cell + 2] = part_low.reshape(48, 128)
                part_high, part_low = split(grad_pre)
                gch[at, 16 * cell : 16 * cell + 16] = part_high
                gcl[at, 16 * cell : 16 * cell + 16] = part_low

    total = jnp.zeros((384, 96), F32)
    for pair in range(2):
        def two(ref):
            return lanes([ref[2 * pair], ref[2 * pair + 1]])
        total = total + nt3(two(guh), two(gul), two(ch), two(cl))
    total = lanes([total, jnp.zeros((384, 32), F32)])
    part_up = sum(roll(total[64 * y : 64 * y + 64], -16 * y) for y in range(6))

    nothing = jnp.zeros((96, 128), BF16)
    total = jnp.zeros((288, 384), F32)
    for pair in range(3):
        def moved_cells(ref):
            return rows([
                lanes([ref[2 * pair + j - dx] if 0 <= 2 * pair + j - dx < 4 else nothing for j in range(2)])
                for dx in range(3)
            ])
        def plane_pair(ref):
            return lanes([ref[2 * pair + j].reshape(384, 128) for j in range(2)])
        total = total + nt3(moved_cells(gch), moved_cells(gcl), plane_pair(pdh), plane_pair(pdl))
    lane_512 = lane_of((1, 512))
    tap, chan = lane_512 & 31, lane_512 >> 5
    tap_y = (tap * 11) >> 5
    row_256 = lax.broadcasted_iota(jnp.int32, (256, 512), 0)
    to_taps = jnp.where(row_256 == jnp.where(tap < 9, 16 * tap + chan, -1), 1.0, 0.0).astype(BF16)
    parts = [
        sum(roll(total[96 * dx + 16 * y : 96 * dx + 16 * y + 16], -48 * y) for y in range(6))[:, 0:256]
        for dx in range(3)
    ]
    part_coarse = by_tap(parts, to_taps)
    key = 64 * tap_y + 32 * (chan >> 3) + 8 * (tap - 3 * tap_y) + (chan & 7)
    to_taps = jnp.where(row_256 == jnp.where(tap < 9, key, -1), 1.0, 0.0).astype(BF16)
    part_joined = by_tap([part_joined[8 * dx : 8 * dx + 8] for dx in range(3)], to_taps)

    base = b_coarse_t[...]
    w_back_coarse = stacked(
        rows([
            roll(base[:, 256 * dx : 256 * dx + 256], 48 * k) for dx in range(3) for k in range(2)
        ])[:, :192]
    )
    for pair in range(2):
        for k in range(4):
            def shifted(ref):
                return lanes([ref[2 * pair + j, 2 * k : 2 * k + 4].reshape(192, 128) for j in range(2)])
            part = mm3(w_back_coarse, shifted(pch), shifted(pcl))
            for j in range(2):
                rd[2 * pair + j, k] = part[:, 128 * j : 128 * j + 128]
    for at in range(6):
        for k in range(4):
            mine = slice(32 * k, 32 * k + 32)
            grad = sum(rd[at - 2 + dx, k, 32 * dx : 32 * dx + 32] for dx in range(3) if 0 <= at - 2 + dx < 4)
            high, low = split(grad * slope_d[at, mine])
            gdh[at, mine] = high
            gdl[at, mine] = low

    total = jnp.zeros((1024, 256), F32)
    for pair in range(3):
        def cells(ref):
            return lanes([ref[2 * pair], ref[2 * pair + 1]])
        def fine(ref):
            return rows([lanes([ref[2 * pair + j, :, 128 * a : 128 * a + 128] for j in range(2)]) for a in range(2)])
        total = total + nt(rows([fine(fh), fine(fl)]), rows([cells(gdh), cells(gdl)]))
    total = total[:512, :128] + total[:512, 128:] + total[512:, :128]
    part_down = rows([
        sum(roll(total[256 * a + 32 * y : 256 * a + 32 * y + 32], -16 * y) for y in range(8)) for a in range(2)
    ])

    base = b_down_t[...]
    base = thrice(wider(base), 64)
    w_back_down = rows([roll(base[32 * a : 32 * a + 32], 16 * k) for a in range(2) for k in range(4)])
    w_back_down = w_back_down[:, :192].astype(BF16)
    total = jnp.zeros((128, 256), F32)
    for pair in range(3):
        for window in range(2):
            mine = slice(64 * window, 64 * window + 64)
            high = lanes([gdh[2 * pair, mine], gdh[2 * pair + 1, mine]])
            low = lanes([gdl[2 * pair, mine], gdl[2 * pair + 1, mine]])
            back = nn(w_back_down, rows([high, low, high]))
            for j in range(2):
                at = 2 * pair + j
                halves = []
                for a in range(2):
                    half = back[128 * a : 128 * a + 128, 128 * j : 128 * j + 128]
                    if 1 <= at <= 4:
                        blocks = [
                            gdir[at - 1, y - 1, 32 * a : 32 * a + 32] if 1 <= y <= 6 else jnp.zeros((32, 128), F32)
                            for y in range(4 * window, 4 * window + 4)
                        ]
                        half = half + rows(blocks)
                    halves.append(half)
                high, low = split(lanes(halves) * slope_f[at, 128 * window : 128 * window + 128])
                pad = jnp.zeros((64, 256), BF16)
                total = total + nt3(
                    high, low, rows([first_rhs(vh, at, window), pad]), rows([first_rhs(vl, at, window), pad])
                )
    part_first = sum(
        roll(total[16 * y + 8 * c : 16 * y + 8 * c + 8], -(y + 16 * c)) for y in range(8) for c in range(2)
    )

    tap = lane_of((1, 128))
    tap_x = (tap * 57) >> 9
    tap_y = ((tap - 9 * tap_x) * 11) >> 5
    key = jnp.where(tap < 27, 64 * tap_x + 16 * (tap - 9 * tap_x - 3 * tap_y) + tap_y, -1)
    row_256 = lax.broadcasted_iota(jnp.int32, (256, 128), 0)
    part_first = exact(part_first, jnp.where(row_256 == key, 1.0, 0.0).astype(BF16))
    for m in range(4):
        pay[16 * m : 16 * m + 16] = part_coarse[:, 128 * m : 128 * m + 128]
        pay[64 + 8 * m : 72 + 8 * m] = part_joined[:, 128 * m : 128 * m + 128]
    lane = lane_of((16, 128))
    pay[96:112] = sum(
        roll(jnp.where(lane < 16, part[16 * m : 16 * m + 16], 0.0), 32 * m + at)
        for m in range(4)
        for part, at in ((part_down, 0), (part_up, 16))
    )
    lane, row = lane_of((8, 128)), lax.broadcasted_iota(jnp.int32, (8, 128), 0)
    pay[112:120] = part_first + jnp.where(lane == 64 + row, part_final, 0.0)


def image(act_own, wf_lanes, img):
    zt = lane_of((256, 256))
    rt = lax.broadcasted_iota(jnp.int32, (256, 256), 0)
    merge = jnp.where(zt == 2 * (rt & 127) + (rt >> 7), 1.0, 0.0).astype(BF16)
    f_row = lax.broadcasted_iota(jnp.int32, (16, 128), 0)
    f_col = lane_of((16, 128))
    w_final = stacked(
        jnp.where((f_row >> 3 == (f_col >> 3) & 1) & (f_row & 7 == f_col >> 4), wf_lanes[...], 0.0)
    )
    out_rows = []
    for at in range(2):
        result = mm3(w_final, *split(act_own[at]))
        for a in range(2):
            out_rows.append(lanes([result[8 * c : 8 * c + 8, 128 * a : 128 * a + 128] for c in range(2)]))
    whole = nn(stacked(rows(out_rows)), merge)
    img[...] = (whole[:32] + whole[32:]).reshape(4, 8, 256)


def run_image(act_own, wf_lanes):
    vmem = pl.BlockSpec(memory_space=pltpu.VMEM)
    return pl.pallas_call(
        image,
        out_shape=jax.ShapeDtypeStruct((4, 8, 256), F32),
        in_specs=[vmem, vmem],
        out_specs=vmem,
        compiler_params=pltpu.CompilerParams(vmem_limit_bytes=8 * 1024 * 1024),
        cost_estimate=pl.CostEstimate(flops=200_000_000, bytes_accessed=400_000, transcendentals=0),
    )(act_own, wf_lanes)


def exact(block, choice):
    high, low = split(block)
    rest = (block - high.astype(F32) - low.astype(F32)).astype(BF16)
    count = block.shape[0]
    found = nn(jnp.concatenate([high.astype(F32), low.astype(F32), rest.astype(F32)], axis=0).astype(BF16), choice)
    return found[:count] + found[count : 2 * count] + found[2 * count :]


def by_tap(parts, choice):
    count = parts[0].shape[0]
    found = exact(rows(parts), choice)
    return sum(roll(found[count * dx : count * dx + count], 9 * dx) for dx in range(len(parts)))


def outputs(*refs):
    blocks, (coarse, joined, first, down, up, final) = refs[:-6], refs[-6:]
    total = [ref[...] for ref in blocks]
    while len(total) > 1:
        total = [total[i] + total[i + 1] for i in range(0, len(total), 2)]
    total = total[0]

    def slot(start, count, at, width):
        block = total[start : start + count]
        return roll(block, -at)[:, :width]

    for i in range(16):
        coarse[:, i, :] = slot(16 * (i // 4), 16, 32 * (i % 4), 27)
        joined[:, i, :] = slot(64 + 8 * (i // 4), 8, 32 * (i % 4), 27)
    for k in range(8):
        down[:, k // 2, k % 2, :] = slot(96 + 8 * (k % 2), 8, 32 * (k // 2), 16)
        up[:, k // 2, k % 2, :] = slot(96 + 8 * (k % 2), 8, 32 * (k // 2) + 16, 16)
    first[:, 0, :] = total[112:120, :27]
    lane, row = lane_of((8, 128)), lax.broadcasted_iota(jnp.int32, (8, 128), 0)
    row_sum = jnp.sum(jnp.where(lane == 64 + row, total[112:120], 0.0), axis=0, keepdims=True)
    final[...] = roll(row_sum, -64)[:, :8]


def run_outputs(blocks):
    vmem = pl.BlockSpec(memory_space=pltpu.VMEM)
    shapes = ((16, 16, 27), (8, 16, 27), (8, 1, 27), (8, 4, 2, 16), (8, 4, 2, 16), (1, 8))
    return pl.pallas_call(
        outputs,
        out_shape=tuple(jax.ShapeDtypeStruct(shape, F32) for shape in shapes),
        in_specs=[vmem] * len(blocks),
        out_specs=(vmem,) * len(shapes),
        compiler_params=pltpu.CompilerParams(vmem_limit_bytes=4 * 1024 * 1024),
    )(*blocks)


def run_kernel(args, scale, size_x, size_y):
    vmem = pl.BlockSpec(memory_space=pltpu.VMEM)

    def pair(*shape):
        return [pltpu.VMEM(shape, BF16)] * 2

    def plain(*shape):
        return [pltpu.VMEM(shape, F32)]

    scratch = (
        plain(14, 2, 16, 256)
        + pair(14, 2, 64, 128)
        + pair(6, 256, 256)
        + plain(6, 256, 256)
        + pair(6, 8, 48, 128)
        + plain(6, 128, 128)
        + plain(6, 3, 96, 128)
        + plain(4, 96, 128)
        + pair(4, 96, 128)
        + pair(3, 12, 64, 256)
        + pair(4, 128, 128)
        + pair(4, 14, 32, 128)
        + plain(4, 6, 64, 128)
        + pair(4, 384, 128)
        + pair(4, 10, 48, 128)
        + pair(4, 96, 128)
        + plain(4, 4, 96, 128)
        + pair(6, 128, 128)
    )

    def unet_tile(*refs):
        kernel(*refs, scale=scale, size_x=size_x, size_y=size_y)

    return pl.pallas_call(
        unet_tile,
        out_shape=(jax.ShapeDtypeStruct((2, 128, 256), F32), jax.ShapeDtypeStruct((120, 128), F32)),
        in_specs=[pl.BlockSpec(memory_space=pltpu.SMEM)] + [vmem] * (len(args) - 1),
        out_specs=(vmem, vmem),
        scratch_shapes=scratch,
        compiler_params=pltpu.CompilerParams(vmem_limit_bytes=48 * 1024 * 1024),
        cost_estimate=pl.CostEstimate(flops=3_000_000_000, bytes_accessed=2_000_000, transcendentals=2_000_000),
    )(*args)


def swap(first, second, axis, by):
    count = lax.axis_size(axis)

    def pairs(parity):
        return [(i, (i + (by if (i // by) % 2 == parity else -by)) % count) for i in range(count)]

    return lax.ppermute(first, axis, pairs(0)), lax.ppermute(second, axis, pairs(1))


def rounds(count, apart):
    groups = [[k * by for k in (1, 2, 3) if k * by < count] for by in (1, 4, 16, 64) if by < count]
    if apart and len(groups[0]) == 3:
        groups = [[1], [3]] + groups[1:]
    return groups


def padded(block, *shape):
    return jnp.pad(block, [(0, want - have) for want, have in zip(shape, block.shape)])


def bases_now(w_first, w_joined, w_final):
    first = w_first.reshape(3, 3, 3, 8).transpose(3, 0, 2, 1)
    first = padded(first, 8, 4, 4, 16).reshape(8, 256)
    joined = w_joined.reshape(3, 3, 3, 8, 2, 8)
    joined_out = padded(joined.transpose(0, 3, 1, 4, 2, 5), 3, 8, 4, 2, 4, 8).reshape(24, 256)
    joined_t = joined[::-1, ::-1, ::-1, :, ::-1].transpose(4, 5, 0, 1, 2, 3)
    joined_t = padded(joined_t, 2, 8, 4, 4, 4, 8).reshape(16, 512)
    wf_lanes = jnp.tile(w_final, (1, 16))
    wf_col = jnp.tile(w_final.reshape(8, 1), (4, 1))
    return first, joined_out, joined_t, wf_lanes, wf_col


def bases_later(w_down, w_coarse, w_up):
    down = padded(w_down.transpose(0, 2, 3, 4, 1).reshape(16, 2, 32), 16, 2, 128).reshape(16, 256)
    down_t = padded(w_down.transpose(2, 3, 4, 1, 0).reshape(64, 16), 64, 128)
    coarse = w_coarse.reshape(3, 3, 3, 16, 16)
    coarse_out = padded(coarse.transpose(0, 3, 1, 2, 4).reshape(48, 144), 48, 256)
    coarse_t = coarse[::-1, ::-1, ::-1].transpose(4, 0, 1, 2, 3).reshape(16, 3, 144)
    coarse_t = padded(coarse_t, 16, 3, 256).reshape(16, 768)
    up = padded(w_up.transpose(2, 3, 4, 0, 1).reshape(64, 16), 64, 128)
    up_t = padded(w_up.transpose(1, 2, 3, 4, 0).reshape(16, 64), 16, 128)
    return down, down_t, coarse_out, coarse_t, up, up_t


def shards(in_field, cotangent, w_first, w_down, w_coarse, w_up, w_joined, w_final):
    size_x, size_y = 4 * lax.axis_size("gx"), 8 * lax.axis_size("gy")
    field, cot = in_field[0], cotangent[0]
    now = bases_now(w_first, w_joined, w_final)
    pos = jnp.stack([lax.axis_index("gx"), lax.axis_index("gy")]).astype(jnp.int32)
    even = ((lax.axis_index("gx") >> 1) & 1) == 0
    low, high = field[:1], field[3:]
    far = swap(jnp.where(even, high, low), jnp.where(even, low, high), "gx", 2)
    near = swap(field, field, "gx", 1)
    near, far, now, pos, (w_down, w_coarse, w_up) = lax.optimization_barrier(
        (near, far, now, pos, (w_down, w_coarse, w_up))
    )
    wide, *sent = run_strips([pos, field, *near, *far])
    beside = swap(*sent, "gy", 1)
    first, joined_out, joined_t, wf_lanes, wf_col = now
    later = bases_later(w_down, w_coarse, w_up)
    weights = [first, *later, joined_out, joined_t, wf_col]

    scale = 1.0 / math.sqrt(size_x * size_y * in_field.shape[3])
    act_own, pay = run_kernel([pos, wide, *beside, cot, *weights], scale, size_x, size_y)

    blocks, imitated = [pay], None
    for axis in ("gy", "gx"):
        count = lax.axis_size(axis)
        for partners in rounds(count, axis == "gx"):
            while len(blocks) > 1:
                blocks = [blocks[i] + blocks[i + 1] for i in range(0, len(blocks), 2)]
            mine = blocks[0]
            blocks = [mine] + [lax.ppermute(mine, axis, [(i, i ^ k) for i in range(count)]) for k in partners]
            if imitated is None:
                act_own, blocks = lax.optimization_barrier((act_own, blocks))
                imitated = run_image(act_own, wf_lanes)
    coarse, joined, first, down, up, final = run_outputs(blocks)
    return (
        imitated[None],
        first.transpose(2, 0, 1),
        down.reshape(8, 2, 2, 2, 16).transpose(4, 0, 1, 2, 3),
        coarse.transpose(2, 0, 1),
        up.reshape(8, 2, 2, 2, 16).transpose(0, 4, 1, 2, 3),
        joined.transpose(2, 0, 1),
        final,
    )


def solution(mesh):
    in_specs = (P(None, "gx", "gy", None), P(None, "gx", "gy", None), P(), P(), P(), P(), P(), P())
    out_specs = (P(None, "gx", "gy", None), P(), P(), P(), P(), P(), P())
    return jax.shard_map(shards, mesh=mesh, in_specs=in_specs, out_specs=out_specs, check_vma=False)
```

```python
import math

import jax
import jax.numpy as jnp
from jax import lax
from jax.experimental import pallas as pl
from jax.experimental.pallas import tpu as pltpu
from jax.sharding import PartitionSpec as P

F32 = jnp.float32
BF16 = jnp.bfloat16


def nn(a, b):
    return lax.dot_general(a, b, (((1,), (0,)), ((), ())), preferred_element_type=F32)


def nt(a, b):
    return lax.dot_general(a, b, (((1,), (1,)), ((), ())), preferred_element_type=F32)


def split(x):
    high = x.astype(BF16)
    return high, (x - high.astype(F32)).astype(BF16)


def rows(parts):
    return jnp.concatenate(parts, axis=0)


def lanes(parts):
    return jnp.concatenate(parts, axis=1)


def stacked(weight):
    return rows(list(split(weight)))


def mm3(both, high, low):
    count = both.shape[0] // 2
    first = nn(both, high)
    return first[:count] + first[count:] + nn(both[:count], low)


def nt3(left_high, left_low, right_high, right_low):
    count = left_high.shape[0]
    first = nt(rows([left_high, left_low]), right_high)
    return first[:count] + first[count:] + nt(left_high, right_low)


def thrice(base, depth):
    high, low = split(base)
    high = high.astype(F32)
    return high + roll(high, depth) + roll(low.astype(F32), 2 * depth)


def wider(base):
    return lanes([base, jnp.zeros((base.shape[0], 256 - base.shape[1]), F32)])


def turned(block):
    m, n = block.shape
    if m % 128:
        block = rows([block, jnp.zeros((128 - m % 128, n), F32)])
    return block.T


def joined_turned(base):
    block = turned(base)
    lane = lane_of((8, 128)) >> 3
    parts = []
    for f in (1, 0):
        groups = []
        for dx in (2, 1, 0):
            groups.append(sum(
                roll(
                    jnp.where(lane == dx, block[64 * dy + 32 * f + 8 * dz : 64 * dy + 32 * f + 8 * dz + 8], 0.0),
                    32 * (2 - dy) + 8 * (2 - dz) - 8 * dx,
                )
                for dy in range(3)
                for dz in range(3)
            ))
        parts.append(lanes(groups + [jnp.zeros((8, 128), F32)]))
    return rows(parts)


def coarse_turned(base):
    block = turned(base)
    lane = lane_of((16, 128)) >> 4
    groups = []
    for dx in (2, 1, 0):
        taps = [
            roll(jnp.where(lane == dx, block[16 * k : 16 * k + 16], 0.0), 16 * ((8 - k) % 8) - 16 * dx)
            for k in range(9)
        ]
        groups.append(lanes([sum(taps[1:]), taps[0]]))
    return groups


def roll(x, shift):
    shift = shift % x.shape[1]
    return x if shift == 0 else pltpu.roll(x, shift, 1)


def sigmoid(x):
    return 1.0 / (1.0 + jnp.exp(-x))


def lane_of(shape):
    return lax.broadcasted_iota(jnp.int32, shape, len(shape) - 1)


def back_one(x):
    return jnp.where(lane_of(x.shape) == 0, 0.0, pltpu.roll(x, 1, 1))


def ahead_one(x):
    return jnp.where(lane_of(x.shape) == 127, 0.0, pltpu.roll(x, 127, 1))


def four_depths(field):
    count = field.shape[0]
    even, odd = field[:, :8], field[:, 8:]
    before = back_one(odd.reshape(count * 8, 128)).reshape(count, 8, 128)
    after = ahead_one(even.reshape(count * 8, 128)).reshape(count, 8, 128)
    return jnp.concatenate([before, even, odd, after], axis=1)


def three_depths(field):
    count = field.shape[0]
    flat = field.reshape(count * 16, 128)
    return jnp.concatenate(
        [back_one(flat).reshape(count, 16, 128), field, ahead_one(flat).reshape(count, 16, 128)],
        axis=1,
    )


def inside(at, extent):
    return jnp.where((at >= 0) & (at < extent), 1.0, 0.0).astype(F32)


def plane_of(field, near, far, even_x, even_far):
    def plane(x):
        if 5 <= x < 9:
            return field[x - 5]
        pair, even, at = (far, even_far, 0) if x in (0, 13) else (near, even_x, x - 1 if x < 5 else x - 9)
        below = x < 5
        return jnp.where(even, pair[1 if below else 0][at], pair[0 if below else 1][at])

    return plane


def strips(pos, field, near_0, near_1, far_0, far_1, wide, out_0, out_1):
    px, py = pos[0], pos[1]
    even_y = (py & 1) == 0
    plane = plane_of(field, (near_0, near_1), (far_0, far_1), (px & 1) == 0, ((px >> 1) & 1) == 0)
    for x in range(14):
        own = plane(x)
        wide[x] = own
        low, high = own[0:5], own[3:8]
        out_0[5 * x : 5 * x + 5] = jnp.where(even_y, high, low)
        out_1[5 * x : 5 * x + 5] = jnp.where(even_y, low, high)


def run_strips(args):
    vmem = pl.BlockSpec(memory_space=pltpu.VMEM)
    return pl.pallas_call(
        strips,
        out_shape=tuple(jax.ShapeDtypeStruct(shape, F32) for shape in ((14, 8, 256), (70, 256), (70, 256))),
        in_specs=[pl.BlockSpec(memory_space=pltpu.SMEM)] + [vmem] * (len(args) - 1),
        out_specs=(vmem,) * 3,
        compiler_params=pltpu.CompilerParams(vmem_limit_bytes=4 * 1024 * 1024),
    )(*args)


def kernel(
    pos, wide, beside_0, beside_1, cot,
    b_first, b_down, b_coarse, b_up, b_joined, w_last,
    act_own, pay,
    fe, vh, vl, fh, fl, slope_f, pdh, pdl, slope_d, rc, slope_c, ch, cl, pjh, pjl, goh, gol,
    pgh, pgl, gdir, guh, gul, pch, pcl, gch, gcl, rd, gdh, gdl,
    *, scale, size_x, size_y,
):
    px, py = pos[0], pos[1]

    z = lax.broadcasted_iota(jnp.int32, (256, 512), 0)
    col = lane_of((256, 512))
    pick = jnp.where(z == 2 * (col & 127) + (col >> 7) - 1, 1.0, 0.0).astype(BF16)
    pick_two = pick[:, 128:384]

    even_y = (py & 1) == 0
    has_head, has_tail = inside(8 * py - 1, size_y), inside(8 * py + 8, size_y)
    for x in range(14):
        own = wide[x]
        first, second = beside_0[5 * x : 5 * x + 5], beside_1[5 * x : 5 * x + 5]
        head, tail = jnp.where(even_y, second, first), jnp.where(even_y, first, second)
        there = inside(4 * px + x - 5, size_x)
        head, own, tail = head * (there * has_head), own * there, tail * (there * has_tail)
        fe[x, 0] = rows([head, own, tail[0:3]])
        fe[x, 1] = rows([own[3:8], tail, jnp.zeros((6, 256), F32)])
    for source, target in zip(split(fe[...].reshape(448, 256)), (vh, vl)):
        found = nn(source, pick).astype(BF16)
        for v in range(4):
            target[:, :, 16 * v : 16 * v + 16, :] = found[:, 128 * v : 128 * v + 128].reshape(14, 2, 16, 128)

    def first_rhs(ref, at, window):
        return rows([lanes([ref[2 * at + a + dx, window] for a in range(2)]) for dx in range(3)])

    base = b_first[...]
    w_first = stacked(rows([roll(base, yo + 16 * c) for yo in range(8) for c in range(2)])[:, :192])
    row_y = (lax.broadcasted_iota(jnp.int32, (128, 256), 0) >> 4) + 8 * py - 4
    lane_a = lane_of((1, 256)) >> 7
    for at in range(6):
        mask_x = inside(4 * px + 2 * (at - 2) + lane_a, size_x)
        for window in range(2):
            mine = slice(128 * window, 128 * window + 128)
            pre = mm3(w_first, first_rhs(vh, at, window), first_rhs(vl, at, window))
            mask = inside(row_y + 8 * window, size_y) * mask_x
            sig = sigmoid(pre)
            act = pre * sig
            slope_f[at, mine] = (sig + act * (1.0 - sig)) * mask
            act = act * mask
            high, low = split(act)
            fh[at, mine] = high
            fl[at, mine] = low
            part = act.reshape(8, 16, 256)[2:8] if window == 0 else act.reshape(8, 16, 256)[0:6]
            for a in range(2):
                plane = 2 * (at - 1) + a - 1
                if 0 <= plane < 6:
                    half = slice(128 * (plane % 2), 128 * (plane % 2) + 128)
                    high, low = split(four_depths(part[:, :, 128 * a : 128 * a + 128]))
                    pjh[plane // 2, 6 * window : 6 * window + 6, 0:32, half] = high
                    pjl[plane // 2, 6 * window : 6 * window + 6, 0:32, half] = low

    base = b_down[...]
    w_down = stacked(rows([roll(base, 32 * k) for k in range(4)]))
    row_64 = lax.broadcasted_iota(jnp.int32, (64, 256), 0) >> 4
    for pair in range(3):
        mask_x = inside(2 * px + 2 * pair + lane_a - 2, size_x // 2)
        for y0 in (0, 4):
            def down_rhs(ref):
                return rows([
                    lanes([ref[2 * pair + j, 32 * y0 : 32 * y0 + 128, 128 * a : 128 * a + 128] for j in range(2)])
                    for a in range(2)
                ])
            pre = mm3(w_down, down_rhs(fh), down_rhs(fl))
            mask = inside(row_64 + y0 - 2 + 4 * py, size_y // 2) * mask_x
            sig = sigmoid(pre)
            act = pre * sig
            sloped = (sig + act * (1.0 - sig)) * mask
            act = act * mask
            for j in range(2):
                mine = slice(128 * j, 128 * j + 128)
                high, low = split(three_depths(act[:, mine].reshape(4, 16, 128)))
                pdh[2 * pair + j, y0 : y0 + 4] = high
                pdl[2 * pair + j, y0 : y0 + 4] = low
                slope_d[2 * pair + j, 16 * y0 : 16 * y0 + 64] = sloped[:, mine]

    base = b_coarse[...]
    w_coarse = stacked(
        rows([roll(base[16 * dx : 16 * dx + 16], 48 * k) for dx in range(3) for k in range(2)])[:, :192]
    )
    for pair in range(3):
        for k in range(3):
            def coarse_rhs(ref):
                return lanes([ref[2 * pair + j, 2 * k : 2 * k + 4].reshape(192, 128) for j in range(2)])
            part = mm3(w_coarse, coarse_rhs(pdh), coarse_rhs(pdl))
            for j in range(2):
                rc[2 * pair + j, k] = part[:, 128 * j : 128 * j + 128]
    row_32 = lax.broadcasted_iota(jnp.int32, (32, 128), 0) >> 4
    for at in range(4):
        mask_x = inside(2 * px + at - 1, size_x // 2)
        for k in range(3):
            mine = slice(32 * k, 32 * k + 32)
            pre = rc[at, k, 0:32] + rc[at + 1, k, 32:64] + rc[at + 2, k, 64:96]
            mask = inside(row_32 + 2 * k - 1 + 4 * py, size_y // 2) * mask_x
            sig = sigmoid(pre)
            act = pre * sig
            slope_c[at, mine] = (sig + act * (1.0 - sig)) * mask
            high, low = split(act * mask)
            ch[at, mine] = high
            cl[at, mine] = low

    base = b_up[...]
    base = thrice(wider(base), 48)
    w_up = rows([roll(base[32 * a : 32 * a + 32], 16 * k) for a in range(2) for k in range(3)])[:, :144].astype(BF16)
    for pair in range(2):
        for block in range(2):
            mine = slice(48 * block, 48 * block + 48)
            high = lanes([ch[2 * pair, mine], ch[2 * pair + 1, mine]])
            low = lanes([cl[2 * pair, mine], cl[2 * pair + 1, mine]])
            part = nn(w_up, rows([high, low, high]))
            for j in range(2):
                for a in range(2):
                    plane = 2 * (2 * pair + j) + a - 1
                    if 0 <= plane < 6:
                        half = slice(128 * (plane % 2), 128 * (plane % 2) + 128)
                        cells = part[96 * a : 96 * a + 96, 128 * j : 128 * j + 128].reshape(6, 16, 128)
                        high_part, low_part = split(four_depths(cells))
                        pjh[plane // 2, 6 * block : 6 * block + 6, 32:64, half] = high_part
                        pjl[plane // 2, 6 * block : 6 * block + 6, 32:64, half] = low_part

    found = nn(rows(list(split(cot[...].reshape(32, 256)))), pick_two)
    sel_row = lax.broadcasted_iota(jnp.int32, (128, 32), 0)
    sel_col = lane_of((128, 32)) & 15
    spread = jnp.where(sel_col == ((sel_row >> 3) & 1) * 8 + (sel_row >> 4), 1.0, 0.0).astype(BF16)
    cb = [
        nn(
            spread,
            rows([
                lanes([
                    found[32 * s + 16 * at + 8 * a : 32 * s + 16 * at + 8 * a + 8, 128 * c : 128 * c + 128]
                    for a in range(2)
                ])
                for s in range(2)
                for c in range(2)
            ]).astype(BF16),
        )
        for at in range(2)
    ]

    base = b_joined[...]
    w_joined = stacked(
        rows([
            roll(base[8 * dx : 8 * dx + 8], 64 * b + 8 * c) for dx in range(3) for b in range(2) for c in range(2)
        ])
    )
    square = (8, 8)
    diagonal = lane_of(square) == lax.broadcasted_iota(jnp.int32, square, 0)
    column = jnp.sum(jnp.where(diagonal, jnp.broadcast_to(w_last[...][:, :8], square), 0.0), axis=1, keepdims=True)
    wf_rows = rows([column] * 4) * scale
    for x in range(4):
        for ref in (pgh, pgl):
            ref[x, 0:3] = jnp.zeros((3, 32, 128), BF16)
            ref[x, 11:14] = jnp.zeros((3, 32, 128), BF16)

    def around_pair(ref, pair, k):
        return ref[pair, 2 * k + 1 : 2 * k + 5].reshape(256, 256)

    for k in range(4):
        part = [mm3(w_joined, around_pair(pjh, pair, k), around_pair(pjl, pair, k)) for pair in range(3)]
        for x in range(4):
            pre = sum(
                part[(x + dx) // 2][32 * dx : 32 * dx + 32, 128 * ((x + dx) % 2) : 128 * ((x + dx) % 2) + 128]
                for dx in range(3)
            )
            at, half = x // 2, slice(128 * (x % 2), 128 * (x % 2) + 128)
            mine = slice(32 * k, 32 * k + 32)
            sig = sigmoid(pre)
            act = pre * sig
            grad = cb[at][mine, half] * wf_rows * (sig + act * (1.0 - sig))
            high, low = split(four_depths(grad.reshape(2, 16, 128)))
            pgh[x, 2 * k + 3 : 2 * k + 5] = high
            pgl[x, 2 * k + 3 : 2 * k + 5] = low
            act_own[at, mine, half] = act
            high, low = split(grad)
            goh[x, mine] = high
            gol[x, mine] = low

    part_final = sum(jnp.sum((act_own[at] * cb[at]).reshape(16, 8, 256), axis=0) for at in range(2))
    part_final = jnp.sum(part_final, axis=1, keepdims=True) * scale

    nothing = jnp.zeros((32, 128), BF16)
    total = jnp.zeros((96, 256), F32)
    for pair in range(3):
        for k in range(4):
            def moved_rows(ref):
                return rows([
                    lanes([
                        ref[2 * pair + j - dx, 32 * k : 32 * k + 32] if 0 <= 2 * pair + j - dx < 4 else nothing
                        for j in range(2)
                    ])
                    for dx in range(3)
                ])
            total = total + nt3(
                moved_rows(goh), moved_rows(gol), around_pair(pjh, pair, k), around_pair(pjl, pair, k)
            )
    part_joined = rows([
        sum(
            roll(total[32 * dx + 16 * b + 8 * c : 32 * dx + 16 * b + 8 * c + 8], -(64 * b + 8 * c))
            for b in range(2)
            for c in range(2)
        )
        for dx in range(3)
    ])

    base = joined_turned(b_joined[...])
    w_back = stacked(
        rows([
            roll(base[8 * f : 8 * f + 8], 128 * a + 32 * b + 8 * c)
            for f in range(2)
            for a in range(2)
            for b in range(2)
            for c in range(2)
        ])
    )
    w_up_t = stacked(turned(b_up[...])[:16, :64])
    for ref in (pch, pcl):
        for at in range(4):
            ref[at, 0:2] = jnp.zeros((2, 48, 128), BF16)
            ref[at, 8:10] = jnp.zeros((2, 48, 128), BF16)
    for at in range(4):
        planes = [(2 * at - 3 + xw, xw) for xw in range(4) if 0 <= 2 * at - 3 + xw < 4]
        weight = w_back[:, 128 * planes[0][1] : 128 * planes[-1][1] + 128]
        for pair in range(3):
            def back_rhs(ref):
                return rows([
                    lanes([ref[x, 4 * pair + 2 * j : 4 * pair + 2 * j + 4].reshape(128, 128) for j in range(2)])
                    for x, _ in planes
                ])
            result = mm3(weight, back_rhs(pgh), back_rhs(pgl))
            high, low = split(result[:64])
            grad_act = mm3(w_up_t, high, low)
            for j in range(2):
                cell = 2 * pair + j
                mine = slice(128 * j, 128 * j + 128)
                gdir[at, cell] = result[64:, mine]
                guh[at, 64 * cell : 64 * cell + 64] = high[:, mine]
                gul[at, 64 * cell : 64 * cell + 64] = low[:, mine]
                grad_pre = grad_act[:, mine] * slope_c[at, 16 * cell : 16 * cell + 16]
                part_high, part_low = split(three_depths(grad_pre.reshape(1, 16, 128)))
                pch[at, cell + 2] = part_high.reshape(48, 128)
                pcl[at, cell + 2] = part_low.reshape(48, 128)
                part_high, part_low = split(grad_pre)
                gch[at, 16 * cell : 16 * cell + 16] = part_high
                gcl[at, 16 * cell : 16 * cell + 16] = part_low

    total = jnp.zeros((384, 96), F32)
    for pair in range(2):
        def two(ref):
            return lanes([ref[2 * pair], ref[2 * pair + 1]])
        total = total + nt3(two(guh), two(gul), two(ch), two(cl))
    total = lanes([total, jnp.zeros((384, 32), F32)])
    part_up = sum(roll(total[64 * y : 64 * y + 64], -16 * y) for y in range(6))

    nothing = jnp.zeros((96, 128), BF16)
    total = jnp.zeros((288, 384), F32)
    for pair in range(3):
        def moved_cells(ref):
            return rows([
                lanes([ref[2 * pair + j - dx] if 0 <= 2 * pair + j - dx < 4 else nothing for j in range(2)])
                for dx in range(3)
            ])
        def plane_pair(ref):
            return lanes([ref[2 * pair + j].reshape(384, 128) for j in range(2)])
        total = total + nt3(moved_cells(gch), moved_cells(gcl), plane_pair(pdh), plane_pair(pdl))
    lane_512 = lane_of((1, 512))
    tap, chan = lane_512 & 31, lane_512 >> 5
    tap_y = (tap * 11) >> 5
    row_256 = lax.broadcasted_iota(jnp.int32, (256, 512), 0)
    to_taps = jnp.where(row_256 == jnp.where(tap < 9, 16 * tap + chan, -1), 1.0, 0.0).astype(BF16)
    parts = [
        sum(roll(total[96 * dx + 16 * y : 96 * dx + 16 * y + 16], -48 * y) for y in range(6))[:, 0:256]
        for dx in range(3)
    ]
    part_coarse = by_tap(parts, to_taps)
    key = 64 * tap_y + 32 * (chan >> 3) + 8 * (tap - 3 * tap_y) + (chan & 7)
    to_taps = jnp.where(row_256 == jnp.where(tap < 9, key, -1), 1.0, 0.0).astype(BF16)
    part_joined = by_tap([part_joined[8 * dx : 8 * dx + 8] for dx in range(3)], to_taps)

    w_back_coarse = stacked(
        rows([roll(group, 48 * k) for group in coarse_turned(b_coarse[...]) for k in range(2)])[:, :192]
    )
    for pair in range(2):
        for k in range(4):
            def shifted(ref):
                return lanes([ref[2 * pair + j, 2 * k : 2 * k + 4].reshape(192, 128) for j in range(2)])
            part = mm3(w_back_coarse, shifted(pch), shifted(pcl))
            for j in range(2):
                rd[2 * pair + j, k] = part[:, 128 * j : 128 * j + 128]
    for at in range(6):
        for k in range(4):
            mine = slice(32 * k, 32 * k + 32)
            grad = sum(rd[at - 2 + dx, k, 32 * dx : 32 * dx + 32] for dx in range(3) if 0 <= at - 2 + dx < 4)
            high, low = split(grad * slope_d[at, mine])
            gdh[at, mine] = high
            gdl[at, mine] = low

    total = jnp.zeros((1024, 256), F32)
    for pair in range(3):
        def cells(ref):
            return lanes([ref[2 * pair], ref[2 * pair + 1]])
        def fine(ref):
            return rows([lanes([ref[2 * pair + j, :, 128 * a : 128 * a + 128] for j in range(2)]) for a in range(2)])
        total = total + nt(rows([fine(fh), fine(fl)]), rows([cells(gdh), cells(gdl)]))
    total = total[:512, :128] + total[:512, 128:] + total[512:, :128]
    part_down = rows([
        sum(roll(total[256 * a + 32 * y : 256 * a + 32 * y + 32], -16 * y) for y in range(8)) for a in range(2)
    ])

    base = turned(b_down[...])
    base = rows([base[0:32], base[128:160]])
    base = thrice(wider(base), 64)
    w_back_down = rows([roll(base[32 * a : 32 * a + 32], 16 * k) for a in range(2) for k in range(4)])
    w_back_down = w_back_down[:, :192].astype(BF16)
    total = jnp.zeros((128, 256), F32)
    for pair in range(3):
        for window in range(2):
            mine = slice(64 * window, 64 * window + 64)
            high = lanes([gdh[2 * pair, mine], gdh[2 * pair + 1, mine]])
            low = lanes([gdl[2 * pair, mine], gdl[2 * pair + 1, mine]])
            back = nn(w_back_down, rows([high, low, high]))
            for j in range(2):
                at = 2 * pair + j
                halves = []
                for a in range(2):
                    half = back[128 * a : 128 * a + 128, 128 * j : 128 * j + 128]
                    if 1 <= at <= 4:
                        blocks = [
                            gdir[at - 1, y - 1, 32 * a : 32 * a + 32] if 1 <= y <= 6 else jnp.zeros((32, 128), F32)
                            for y in range(4 * window, 4 * window + 4)
                        ]
                        half = half + rows(blocks)
                    halves.append(half)
                high, low = split(lanes(halves) * slope_f[at, 128 * window : 128 * window + 128])
                pad = jnp.zeros((64, 256), BF16)
                total = total + nt3(
                    high, low, rows([first_rhs(vh, at, window), pad]), rows([first_rhs(vl, at, window), pad])
                )
    part_first = sum(
        roll(total[16 * y + 8 * c : 16 * y + 8 * c + 8], -(y + 16 * c)) for y in range(8) for c in range(2)
    )

    tap = lane_of((1, 128))
    tap_x = (tap * 57) >> 9
    tap_y = ((tap - 9 * tap_x) * 11) >> 5
    key = jnp.where(tap < 27, 64 * tap_x + 16 * (tap - 9 * tap_x - 3 * tap_y) + tap_y, -1)
    row_256 = lax.broadcasted_iota(jnp.int32, (256, 128), 0)
    part_first = exact(part_first, jnp.where(row_256 == key, 1.0, 0.0).astype(BF16))
    for m in range(4):
        pay[16 * m : 16 * m + 16] = part_coarse[:, 128 * m : 128 * m + 128]
        pay[64 + 8 * m : 72 + 8 * m] = part_joined[:, 128 * m : 128 * m + 128]
    lane = lane_of((16, 128))
    pay[96:112] = sum(
        roll(jnp.where(lane < 16, part[16 * m : 16 * m + 16], 0.0), 32 * m + at)
        for m in range(4)
        for part, at in ((part_down, 0), (part_up, 16))
    )
    lane, row = lane_of((8, 128)), lax.broadcasted_iota(jnp.int32, (8, 128), 0)
    pay[112:120] = part_first + jnp.where(lane == 64 + row, part_final, 0.0)


def image(act_own, w_last, img):
    zt = lane_of((256, 256))
    rt = lax.broadcasted_iota(jnp.int32, (256, 256), 0)
    merge = jnp.where(zt == 2 * (rt & 127) + (rt >> 7), 1.0, 0.0).astype(BF16)
    f_row = lax.broadcasted_iota(jnp.int32, (16, 128), 0)
    f_col = lane_of((16, 128))
    wf_lanes = w_last[...]
    for by in (8, 16, 32, 64):
        wf_lanes = wf_lanes + roll(wf_lanes, by)
    w_final = stacked(
        jnp.where((f_row >> 3 == (f_col >> 3) & 1) & (f_row & 7 == f_col >> 4), wf_lanes, 0.0)
    )
    out_rows = []
    for at in range(2):
        result = mm3(w_final, *split(act_own[at]))
        for a in range(2):
            out_rows.append(lanes([result[8 * c : 8 * c + 8, 128 * a : 128 * a + 128] for c in range(2)]))
    whole = nn(stacked(rows(out_rows)), merge)
    img[...] = (whole[:32] + whole[32:]).reshape(4, 8, 256)


def run_image(act_own, w_last):
    vmem = pl.BlockSpec(memory_space=pltpu.VMEM)
    return pl.pallas_call(
        image,
        out_shape=jax.ShapeDtypeStruct((4, 8, 256), F32),
        in_specs=[vmem, vmem],
        out_specs=vmem,
        compiler_params=pltpu.CompilerParams(vmem_limit_bytes=8 * 1024 * 1024),
        cost_estimate=pl.CostEstimate(flops=200_000_000, bytes_accessed=400_000, transcendentals=0),
    )(act_own, w_last)


def exact(block, choice):
    high, low = split(block)
    rest = (block - high.astype(F32) - low.astype(F32)).astype(BF16)
    count = block.shape[0]
    found = nn(jnp.concatenate([high.astype(F32), low.astype(F32), rest.astype(F32)], axis=0).astype(BF16), choice)
    return found[:count] + found[count : 2 * count] + found[2 * count :]


def by_tap(parts, choice):
    count = parts[0].shape[0]
    found = exact(rows(parts), choice)
    return sum(roll(found[count * dx : count * dx + count], 9 * dx) for dx in range(len(parts)))


def outputs(*refs):
    blocks, (coarse, joined, first, down, up, final) = refs[:-6], refs[-6:]
    total = [ref[...] for ref in blocks]
    while len(total) > 1:
        total = [total[i] + total[i + 1] for i in range(0, len(total), 2)]
    total = total[0]

    def slot(start, count, at, width):
        block = total[start : start + count]
        return roll(block, -at)[:, :width]

    for i in range(16):
        coarse[:, i, :] = slot(16 * (i // 4), 16, 32 * (i % 4), 27)
        joined[:, i, :] = slot(64 + 8 * (i // 4), 8, 32 * (i % 4), 27)
    for k in range(8):
        down[:, k // 2, k % 2, :] = slot(96 + 8 * (k % 2), 8, 32 * (k // 2), 16)
        up[:, k // 2, k % 2, :] = slot(96 + 8 * (k % 2), 8, 32 * (k // 2) + 16, 16)
    first[:, 0, :] = total[112:120, :27]
    lane, row = lane_of((8, 128)), lax.broadcasted_iota(jnp.int32, (8, 128), 0)
    row_sum = jnp.sum(jnp.where(lane == 64 + row, total[112:120], 0.0), axis=0, keepdims=True)
    final[...] = roll(row_sum, -64)[:, :8]


def run_outputs(blocks):
    vmem = pl.BlockSpec(memory_space=pltpu.VMEM)
    shapes = ((16, 16, 27), (8, 16, 27), (8, 1, 27), (8, 4, 2, 16), (8, 4, 2, 16), (1, 8))
    return pl.pallas_call(
        outputs,
        out_shape=tuple(jax.ShapeDtypeStruct(shape, F32) for shape in shapes),
        in_specs=[vmem] * len(blocks),
        out_specs=(vmem,) * len(shapes),
        compiler_params=pltpu.CompilerParams(vmem_limit_bytes=4 * 1024 * 1024),
    )(*blocks)


def run_kernel(args, scale, size_x, size_y):
    vmem = pl.BlockSpec(memory_space=pltpu.VMEM)

    def pair(*shape):
        return [pltpu.VMEM(shape, BF16)] * 2

    def plain(*shape):
        return [pltpu.VMEM(shape, F32)]

    scratch = (
        plain(14, 2, 16, 256)
        + pair(14, 2, 64, 128)
        + pair(6, 256, 256)
        + plain(6, 256, 256)
        + pair(6, 8, 48, 128)
        + plain(6, 128, 128)
        + plain(6, 3, 96, 128)
        + plain(4, 96, 128)
        + pair(4, 96, 128)
        + pair(3, 12, 64, 256)
        + pair(4, 128, 128)
        + pair(4, 14, 32, 128)
        + plain(4, 6, 64, 128)
        + pair(4, 384, 128)
        + pair(4, 10, 48, 128)
        + pair(4, 96, 128)
        + plain(4, 4, 96, 128)
        + pair(6, 128, 128)
    )

    def unet_tile(*refs):
        kernel(*refs, scale=scale, size_x=size_x, size_y=size_y)

    return pl.pallas_call(
        unet_tile,
        out_shape=(jax.ShapeDtypeStruct((2, 128, 256), F32), jax.ShapeDtypeStruct((120, 128), F32)),
        in_specs=[pl.BlockSpec(memory_space=pltpu.SMEM)] + [vmem] * (len(args) - 1),
        out_specs=(vmem, vmem),
        scratch_shapes=scratch,
        compiler_params=pltpu.CompilerParams(vmem_limit_bytes=48 * 1024 * 1024),
        cost_estimate=pl.CostEstimate(flops=3_000_000_000, bytes_accessed=2_000_000, transcendentals=2_000_000),
    )(*args)


def swap(first, second, axis, by):
    count = lax.axis_size(axis)

    def pairs(parity):
        return [(i, (i + (by if (i // by) % 2 == parity else -by)) % count) for i in range(count)]

    return lax.ppermute(first, axis, pairs(0)), lax.ppermute(second, axis, pairs(1))


def rounds(count, apart):
    groups = [[k * by for k in (1, 2, 3) if k * by < count] for by in (1, 4, 16, 64) if by < count]
    if apart and len(groups[0]) == 3:
        groups = [[1], [3]] + groups[1:]
    return groups


def padded(block, *shape):
    return jnp.pad(block, [(0, want - have) for want, have in zip(shape, block.shape)])


def bases_now(w_first, w_joined, w_final):
    first = w_first.reshape(3, 3, 3, 8).transpose(3, 0, 2, 1)
    first = padded(first, 8, 4, 4, 16).reshape(8, 256)
    joined = w_joined.reshape(3, 3, 3, 8, 2, 8)
    joined = padded(joined.transpose(0, 3, 1, 4, 2, 5), 3, 8, 4, 2, 4, 8).reshape(24, 256)
    return first, joined, padded(w_final, 1, 128)


def bases_later(w_down, w_coarse, w_up):
    down = padded(w_down.transpose(0, 2, 3, 4, 1).reshape(16, 2, 32), 16, 2, 128).reshape(16, 256)
    coarse = w_coarse.reshape(3, 3, 3, 16, 16)
    coarse = padded(coarse.transpose(0, 3, 1, 2, 4).reshape(48, 144), 48, 256)
    up = padded(w_up.transpose(2, 3, 4, 0, 1).reshape(64, 16), 64, 128)
    return down, coarse, up


def shards(in_field, cotangent, w_first, w_down, w_coarse, w_up, w_joined, w_final):
    size_x, size_y = 4 * lax.axis_size("gx"), 8 * lax.axis_size("gy")
    field, cot = in_field[0], cotangent[0]
    now = bases_now(w_first, w_joined, w_final)
    pos = jnp.stack([lax.axis_index("gx"), lax.axis_index("gy")]).astype(jnp.int32)
    even = ((lax.axis_index("gx") >> 1) & 1) == 0
    low, high = field[:1], field[3:]
    far = swap(jnp.where(even, high, low), jnp.where(even, low, high), "gx", 2)
    near = swap(field, field, "gx", 1)
    near, far, now, pos, (w_down, w_coarse, w_up) = lax.optimization_barrier(
        (near, far, now, pos, (w_down, w_coarse, w_up))
    )
    wide, *sent = run_strips([pos, field, *near, *far])
    beside = swap(*sent, "gy", 1)
    first, joined, last = now
    later = bases_later(w_down, w_coarse, w_up)
    weights = [first, *later, joined, last]

    scale = 1.0 / math.sqrt(size_x * size_y * in_field.shape[3])
    act_own, pay = run_kernel([pos, wide, *beside, cot, *weights], scale, size_x, size_y)

    blocks, imitated = [pay], None
    for axis in ("gy", "gx"):
        count = lax.axis_size(axis)
        for partners in rounds(count, axis == "gx"):
            while len(blocks) > 1:
                blocks = [blocks[i] + blocks[i + 1] for i in range(0, len(blocks), 2)]
            mine = blocks[0]
            blocks = [mine] + [lax.ppermute(mine, axis, [(i, i ^ k) for i in range(count)]) for k in partners]
            if imitated is None:
                act_own, blocks = lax.optimization_barrier((act_own, blocks))
                imitated = run_image(act_own, last)
    coarse, joined, first, down, up, final = run_outputs(blocks)
    return (
        imitated[None],
        first.transpose(2, 0, 1),
        down.reshape(8, 2, 2, 2, 16).transpose(4, 0, 1, 2, 3),
        coarse.transpose(2, 0, 1),
        up.reshape(8, 2, 2, 2, 16).transpose(0, 4, 1, 2, 3),
        joined.transpose(2, 0, 1),
        final,
    )


def solution(mesh):
    in_specs = (P(None, "gx", "gy", None), P(None, "gx", "gy", None), P(), P(), P(), P(), P(), P())
    out_specs = (P(None, "gx", "gy", None), P(), P(), P(), P(), P(), P())
    return jax.shard_map(shards, mesh=mesh, in_specs=in_specs, out_specs=out_specs, check_vma=False)
```

```python
import math

import jax
import jax.numpy as jnp
from jax import lax
from jax.experimental import pallas as pl
from jax.experimental.pallas import tpu as pltpu
from jax.sharding import PartitionSpec as P

F32 = jnp.float32
BF16 = jnp.bfloat16


def nn(a, b):
    return lax.dot_general(a, b, (((1,), (0,)), ((), ())), preferred_element_type=F32)


def nt(a, b):
    return lax.dot_general(a, b, (((1,), (1,)), ((), ())), preferred_element_type=F32)


def split(x):
    high = x.astype(BF16)
    return high, (x - high.astype(F32)).astype(BF16)


def rows(parts):
    return jnp.concatenate(parts, axis=0)


def lanes(parts):
    return jnp.concatenate(parts, axis=1)


def stacked(weight):
    return rows(list(split(weight)))


def mm3(both, high, low):
    count = both.shape[0] // 2
    first = nn(both, high)
    return first[:count] + first[count:] + nn(both[:count], low)


def nt3(left_high, left_low, right_high, right_low):
    count = left_high.shape[0]
    first = nt(rows([left_high, left_low]), right_high)
    return first[:count] + first[count:] + nt(left_high, right_low)


def thrice(base, depth):
    high, low = split(base)
    high = high.astype(F32)
    return high + roll(high, depth) + roll(low.astype(F32), 2 * depth)


def wider(base):
    return lanes([base, jnp.zeros((base.shape[0], 256 - base.shape[1]), F32)])


def turned(block):
    m, n = block.shape
    if m % 128:
        block = rows([block, jnp.zeros((128 - m % 128, n), F32)])
    return block.T


def joined_turned(base):
    block = turned(base)
    lane = lane_of((8, 128)) >> 3
    parts = []
    for f in (1, 0):
        groups = []
        for dx in (2, 1, 0):
            groups.append(sum(
                roll(
                    jnp.where(lane == dx, block[64 * dy + 32 * f + 8 * dz : 64 * dy + 32 * f + 8 * dz + 8], 0.0),
                    32 * (2 - dy) + 8 * (2 - dz) - 8 * dx,
                )
                for dy in range(3)
                for dz in range(3)
            ))
        parts.append(lanes(groups + [jnp.zeros((8, 128), F32)]))
    return rows(parts)


def coarse_turned(base):
    block = turned(base)
    lane = lane_of((16, 128)) >> 4
    groups = []
    for dx in (2, 1, 0):
        taps = [
            roll(jnp.where(lane == dx, block[16 * k : 16 * k + 16], 0.0), 16 * ((8 - k) % 8) - 16 * dx)
            for k in range(9)
        ]
        groups.append(lanes([sum(taps[1:]), taps[0]]))
    return groups


def roll(x, shift):
    shift = shift % x.shape[1]
    return x if shift == 0 else pltpu.roll(x, shift, 1)


def sigmoid(x):
    return 1.0 / (1.0 + jnp.exp(-x))


def lane_of(shape):
    return lax.broadcasted_iota(jnp.int32, shape, len(shape) - 1)


def back_one(x):
    return jnp.where(lane_of(x.shape) == 0, 0.0, pltpu.roll(x, 1, 1))


def ahead_one(x):
    return jnp.where(lane_of(x.shape) == 127, 0.0, pltpu.roll(x, 127, 1))


def four_depths(field):
    count = field.shape[0]
    even, odd = field[:, :8], field[:, 8:]
    before = back_one(odd.reshape(count * 8, 128)).reshape(count, 8, 128)
    after = ahead_one(even.reshape(count * 8, 128)).reshape(count, 8, 128)
    return jnp.concatenate([before, even, odd, after], axis=1)


def three_depths(field):
    count = field.shape[0]
    flat = field.reshape(count * 16, 128)
    return jnp.concatenate(
        [back_one(flat).reshape(count, 16, 128), field, ahead_one(flat).reshape(count, 16, 128)],
        axis=1,
    )


def inside(at, extent):
    return jnp.where((at >= 0) & (at < extent), 1.0, 0.0).astype(F32)


def plane_of(field, near, far, even_x, even_far):
    def plane(x):
        if 5 <= x < 9:
            return field[x - 5]
        pair, even, at = (far, even_far, 0) if x in (0, 13) else (near, even_x, x - 1 if x < 5 else x - 9)
        below = x < 5
        return jnp.where(even, pair[1 if below else 0][at], pair[0 if below else 1][at])

    return plane


def strips(pos, field, near_0, near_1, far_0, far_1, wide, out_0, out_1):
    px, py = pos[0], pos[1]
    even_y = (py & 1) == 0
    plane = plane_of(field, (near_0, near_1), (far_0, far_1), (px & 1) == 0, ((px >> 1) & 1) == 0)
    for x in range(14):
        own = plane(x)
        wide[x] = own
        low, high = own[0:5], own[3:8]
        out_0[5 * x : 5 * x + 5] = jnp.where(even_y, high, low)
        out_1[5 * x : 5 * x + 5] = jnp.where(even_y, low, high)


def run_strips(args):
    vmem = pl.BlockSpec(memory_space=pltpu.VMEM)
    return pl.pallas_call(
        strips,
        out_shape=tuple(jax.ShapeDtypeStruct(shape, F32) for shape in ((14, 8, 256), (70, 256), (70, 256))),
        in_specs=[pl.BlockSpec(memory_space=pltpu.SMEM)] + [vmem] * (len(args) - 1),
        out_specs=(vmem,) * 3,
        compiler_params=pltpu.CompilerParams(vmem_limit_bytes=4 * 1024 * 1024),
    )(*args)


def kernel(
    pos, wide, beside_0, beside_1, cot,
    b_first, b_down, b_coarse, b_up, b_joined, w_last,
    act_own, pay,
    fe, vh, vl, fh, fl, slope_f, pdh, pdl, slope_d, rc, slope_c, ch, cl, pjh, pjl, goh, gol,
    pgh, pgl, gdir, guh, gul, pch, pcl, gch, gcl, rd, gdh, gdl,
    *, scale, size_x, size_y,
):
    px, py = pos[0], pos[1]

    z = lax.broadcasted_iota(jnp.int32, (256, 512), 0)
    col = lane_of((256, 512))
    pick = jnp.where(z == 2 * (col & 127) + (col >> 7) - 1, 1.0, 0.0).astype(BF16)
    pick_two = pick[:, 128:384]

    even_y = (py & 1) == 0
    has_head, has_tail = inside(8 * py - 1, size_y), inside(8 * py + 8, size_y)
    for x in range(14):
        own = wide[x]
        first, second = beside_0[5 * x : 5 * x + 5], beside_1[5 * x : 5 * x + 5]
        head, tail = jnp.where(even_y, second, first), jnp.where(even_y, first, second)
        there = inside(4 * px + x - 5, size_x)
        head, own, tail = head * (there * has_head), own * there, tail * (there * has_tail)
        fe[x, 0] = rows([head, own, tail[0:3]])
        fe[x, 1] = rows([own[3:8], tail, jnp.zeros((6, 256), F32)])
    for source, target in zip(split(fe[...].reshape(448, 256)), (vh, vl)):
        found = nn(source, pick).astype(BF16)
        for v in range(4):
            target[:, :, 16 * v : 16 * v + 16, :] = found[:, 128 * v : 128 * v + 128].reshape(14, 2, 16, 128)

    def first_rhs(ref, at, window):
        return rows([lanes([ref[2 * at + a + dx, window] for a in range(2)]) for dx in range(3)])

    base = b_first[...]
    w_first = stacked(rows([roll(base, yo + 16 * c) for yo in range(8) for c in range(2)])[:, :192])
    row_y = (lax.broadcasted_iota(jnp.int32, (128, 256), 0) >> 4) + 8 * py - 4
    lane_a = lane_of((1, 256)) >> 7
    for at in range(6):
        mask_x = inside(4 * px + 2 * (at - 2) + lane_a, size_x)
        for window in range(2):
            mine = slice(128 * window, 128 * window + 128)
            pre = mm3(w_first, first_rhs(vh, at, window), first_rhs(vl, at, window))
            mask = inside(row_y + 8 * window, size_y) * mask_x
            sig = sigmoid(pre)
            act = pre * sig
            slope_f[at, mine] = (sig + act * (1.0 - sig)) * mask
            act = act * mask
            high, low = split(act)
            fh[at, mine] = high
            fl[at, mine] = low
            part = act.reshape(8, 16, 256)[2:8] if window == 0 else act.reshape(8, 16, 256)[0:6]
            for a in range(2):
                plane = 2 * (at - 1) + a - 1
                if 0 <= plane < 6:
                    half = slice(128 * (plane % 2), 128 * (plane % 2) + 128)
                    high, low = split(four_depths(part[:, :, 128 * a : 128 * a + 128]))
                    pjh[plane // 2, 6 * window : 6 * window + 6, 0:32, half] = high
                    pjl[plane // 2, 6 * window : 6 * window + 6, 0:32, half] = low

    base = b_down[...]
    w_down = stacked(rows([roll(base, 32 * k) for k in range(4)]))
    row_64 = lax.broadcasted_iota(jnp.int32, (64, 256), 0) >> 4
    for pair in range(3):
        mask_x = inside(2 * px + 2 * pair + lane_a - 2, size_x // 2)
        for y0 in (0, 4):
            def down_rhs(ref):
                return rows([
                    lanes([ref[2 * pair + j, 32 * y0 : 32 * y0 + 128, 128 * a : 128 * a + 128] for j in range(2)])
                    for a in range(2)
                ])
            pre = mm3(w_down, down_rhs(fh), down_rhs(fl))
            mask = inside(row_64 + y0 - 2 + 4 * py, size_y // 2) * mask_x
            sig = sigmoid(pre)
            act = pre * sig
            sloped = (sig + act * (1.0 - sig)) * mask
            act = act * mask
            for j in range(2):
                mine = slice(128 * j, 128 * j + 128)
                high, low = split(three_depths(act[:, mine].reshape(4, 16, 128)))
                pdh[2 * pair + j, y0 : y0 + 4] = high
                pdl[2 * pair + j, y0 : y0 + 4] = low
                slope_d[2 * pair + j, 16 * y0 : 16 * y0 + 64] = sloped[:, mine]

    base = b_coarse[...]
    w_coarse = stacked(
        rows([roll(base[16 * dx : 16 * dx + 16], 48 * k) for dx in range(3) for k in range(2)])[:, :192]
    )
    for pair in range(3):
        for k in range(3):
            def coarse_rhs(ref):
                return lanes([ref[2 * pair + j, 2 * k : 2 * k + 4].reshape(192, 128) for j in range(2)])
            part = mm3(w_coarse, coarse_rhs(pdh), coarse_rhs(pdl))
            for j in range(2):
                rc[2 * pair + j, k] = part[:, 128 * j : 128 * j + 128]
    row_32 = lax.broadcasted_iota(jnp.int32, (32, 128), 0) >> 4
    for at in range(4):
        mask_x = inside(2 * px + at - 1, size_x // 2)
        for k in range(3):
            mine = slice(32 * k, 32 * k + 32)
            pre = rc[at, k, 0:32] + rc[at + 1, k, 32:64] + rc[at + 2, k, 64:96]
            mask = inside(row_32 + 2 * k - 1 + 4 * py, size_y // 2) * mask_x
            sig = sigmoid(pre)
            act = pre * sig
            slope_c[at, mine] = (sig + act * (1.0 - sig)) * mask
            high, low = split(act * mask)
            ch[at, mine] = high
            cl[at, mine] = low

    base = b_up[...]
    base = thrice(wider(base), 48)
    w_up = rows([roll(base[32 * a : 32 * a + 32], 16 * k) for a in range(2) for k in range(3)])[:, :144].astype(BF16)
    for pair in range(2):
        for block in range(2):
            mine = slice(48 * block, 48 * block + 48)
            high = lanes([ch[2 * pair, mine], ch[2 * pair + 1, mine]])
            low = lanes([cl[2 * pair, mine], cl[2 * pair + 1, mine]])
            part = nn(w_up, rows([high, low, high]))
            for j in range(2):
                for a in range(2):
                    plane = 2 * (2 * pair + j) + a - 1
                    if 0 <= plane < 6:
                        half = slice(128 * (plane % 2), 128 * (plane % 2) + 128)
                        cells = part[96 * a : 96 * a + 96, 128 * j : 128 * j + 128].reshape(6, 16, 128)
                        high_part, low_part = split(four_depths(cells))
                        pjh[plane // 2, 6 * block : 6 * block + 6, 32:64, half] = high_part
                        pjl[plane // 2, 6 * block : 6 * block + 6, 32:64, half] = low_part

    found = nn(rows(list(split(cot[...].reshape(32, 256)))), pick_two)
    sel_row = lax.broadcasted_iota(jnp.int32, (128, 32), 0)
    sel_col = lane_of((128, 32)) & 15
    spread = jnp.where(sel_col == ((sel_row >> 3) & 1) * 8 + (sel_row >> 4), 1.0, 0.0).astype(BF16)
    cb = [
        nn(
            spread,
            rows([
                lanes([
                    found[32 * s + 16 * at + 8 * a : 32 * s + 16 * at + 8 * a + 8, 128 * c : 128 * c + 128]
                    for a in range(2)
                ])
                for s in range(2)
                for c in range(2)
            ]).astype(BF16),
        )
        for at in range(2)
    ]

    base = b_joined[...]
    w_joined = stacked(
        rows([
            roll(base[8 * dx : 8 * dx + 8], 64 * b + 8 * c) for dx in range(3) for b in range(2) for c in range(2)
        ])
    )
    square = (8, 8)
    diagonal = lane_of(square) == lax.broadcasted_iota(jnp.int32, square, 0)
    column = jnp.sum(jnp.where(diagonal, jnp.broadcast_to(w_last[...][:, :8], square), 0.0), axis=1, keepdims=True)
    wf_rows = rows([column] * 4) * scale
    for x in range(4):
        for ref in (pgh, pgl):
            ref[x, 0:3] = jnp.zeros((3, 32, 128), BF16)
            ref[x, 11:14] = jnp.zeros((3, 32, 128), BF16)

    def around_pair(ref, pair, k):
        return ref[pair, 2 * k + 1 : 2 * k + 5].reshape(256, 256)

    for k in range(4):
        part = [mm3(w_joined, around_pair(pjh, pair, k), around_pair(pjl, pair, k)) for pair in range(3)]
        for x in range(4):
            pre = sum(
                part[(x + dx) // 2][32 * dx : 32 * dx + 32, 128 * ((x + dx) % 2) : 128 * ((x + dx) % 2) + 128]
                for dx in range(3)
            )
            at, half = x // 2, slice(128 * (x % 2), 128 * (x % 2) + 128)
            mine = slice(32 * k, 32 * k + 32)
            sig = sigmoid(pre)
            act = pre * sig
            grad = cb[at][mine, half] * wf_rows * (sig + act * (1.0 - sig))
            high, low = split(four_depths(grad.reshape(2, 16, 128)))
            pgh[x, 2 * k + 3 : 2 * k + 5] = high
            pgl[x, 2 * k + 3 : 2 * k + 5] = low
            act_own[at, mine, half] = act
            high, low = split(grad)
            goh[x, mine] = high
            gol[x, mine] = low

    part_final = sum(jnp.sum((act_own[at] * cb[at]).reshape(16, 8, 256), axis=0) for at in range(2))
    part_final = jnp.sum(part_final, axis=1, keepdims=True) * scale

    nothing = jnp.zeros((32, 128), BF16)
    total = jnp.zeros((96, 256), F32)
    for pair in range(3):
        for k in range(4):
            def moved_rows(ref):
                return rows([
                    lanes([
                        ref[2 * pair + j - dx, 32 * k : 32 * k + 32] if 0 <= 2 * pair + j - dx < 4 else nothing
                        for j in range(2)
                    ])
                    for dx in range(3)
                ])
            total = total + nt3(
                moved_rows(goh), moved_rows(gol), around_pair(pjh, pair, k), around_pair(pjl, pair, k)
            )
    part_joined = rows([
        sum(
            roll(total[32 * dx + 16 * b + 8 * c : 32 * dx + 16 * b + 8 * c + 8], -(64 * b + 8 * c))
            for b in range(2)
            for c in range(2)
        )
        for dx in range(3)
    ])

    base = joined_turned(b_joined[...])
    w_back = stacked(
        rows([
            roll(base[8 * f : 8 * f + 8], 128 * a + 32 * b + 8 * c)
            for f in range(2)
            for a in range(2)
            for b in range(2)
            for c in range(2)
        ])
    )
    w_up_t = stacked(turned(b_up[...])[:16, :64])
    for ref in (pch, pcl):
        for at in range(4):
            ref[at, 0:2] = jnp.zeros((2, 48, 128), BF16)
            ref[at, 8:10] = jnp.zeros((2, 48, 128), BF16)
    for at in range(4):
        planes = [(2 * at - 3 + xw, xw) for xw in range(4) if 0 <= 2 * at - 3 + xw < 4]
        weight = w_back[:, 128 * planes[0][1] : 128 * planes[-1][1] + 128]
        for pair in range(3):
            def back_rhs(ref):
                return rows([
                    lanes([ref[x, 4 * pair + 2 * j : 4 * pair + 2 * j + 4].reshape(128, 128) for j in range(2)])
                    for x, _ in planes
                ])
            result = mm3(weight, back_rhs(pgh), back_rhs(pgl))
            high, low = split(result[:64])
            grad_act = mm3(w_up_t, high, low)
            for j in range(2):
                cell = 2 * pair + j
                mine = slice(128 * j, 128 * j + 128)
                gdir[at, cell] = result[64:, mine]
                guh[at, 64 * cell : 64 * cell + 64] = high[:, mine]
                gul[at, 64 * cell : 64 * cell + 64] = low[:, mine]
                grad_pre = grad_act[:, mine] * slope_c[at, 16 * cell : 16 * cell + 16]
                part_high, part_low = split(three_depths(grad_pre.reshape(1, 16, 128)))
                pch[at, cell + 2] = part_high.reshape(48, 128)
                pcl[at, cell + 2] = part_low.reshape(48, 128)
                part_high, part_low = split(grad_pre)
                gch[at, 16 * cell : 16 * cell + 16] = part_high
                gcl[at, 16 * cell : 16 * cell + 16] = part_low

    total = jnp.zeros((384, 96), F32)
    for pair in range(2):
        def two(ref):
            return lanes([ref[2 * pair], ref[2 * pair + 1]])
        total = total + nt3(two(guh), two(gul), two(ch), two(cl))
    total = lanes([total, jnp.zeros((384, 32), F32)])
    part_up = sum(roll(total[64 * y : 64 * y + 64], -16 * y) for y in range(6))

    nothing = jnp.zeros((96, 128), BF16)
    total = jnp.zeros((288, 384), F32)
    for pair in range(3):
        def moved_cells(ref):
            return rows([
                lanes([ref[2 * pair + j - dx] if 0 <= 2 * pair + j - dx < 4 else nothing for j in range(2)])
                for dx in range(3)
            ])
        def plane_pair(ref):
            return lanes([ref[2 * pair + j].reshape(384, 128) for j in range(2)])
        total = total + nt3(moved_cells(gch), moved_cells(gcl), plane_pair(pdh), plane_pair(pdl))
    lane_512 = lane_of((1, 512))
    tap, chan = lane_512 & 31, lane_512 >> 5
    tap_y = (tap * 11) >> 5
    row_256 = lax.broadcasted_iota(jnp.int32, (256, 512), 0)
    to_taps = jnp.where(row_256 == jnp.where(tap < 9, 16 * tap + chan, -1), 1.0, 0.0).astype(BF16)
    parts = [
        sum(roll(total[96 * dx + 16 * y : 96 * dx + 16 * y + 16], -48 * y) for y in range(6))[:, 0:256]
        for dx in range(3)
    ]
    part_coarse = by_tap(parts, to_taps)
    key = 64 * tap_y + 32 * (chan >> 3) + 8 * (tap - 3 * tap_y) + (chan & 7)
    to_taps = jnp.where(row_256 == jnp.where(tap < 9, key, -1), 1.0, 0.0).astype(BF16)
    part_joined = by_tap([part_joined[8 * dx : 8 * dx + 8] for dx in range(3)], to_taps)

    w_back_coarse = stacked(
        rows([roll(group, 48 * k) for group in coarse_turned(b_coarse[...]) for k in range(2)])[:, :192]
    )
    for pair in range(2):
        for k in range(4):
            def shifted(ref):
                return lanes([ref[2 * pair + j, 2 * k : 2 * k + 4].reshape(192, 128) for j in range(2)])
            part = mm3(w_back_coarse, shifted(pch), shifted(pcl))
            for j in range(2):
                rd[2 * pair + j, k] = part[:, 128 * j : 128 * j + 128]
    for at in range(6):
        for k in range(4):
            mine = slice(32 * k, 32 * k + 32)
            grad = sum(rd[at - 2 + dx, k, 32 * dx : 32 * dx + 32] for dx in range(3) if 0 <= at - 2 + dx < 4)
            high, low = split(grad * slope_d[at, mine])
            gdh[at, mine] = high
            gdl[at, mine] = low

    total = jnp.zeros((1024, 256), F32)
    for pair in range(3):
        def cells(ref):
            return lanes([ref[2 * pair], ref[2 * pair + 1]])
        def fine(ref):
            return rows([lanes([ref[2 * pair + j, :, 128 * a : 128 * a + 128] for j in range(2)]) for a in range(2)])
        total = total + nt(rows([fine(fh), fine(fl)]), rows([cells(gdh), cells(gdl)]))
    total = total[:512, :128] + total[:512, 128:] + total[512:, :128]
    part_down = rows([
        sum(roll(total[256 * a + 32 * y : 256 * a + 32 * y + 32], -16 * y) for y in range(8)) for a in range(2)
    ])

    base = turned(b_down[...])
    base = rows([base[0:32], base[128:160]])
    base = thrice(wider(base), 64)
    w_back_down = rows([roll(base[32 * a : 32 * a + 32], 16 * k) for a in range(2) for k in range(4)])
    w_back_down = w_back_down[:, :192].astype(BF16)
    total = jnp.zeros((128, 192), F32)
    for pair in range(3):
        for window in range(2):
            mine = slice(64 * window, 64 * window + 64)
            high = lanes([gdh[2 * pair, mine], gdh[2 * pair + 1, mine]])
            low = lanes([gdl[2 * pair, mine], gdl[2 * pair + 1, mine]])
            back = nn(w_back_down, rows([high, low, high]))
            for j in range(2):
                at = 2 * pair + j
                halves = []
                for a in range(2):
                    half = back[128 * a : 128 * a + 128, 128 * j : 128 * j + 128]
                    if 1 <= at <= 4:
                        blocks = [
                            gdir[at - 1, y - 1, 32 * a : 32 * a + 32] if 1 <= y <= 6 else jnp.zeros((32, 128), F32)
                            for y in range(4 * window, 4 * window + 4)
                        ]
                        half = half + rows(blocks)
                    halves.append(half)
                high, low = split(lanes(halves) * slope_f[at, 128 * window : 128 * window + 128])
                total = total + nt3(high, low, first_rhs(vh, at, window), first_rhs(vl, at, window))
    total = lanes([total, jnp.zeros((128, 64), F32)])
    part_first = sum(
        roll(total[16 * y + 8 * c : 16 * y + 8 * c + 8], -(y + 16 * c)) for y in range(8) for c in range(2)
    )

    tap = lane_of((1, 128))
    tap_x = (tap * 57) >> 9
    tap_y = ((tap - 9 * tap_x) * 11) >> 5
    key = jnp.where(tap < 27, 64 * tap_x + 16 * (tap - 9 * tap_x - 3 * tap_y) + tap_y, -1)
    row_256 = lax.broadcasted_iota(jnp.int32, (256, 128), 0)
    part_first = exact(part_first, jnp.where(row_256 == key, 1.0, 0.0).astype(BF16))
    for m in range(4):
        pay[16 * m : 16 * m + 16] = part_coarse[:, 128 * m : 128 * m + 128]
        pay[64 + 8 * m : 72 + 8 * m] = part_joined[:, 128 * m : 128 * m + 128]
    lane = lane_of((16, 128))
    pay[96:112] = sum(
        roll(jnp.where(lane < 16, part[16 * m : 16 * m + 16], 0.0), 32 * m + at)
        for m in range(4)
        for part, at in ((part_down, 0), (part_up, 16))
    )
    lane, row = lane_of((8, 128)), lax.broadcasted_iota(jnp.int32, (8, 128), 0)
    pay[112:120] = part_first + jnp.where(lane == 64 + row, part_final, 0.0)


def image(act_own, w_last, img):
    zt = lane_of((256, 256))
    rt = lax.broadcasted_iota(jnp.int32, (256, 256), 0)
    merge = jnp.where(zt == 2 * (rt & 127) + (rt >> 7), 1.0, 0.0).astype(BF16)
    f_row = lax.broadcasted_iota(jnp.int32, (16, 128), 0)
    f_col = lane_of((16, 128))
    wf_lanes = w_last[...]
    for by in (8, 16, 32, 64):
        wf_lanes = wf_lanes + roll(wf_lanes, by)
    w_final = stacked(
        jnp.where((f_row >> 3 == (f_col >> 3) & 1) & (f_row & 7 == f_col >> 4), wf_lanes, 0.0)
    )
    out_rows = []
    for at in range(2):
        result = mm3(w_final, *split(act_own[at]))
        for a in range(2):
            out_rows.append(lanes([result[8 * c : 8 * c + 8, 128 * a : 128 * a + 128] for c in range(2)]))
    whole = nn(stacked(rows(out_rows)), merge)
    img[...] = (whole[:32] + whole[32:]).reshape(4, 8, 256)


def run_image(act_own, w_last):
    vmem = pl.BlockSpec(memory_space=pltpu.VMEM)
    return pl.pallas_call(
        image,
        out_shape=jax.ShapeDtypeStruct((4, 8, 256), F32),
        in_specs=[vmem, vmem],
        out_specs=vmem,
        compiler_params=pltpu.CompilerParams(vmem_limit_bytes=8 * 1024 * 1024),
        cost_estimate=pl.CostEstimate(flops=200_000_000, bytes_accessed=400_000, transcendentals=0),
    )(act_own, w_last)


def exact(block, choice):
    high, low = split(block)
    rest = (block - high.astype(F32) - low.astype(F32)).astype(BF16)
    count = block.shape[0]
    found = nn(jnp.concatenate([high.astype(F32), low.astype(F32), rest.astype(F32)], axis=0).astype(BF16), choice)
    return found[:count] + found[count : 2 * count] + found[2 * count :]


def by_tap(parts, choice):
    count = parts[0].shape[0]
    found = exact(rows(parts), choice)
    return sum(roll(found[count * dx : count * dx + count], 9 * dx) for dx in range(len(parts)))


def outputs(*refs):
    blocks, (coarse, joined, first, down, up, final) = refs[:-6], refs[-6:]
    total = [ref[...] for ref in blocks]
    while len(total) > 1:
        total = [total[i] + total[i + 1] for i in range(0, len(total), 2)]
    total = total[0]

    def slot(start, count, at, width):
        block = total[start : start + count]
        return roll(block, -at)[:, :width]

    for i in range(16):
        coarse[:, i, :] = slot(16 * (i // 4), 16, 32 * (i % 4), 27)
        joined[:, i, :] = slot(64 + 8 * (i // 4), 8, 32 * (i % 4), 27)
    for k in range(8):
        down[:, k // 2, k % 2, :] = slot(96 + 8 * (k % 2), 8, 32 * (k // 2), 16)
        up[:, k // 2, k % 2, :] = slot(96 + 8 * (k % 2), 8, 32 * (k // 2) + 16, 16)
    first[:, 0, :] = total[112:120, :27]
    lane, row = lane_of((8, 128)), lax.broadcasted_iota(jnp.int32, (8, 128), 0)
    row_sum = jnp.sum(jnp.where(lane == 64 + row, total[112:120], 0.0), axis=0, keepdims=True)
    final[...] = roll(row_sum, -64)[:, :8]


def run_outputs(blocks):
    vmem = pl.BlockSpec(memory_space=pltpu.VMEM)
    shapes = ((16, 16, 27), (8, 16, 27), (8, 1, 27), (8, 4, 2, 16), (8, 4, 2, 16), (1, 8))
    return pl.pallas_call(
        outputs,
        out_shape=tuple(jax.ShapeDtypeStruct(shape, F32) for shape in shapes),
        in_specs=[vmem] * len(blocks),
        out_specs=(vmem,) * len(shapes),
        compiler_params=pltpu.CompilerParams(vmem_limit_bytes=4 * 1024 * 1024),
    )(*blocks)


def run_kernel(args, scale, size_x, size_y):
    vmem = pl.BlockSpec(memory_space=pltpu.VMEM)

    def pair(*shape):
        return [pltpu.VMEM(shape, BF16)] * 2

    def plain(*shape):
        return [pltpu.VMEM(shape, F32)]

    scratch = (
        plain(14, 2, 16, 256)
        + pair(14, 2, 64, 128)
        + pair(6, 256, 256)
        + plain(6, 256, 256)
        + pair(6, 8, 48, 128)
        + plain(6, 128, 128)
        + plain(6, 3, 96, 128)
        + plain(4, 96, 128)
        + pair(4, 96, 128)
        + pair(3, 12, 64, 256)
        + pair(4, 128, 128)
        + pair(4, 14, 32, 128)
        + plain(4, 6, 64, 128)
        + pair(4, 384, 128)
        + pair(4, 10, 48, 128)
        + pair(4, 96, 128)
        + plain(4, 4, 96, 128)
        + pair(6, 128, 128)
    )

    def unet_tile(*refs):
        kernel(*refs, scale=scale, size_x=size_x, size_y=size_y)

    return pl.pallas_call(
        unet_tile,
        out_shape=(jax.ShapeDtypeStruct((2, 128, 256), F32), jax.ShapeDtypeStruct((120, 128), F32)),
        in_specs=[pl.BlockSpec(memory_space=pltpu.SMEM)] + [vmem] * (len(args) - 1),
        out_specs=(vmem, vmem),
        scratch_shapes=scratch,
        compiler_params=pltpu.CompilerParams(vmem_limit_bytes=48 * 1024 * 1024),
        cost_estimate=pl.CostEstimate(flops=3_000_000_000, bytes_accessed=2_000_000, transcendentals=2_000_000),
    )(*args)


def swap(first, second, axis, by):
    count = lax.axis_size(axis)

    def pairs(parity):
        return [(i, (i + (by if (i // by) % 2 == parity else -by)) % count) for i in range(count)]

    return lax.ppermute(first, axis, pairs(0)), lax.ppermute(second, axis, pairs(1))


def rounds(count, apart):
    groups = [[k * by for k in (1, 2, 3) if k * by < count] for by in (1, 4, 16, 64) if by < count]
    if apart and len(groups[0]) == 3:
        groups = [[1], [3]] + groups[1:]
    return groups


def padded(block, *shape):
    return jnp.pad(block, [(0, want - have) for want, have in zip(shape, block.shape)])


def bases_now(w_first, w_joined, w_final):
    first = w_first.reshape(3, 3, 3, 8).transpose(3, 0, 2, 1)
    first = padded(first, 8, 4, 4, 16).reshape(8, 256)
    joined = w_joined.reshape(3, 3, 3, 8, 2, 8)
    joined = padded(joined.transpose(0, 3, 1, 4, 2, 5), 3, 8, 4, 2, 4, 8).reshape(24, 256)
    return first, joined, padded(w_final, 1, 128)


def bases_later(w_down, w_coarse, w_up):
    down = padded(w_down.transpose(0, 2, 3, 4, 1).reshape(16, 2, 32), 16, 2, 128).reshape(16, 256)
    coarse = w_coarse.reshape(3, 3, 3, 16, 16)
    coarse = padded(coarse.transpose(0, 3, 1, 2, 4).reshape(48, 144), 48, 256)
    up = padded(w_up.transpose(2, 3, 4, 0, 1).reshape(64, 16), 64, 128)
    return down, coarse, up


def shards(in_field, cotangent, w_first, w_down, w_coarse, w_up, w_joined, w_final):
    size_x, size_y = 4 * lax.axis_size("gx"), 8 * lax.axis_size("gy")
    field, cot = in_field[0], cotangent[0]
    now = bases_now(w_first, w_joined, w_final)
    pos = jnp.stack([lax.axis_index("gx"), lax.axis_index("gy")]).astype(jnp.int32)
    even = ((lax.axis_index("gx") >> 1) & 1) == 0
    low, high = field[:1], field[3:]
    low, high = jnp.where(even, high, low), jnp.where(even, low, high)
    low, high, tile = lax.optimization_barrier((low, high, field))
    near = swap(tile, tile, "gx", 1)
    far = swap(low, high, "gx", 2)
    near, far, now, pos, (w_down, w_coarse, w_up) = lax.optimization_barrier(
        (near, far, now, pos, (w_down, w_coarse, w_up))
    )
    wide, *sent = run_strips([pos, field, *near, *far])
    beside = swap(*sent, "gy", 1)
    first, joined, last = now
    later = bases_later(w_down, w_coarse, w_up)
    weights = [first, *later, joined, last]

    scale = 1.0 / math.sqrt(size_x * size_y * in_field.shape[3])
    act_own, pay = run_kernel([pos, wide, *beside, cot, *weights], scale, size_x, size_y)

    blocks, imitated = [pay], None
    for axis in ("gy", "gx"):
        count = lax.axis_size(axis)
        for partners in rounds(count, axis == "gx"):
            while len(blocks) > 1:
                blocks = [blocks[i] + blocks[i + 1] for i in range(0, len(blocks), 2)]
            mine = blocks[0]
            blocks = [mine] + [lax.ppermute(mine, axis, [(i, i ^ k) for i in range(count)]) for k in partners]
            if imitated is None:
                act_own, blocks = lax.optimization_barrier((act_own, blocks))
                imitated = run_image(act_own, last)
    coarse, joined, first, down, up, final = run_outputs(blocks)
    return (
        imitated[None],
        first.transpose(2, 0, 1),
        down.reshape(8, 2, 2, 2, 16).transpose(4, 0, 1, 2, 3),
        coarse.transpose(2, 0, 1),
        up.reshape(8, 2, 2, 2, 16).transpose(0, 4, 1, 2, 3),
        joined.transpose(2, 0, 1),
        final,
    )


def solution(mesh):
    in_specs = (P(None, "gx", "gy", None), P(None, "gx", "gy", None), P(), P(), P(), P(), P(), P())
    out_specs = (P(None, "gx", "gy", None), P(), P(), P(), P(), P(), P())
    return jax.shard_map(shards, mesh=mesh, in_specs=in_specs, out_specs=out_specs, check_vma=False)
```

```python
import math

import jax
import jax.numpy as jnp
from jax import lax
from jax.experimental import pallas as pl
from jax.experimental.pallas import tpu as pltpu
from jax.sharding import PartitionSpec as P

F32 = jnp.float32
BF16 = jnp.bfloat16


def nn(a, b):
    return lax.dot_general(a, b, (((1,), (0,)), ((), ())), preferred_element_type=F32)


def nt(a, b):
    return lax.dot_general(a, b, (((1,), (1,)), ((), ())), preferred_element_type=F32)


def split(x):
    high = x.astype(BF16)
    return high, (x - high.astype(F32)).astype(BF16)


def rows(parts):
    return jnp.concatenate(parts, axis=0)


def lanes(parts):
    return jnp.concatenate(parts, axis=1)


def stacked(weight):
    return rows(list(split(weight)))


def mm3(both, high, low):
    count = both.shape[0] // 2
    first = nn(both, high)
    return first[:count] + first[count:] + nn(both[:count], low)


def nt3(left_high, left_low, right_high, right_low):
    count = left_high.shape[0]
    first = nt(rows([left_high, left_low]), right_high)
    return first[:count] + first[count:] + nt(left_high, right_low)


def thrice(base, depth):
    high, low = split(base)
    high = high.astype(F32)
    return high + roll(high, depth) + roll(low.astype(F32), 2 * depth)


def wider(base):
    return lanes([base, jnp.zeros((base.shape[0], 256 - base.shape[1]), F32)])


def turned(block):
    m, n = block.shape
    if m % 128:
        block = rows([block, jnp.zeros((128 - m % 128, n), F32)])
    return block.T


def joined_turned(base):
    block = turned(base)
    lane = lane_of((8, 128)) >> 3
    parts = []
    for f in (1, 0):
        groups = []
        for dx in (2, 1, 0):
            groups.append(sum(
                roll(
                    jnp.where(lane == dx, block[64 * dy + 32 * f + 8 * dz : 64 * dy + 32 * f + 8 * dz + 8], 0.0),
                    32 * (2 - dy) + 8 * (2 - dz) - 8 * dx,
                )
                for dy in range(3)
                for dz in range(3)
            ))
        parts.append(lanes(groups + [jnp.zeros((8, 128), F32)]))
    return rows(parts)


def coarse_turned(base):
    block = turned(base)
    lane = lane_of((16, 128)) >> 4
    groups = []
    for dx in (2, 1, 0):
        taps = [
            roll(jnp.where(lane == dx, block[16 * k : 16 * k + 16], 0.0), 16 * ((8 - k) % 8) - 16 * dx)
            for k in range(9)
        ]
        groups.append(lanes([sum(taps[1:]), taps[0]]))
    return groups


def roll(x, shift):
    shift = shift % x.shape[1]
    return x if shift == 0 else pltpu.roll(x, shift, 1)


def sigmoid(x):
    return 1.0 / (1.0 + jnp.exp(-x))


def lane_of(shape):
    return lax.broadcasted_iota(jnp.int32, shape, len(shape) - 1)


def back_one(x):
    return jnp.where(lane_of(x.shape) == 0, 0.0, pltpu.roll(x, 1, 1))


def ahead_one(x):
    return jnp.where(lane_of(x.shape) == 127, 0.0, pltpu.roll(x, 127, 1))


def four_depths(field):
    count = field.shape[0]
    even, odd = field[:, :8], field[:, 8:]
    before = back_one(odd.reshape(count * 8, 128)).reshape(count, 8, 128)
    after = ahead_one(even.reshape(count * 8, 128)).reshape(count, 8, 128)
    return jnp.concatenate([before, even, odd, after], axis=1)


def three_depths(field):
    count = field.shape[0]
    flat = field.reshape(count * 16, 128)
    return jnp.concatenate(
        [back_one(flat).reshape(count, 16, 128), field, ahead_one(flat).reshape(count, 16, 128)],
        axis=1,
    )


def inside(at, extent):
    return jnp.where((at >= 0) & (at < extent), 1.0, 0.0).astype(F32)


def plane_of(field, near, far, even_x, even_far):
    def plane(x):
        if 5 <= x < 9:
            return field[x - 5]
        pair, even, at = (far, even_far, 0) if x in (0, 13) else (near, even_x, x - 1 if x < 5 else x - 9)
        below = x < 5
        return jnp.where(even, pair[1 if below else 0][at], pair[0 if below else 1][at])

    return plane


def strips(pos, field, near_0, near_1, far_0, far_1, wide, out_0, out_1):
    px, py = pos[0], pos[1]
    even_y = (py & 1) == 0
    plane = plane_of(field, (near_0, near_1), (far_0, far_1), (px & 1) == 0, ((px >> 1) & 1) == 0)
    for x in range(14):
        own = plane(x)
        wide[x] = own
        low, high = own[0:5], own[3:8]
        out_0[5 * x : 5 * x + 5] = jnp.where(even_y, high, low)
        out_1[5 * x : 5 * x + 5] = jnp.where(even_y, low, high)


def run_strips(args):
    vmem = pl.BlockSpec(memory_space=pltpu.VMEM)
    return pl.pallas_call(
        strips,
        out_shape=tuple(jax.ShapeDtypeStruct(shape, F32) for shape in ((14, 8, 256), (70, 256), (70, 256))),
        in_specs=[pl.BlockSpec(memory_space=pltpu.SMEM)] + [vmem] * (len(args) - 1),
        out_specs=(vmem,) * 3,
        compiler_params=pltpu.CompilerParams(vmem_limit_bytes=4 * 1024 * 1024),
    )(*args)


def kernel(
    pos, wide, beside_0, beside_1, cot,
    b_first, b_down, b_coarse, b_up, b_joined, w_last,
    act_own, pay,
    fe, vh, vl, fh, fl, slope_f, pdh, pdl, slope_d, rc, slope_c, ch, cl, pjh, pjl, goh, gol,
    pgh, pgl, gdir, guh, gul, pch, pcl, gch, gcl, rd, gdh, gdl,
    *, scale, size_x, size_y,
):
    px, py = pos[0], pos[1]

    z = lax.broadcasted_iota(jnp.int32, (256, 512), 0)
    col = lane_of((256, 512))
    pick = jnp.where(z == 2 * (col & 127) + (col >> 7) - 1, 1.0, 0.0).astype(BF16)
    pick_two = pick[:, 128:384]

    even_y = (py & 1) == 0
    has_head, has_tail = inside(8 * py - 1, size_y), inside(8 * py + 8, size_y)
    for x in range(14):
        own = wide[x]
        first, second = beside_0[5 * x : 5 * x + 5], beside_1[5 * x : 5 * x + 5]
        head, tail = jnp.where(even_y, second, first), jnp.where(even_y, first, second)
        there = inside(4 * px + x - 5, size_x)
        head, own, tail = head * (there * has_head), own * there, tail * (there * has_tail)
        fe[x, 0] = rows([head, own, tail[0:3]])
        fe[x, 1] = rows([own[3:8], tail, jnp.zeros((6, 256), F32)])
    for source, target in zip(split(fe[...].reshape(448, 256)), (vh, vl)):
        found = nn(source, pick).astype(BF16)
        for v in range(4):
            target[:, :, 16 * v : 16 * v + 16, :] = found[:, 128 * v : 128 * v + 128].reshape(14, 2, 16, 128)

    def first_rhs(ref, at, window):
        return rows([lanes([ref[2 * at + a + dx, window] for a in range(2)]) for dx in range(3)])

    base = b_first[...]
    w_first = stacked(rows([roll(base, yo + 16 * c) for yo in range(8) for c in range(2)])[:, :192])
    row_y = (lax.broadcasted_iota(jnp.int32, (128, 256), 0) >> 4) + 8 * py - 4
    lane_a = lane_of((1, 256)) >> 7
    for at in range(6):
        mask_x = inside(4 * px + 2 * (at - 2) + lane_a, size_x)
        for window in range(2):
            mine = slice(128 * window, 128 * window + 128)
            pre = mm3(w_first, first_rhs(vh, at, window), first_rhs(vl, at, window))
            mask = inside(row_y + 8 * window, size_y) * mask_x
            sig = sigmoid(pre)
            act = pre * sig
            slope_f[at, mine] = (sig + act * (1.0 - sig)) * mask
            act = act * mask
            high, low = split(act)
            fh[at, mine] = high
            fl[at, mine] = low
            part = act.reshape(8, 16, 256)[2:8] if window == 0 else act.reshape(8, 16, 256)[0:6]
            for a in range(2):
                plane = 2 * (at - 1) + a - 1
                if 0 <= plane < 6:
                    half = slice(128 * (plane % 2), 128 * (plane % 2) + 128)
                    high, low = split(four_depths(part[:, :, 128 * a : 128 * a + 128]))
                    pjh[plane // 2, 6 * window : 6 * window + 6, 0:32, half] = high
                    pjl[plane // 2, 6 * window : 6 * window + 6, 0:32, half] = low

    base = b_down[...]
    w_down = stacked(rows([roll(base, 32 * k) for k in range(4)]))
    row_64 = lax.broadcasted_iota(jnp.int32, (64, 256), 0) >> 4
    for pair in range(3):
        mask_x = inside(2 * px + 2 * pair + lane_a - 2, size_x // 2)
        for y0 in (0, 4):
            def down_rhs(ref):
                return rows([
                    lanes([ref[2 * pair + j, 32 * y0 : 32 * y0 + 128, 128 * a : 128 * a + 128] for j in range(2)])
                    for a in range(2)
                ])
            pre = mm3(w_down, down_rhs(fh), down_rhs(fl))
            mask = inside(row_64 + y0 - 2 + 4 * py, size_y // 2) * mask_x
            sig = sigmoid(pre)
            act = pre * sig
            sloped = (sig + act * (1.0 - sig)) * mask
            act = act * mask
            for j in range(2):
                mine = slice(128 * j, 128 * j + 128)
                high, low = split(three_depths(act[:, mine].reshape(4, 16, 128)))
                pdh[2 * pair + j, y0 : y0 + 4] = high
                pdl[2 * pair + j, y0 : y0 + 4] = low
                slope_d[2 * pair + j, 16 * y0 : 16 * y0 + 64] = sloped[:, mine]

    base = b_coarse[...]
    w_coarse = stacked(
        rows([roll(base[16 * dx : 16 * dx + 16], 48 * k) for dx in range(3) for k in range(2)])[:, :192]
    )
    for pair in range(3):
        for k in range(3):
            def coarse_rhs(ref):
                return lanes([ref[2 * pair + j, 2 * k : 2 * k + 4].reshape(192, 128) for j in range(2)])
            part = mm3(w_coarse, coarse_rhs(pdh), coarse_rhs(pdl))
            for j in range(2):
                rc[2 * pair + j, k] = part[:, 128 * j : 128 * j + 128]
    row_32 = lax.broadcasted_iota(jnp.int32, (32, 128), 0) >> 4
    for at in range(4):
        mask_x = inside(2 * px + at - 1, size_x // 2)
        for k in range(3):
            mine = slice(32 * k, 32 * k + 32)
            pre = rc[at, k, 0:32] + rc[at + 1, k, 32:64] + rc[at + 2, k, 64:96]
            mask = inside(row_32 + 2 * k - 1 + 4 * py, size_y // 2) * mask_x
            sig = sigmoid(pre)
            act = pre * sig
            slope_c[at, mine] = (sig + act * (1.0 - sig)) * mask
            high, low = split(act * mask)
            ch[at, mine] = high
            cl[at, mine] = low

    base = b_up[...]
    base = thrice(wider(base), 48)
    w_up = rows([roll(base[32 * a : 32 * a + 32], 16 * k) for a in range(2) for k in range(3)])[:, :144].astype(BF16)
    for pair in range(2):
        for block in range(2):
            mine = slice(48 * block, 48 * block + 48)
            high = lanes([ch[2 * pair, mine], ch[2 * pair + 1, mine]])
            low = lanes([cl[2 * pair, mine], cl[2 * pair + 1, mine]])
            part = nn(w_up, rows([high, low, high]))
            for j in range(2):
                for a in range(2):
                    plane = 2 * (2 * pair + j) + a - 1
                    if 0 <= plane < 6:
                        half = slice(128 * (plane % 2), 128 * (plane % 2) + 128)
                        cells = part[96 * a : 96 * a + 96, 128 * j : 128 * j + 128].reshape(6, 16, 128)
                        high_part, low_part = split(four_depths(cells))
                        pjh[plane // 2, 6 * block : 6 * block + 6, 32:64, half] = high_part
                        pjl[plane // 2, 6 * block : 6 * block + 6, 32:64, half] = low_part

    found = nn(rows(list(split(cot[...].reshape(32, 256)))), pick_two)
    sel_row = lax.broadcasted_iota(jnp.int32, (128, 32), 0)
    sel_col = lane_of((128, 32)) & 15
    spread = jnp.where(sel_col == ((sel_row >> 3) & 1) * 8 + (sel_row >> 4), 1.0, 0.0).astype(BF16)
    cb = [
        nn(
            spread,
            rows([
                lanes([
                    found[32 * s + 16 * at + 8 * a : 32 * s + 16 * at + 8 * a + 8, 128 * c : 128 * c + 128]
                    for a in range(2)
                ])
                for s in range(2)
                for c in range(2)
            ]).astype(BF16),
        )
        for at in range(2)
    ]

    base = b_joined[...]
    w_joined = stacked(
        rows([
            roll(base[8 * dx : 8 * dx + 8], 64 * b + 8 * c) for dx in range(3) for b in range(2) for c in range(2)
        ])
    )
    square = (8, 8)
    diagonal = lane_of(square) == lax.broadcasted_iota(jnp.int32, square, 0)
    column = jnp.sum(jnp.where(diagonal, jnp.broadcast_to(w_last[...][:, :8], square), 0.0), axis=1, keepdims=True)
    wf_rows = rows([column] * 4) * scale
    for x in range(4):
        for ref in (pgh, pgl):
            ref[x, 0:3] = jnp.zeros((3, 32, 128), BF16)
            ref[x, 11:14] = jnp.zeros((3, 32, 128), BF16)

    def around_pair(ref, pair, k):
        return ref[pair, 2 * k + 1 : 2 * k + 5].reshape(256, 256)

    for k in range(4):
        part = [mm3(w_joined, around_pair(pjh, pair, k), around_pair(pjl, pair, k)) for pair in range(3)]
        for x in range(4):
            pre = sum(
                part[(x + dx) // 2][32 * dx : 32 * dx + 32, 128 * ((x + dx) % 2) : 128 * ((x + dx) % 2) + 128]
                for dx in range(3)
            )
            at, half = x // 2, slice(128 * (x % 2), 128 * (x % 2) + 128)
            mine = slice(32 * k, 32 * k + 32)
            sig = sigmoid(pre)
            act = pre * sig
            grad = cb[at][mine, half] * wf_rows * (sig + act * (1.0 - sig))
            high, low = split(four_depths(grad.reshape(2, 16, 128)))
            pgh[x, 2 * k + 3 : 2 * k + 5] = high
            pgl[x, 2 * k + 3 : 2 * k + 5] = low
            act_own[at, mine, half] = act
            high, low = split(grad)
            goh[x, mine] = high
            gol[x, mine] = low

    part_final = sum(jnp.sum((act_own[at] * cb[at]).reshape(16, 8, 256), axis=0) for at in range(2))
    part_final = jnp.sum(part_final, axis=1, keepdims=True) * scale

    nothing = jnp.zeros((32, 128), BF16)
    total = jnp.zeros((96, 256), F32)
    for pair in range(3):
        for k in range(4):
            def moved_rows(ref):
                return rows([
                    lanes([
                        ref[2 * pair + j - dx, 32 * k : 32 * k + 32] if 0 <= 2 * pair + j - dx < 4 else nothing
                        for j in range(2)
                    ])
                    for dx in range(3)
                ])
            total = total + nt3(
                moved_rows(goh), moved_rows(gol), around_pair(pjh, pair, k), around_pair(pjl, pair, k)
            )
    part_joined = rows([
        sum(
            roll(total[32 * dx + 16 * b + 8 * c : 32 * dx + 16 * b + 8 * c + 8], -(64 * b + 8 * c))
            for b in range(2)
            for c in range(2)
        )
        for dx in range(3)
    ])

    base = joined_turned(b_joined[...])
    w_back = stacked(
        rows([
            roll(base[8 * f : 8 * f + 8], 128 * a + 32 * b + 8 * c)
            for f in range(2)
            for a in range(2)
            for b in range(2)
            for c in range(2)
        ])
    )
    w_up_t = stacked(turned(b_up[...])[:16, :64])
    for ref in (pch, pcl):
        for at in range(4):
            ref[at, 0:2] = jnp.zeros((2, 48, 128), BF16)
            ref[at, 8:10] = jnp.zeros((2, 48, 128), BF16)
    for at in range(4):
        planes = [(2 * at - 3 + xw, xw) for xw in range(4) if 0 <= 2 * at - 3 + xw < 4]
        weight = w_back[:, 128 * planes[0][1] : 128 * planes[-1][1] + 128]
        for pair in range(3):
            def back_rhs(ref):
                return rows([
                    lanes([ref[x, 4 * pair + 2 * j : 4 * pair + 2 * j + 4].reshape(128, 128) for j in range(2)])
                    for x, _ in planes
                ])
            result = mm3(weight, back_rhs(pgh), back_rhs(pgl))
            high, low = split(result[:64])
            grad_act = mm3(w_up_t, high, low)
            for j in range(2):
                cell = 2 * pair + j
                mine = slice(128 * j, 128 * j + 128)
                gdir[at, cell] = result[64:, mine]
                guh[at, 64 * cell : 64 * cell + 64] = high[:, mine]
                gul[at, 64 * cell : 64 * cell + 64] = low[:, mine]
                grad_pre = grad_act[:, mine] * slope_c[at, 16 * cell : 16 * cell + 16]
                part_high, part_low = split(three_depths(grad_pre.reshape(1, 16, 128)))
                pch[at, cell + 2] = part_high.reshape(48, 128)
                pcl[at, cell + 2] = part_low.reshape(48, 128)
                part_high, part_low = split(grad_pre)
                gch[at, 16 * cell : 16 * cell + 16] = part_high
                gcl[at, 16 * cell : 16 * cell + 16] = part_low

    total = jnp.zeros((384, 96), F32)
    for pair in range(2):
        def two(ref):
            return lanes([ref[2 * pair], ref[2 * pair + 1]])
        total = total + nt3(two(guh), two(gul), two(ch), two(cl))
    total = lanes([total, jnp.zeros((384, 32), F32)])
    part_up = sum(roll(total[64 * y : 64 * y + 64], -16 * y) for y in range(6))

    nothing = jnp.zeros((96, 128), BF16)
    total = jnp.zeros((288, 384), F32)
    for pair in range(3):
        def moved_cells(ref):
            return rows([
                lanes([ref[2 * pair + j - dx] if 0 <= 2 * pair + j - dx < 4 else nothing for j in range(2)])
                for dx in range(3)
            ])
        def plane_pair(ref):
            return lanes([ref[2 * pair + j].reshape(384, 128) for j in range(2)])
        total = total + nt3(moved_cells(gch), moved_cells(gcl), plane_pair(pdh), plane_pair(pdl))
    lane_512 = lane_of((1, 512))
    tap, chan = lane_512 & 31, lane_512 >> 5
    tap_y = (tap * 11) >> 5
    row_256 = lax.broadcasted_iota(jnp.int32, (256, 512), 0)
    to_taps = jnp.where(row_256 == jnp.where(tap < 9, 16 * tap + chan, -1), 1.0, 0.0).astype(BF16)
    parts = [
        sum(roll(total[96 * dx + 16 * y : 96 * dx + 16 * y + 16], -48 * y) for y in range(6))[:, 0:256]
        for dx in range(3)
    ]
    part_coarse = by_tap(parts, to_taps)
    key = 64 * tap_y + 32 * (chan >> 3) + 8 * (tap - 3 * tap_y) + (chan & 7)
    to_taps = jnp.where(row_256 == jnp.where(tap < 9, key, -1), 1.0, 0.0).astype(BF16)
    part_joined = by_tap([part_joined[8 * dx : 8 * dx + 8] for dx in range(3)], to_taps)

    w_back_coarse = stacked(
        rows([roll(group, 48 * k) for group in coarse_turned(b_coarse[...]) for k in range(2)])[:, :192]
    )
    for pair in range(2):
        for k in range(4):
            def shifted(ref):
                return lanes([ref[2 * pair + j, 2 * k : 2 * k + 4].reshape(192, 128) for j in range(2)])
            part = mm3(w_back_coarse, shifted(pch), shifted(pcl))
            for j in range(2):
                rd[2 * pair + j, k] = part[:, 128 * j : 128 * j + 128]
    for at in range(6):
        for k in range(4):
            mine = slice(32 * k, 32 * k + 32)
            grad = sum(rd[at - 2 + dx, k, 32 * dx : 32 * dx + 32] for dx in range(3) if 0 <= at - 2 + dx < 4)
            high, low = split(grad * slope_d[at, mine])
            gdh[at, mine] = high
            gdl[at, mine] = low

    total = jnp.zeros((1024, 256), F32)
    for pair in range(3):
        def cells(ref):
            return lanes([ref[2 * pair], ref[2 * pair + 1]])
        def fine(ref):
            return rows([lanes([ref[2 * pair + j, :, 128 * a : 128 * a + 128] for j in range(2)]) for a in range(2)])
        total = total + nt(rows([fine(fh), fine(fl)]), rows([cells(gdh), cells(gdl)]))
    total = total[:512, :128] + total[:512, 128:] + total[512:, :128]
    part_down = rows([
        sum(roll(total[256 * a + 32 * y : 256 * a + 32 * y + 32], -16 * y) for y in range(8)) for a in range(2)
    ])

    base = turned(b_down[...])
    base = rows([base[0:32], base[128:160]])
    base = thrice(wider(base), 64)
    w_back_down = rows([roll(base[32 * a : 32 * a + 32], 16 * k) for a in range(2) for k in range(4)])
    w_back_down = w_back_down[:, :192].astype(BF16)
    total = jnp.zeros((128, 192), F32)
    for pair in range(3):
        for window in range(2):
            mine = slice(64 * window, 64 * window + 64)
            high = lanes([gdh[2 * pair, mine], gdh[2 * pair + 1, mine]])
            low = lanes([gdl[2 * pair, mine], gdl[2 * pair + 1, mine]])
            back = nn(w_back_down, rows([high, low, high]))
            for j in range(2):
                at = 2 * pair + j
                halves = []
                for a in range(2):
                    half = back[128 * a : 128 * a + 128, 128 * j : 128 * j + 128]
                    if 1 <= at <= 4:
                        blocks = [
                            gdir[at - 1, y - 1, 32 * a : 32 * a + 32] if 1 <= y <= 6 else jnp.zeros((32, 128), F32)
                            for y in range(4 * window, 4 * window + 4)
                        ]
                        half = half + rows(blocks)
                    halves.append(half)
                high, low = split(lanes(halves) * slope_f[at, 128 * window : 128 * window + 128])
                total = total + nt3(high, low, first_rhs(vh, at, window), first_rhs(vl, at, window))
    total = lanes([total, jnp.zeros((128, 64), F32)])
    part_first = sum(
        roll(total[16 * y + 8 * c : 16 * y + 8 * c + 8], -(y + 16 * c)) for y in range(8) for c in range(2)
    )

    tap = lane_of((1, 128))
    tap_x = (tap * 57) >> 9
    tap_y = ((tap - 9 * tap_x) * 11) >> 5
    key = jnp.where(tap < 27, 64 * tap_x + 16 * (tap - 9 * tap_x - 3 * tap_y) + tap_y, -1)
    row_256 = lax.broadcasted_iota(jnp.int32, (256, 128), 0)
    part_first = exact(part_first, jnp.where(row_256 == key, 1.0, 0.0).astype(BF16))
    for m in range(4):
        pay[16 * m : 16 * m + 16] = part_coarse[:, 128 * m : 128 * m + 128]
        pay[64 + 8 * m : 72 + 8 * m] = part_joined[:, 128 * m : 128 * m + 128]
    lane = lane_of((16, 128))
    pay[96:112] = sum(
        roll(jnp.where(lane < 16, part[16 * m : 16 * m + 16], 0.0), 32 * m + at)
        for m in range(4)
        for part, at in ((part_down, 0), (part_up, 16))
    )
    lane, row = lane_of((8, 128)), lax.broadcasted_iota(jnp.int32, (8, 128), 0)
    pay[112:120] = part_first + jnp.where(lane == 64 + row, part_final, 0.0)
    pay[120:128] = jnp.zeros((8, 128), F32)


def image(act_own, w_last, img):
    zt = lane_of((256, 256))
    rt = lax.broadcasted_iota(jnp.int32, (256, 256), 0)
    merge = jnp.where(zt == 2 * (rt & 127) + (rt >> 7), 1.0, 0.0).astype(BF16)
    f_row = lax.broadcasted_iota(jnp.int32, (16, 128), 0)
    f_col = lane_of((16, 128))
    wf_lanes = w_last[...]
    for by in (8, 16, 32, 64):
        wf_lanes = wf_lanes + roll(wf_lanes, by)
    w_final = stacked(
        jnp.where((f_row >> 3 == (f_col >> 3) & 1) & (f_row & 7 == f_col >> 4), wf_lanes, 0.0)
    )
    out_rows = []
    for at in range(2):
        result = mm3(w_final, *split(act_own[at]))
        for a in range(2):
            out_rows.append(lanes([result[8 * c : 8 * c + 8, 128 * a : 128 * a + 128] for c in range(2)]))
    whole = nn(stacked(rows(out_rows)), merge)
    img[...] = (whole[:32] + whole[32:]).reshape(4, 8, 256)


def run_image(act_own, w_last):
    vmem = pl.BlockSpec(memory_space=pltpu.VMEM)
    return pl.pallas_call(
        image,
        out_shape=jax.ShapeDtypeStruct((4, 8, 256), F32),
        in_specs=[vmem, vmem],
        out_specs=vmem,
        compiler_params=pltpu.CompilerParams(vmem_limit_bytes=8 * 1024 * 1024),
        cost_estimate=pl.CostEstimate(flops=200_000_000, bytes_accessed=400_000, transcendentals=0),
    )(act_own, w_last)


def exact(block, choice):
    high, low = split(block)
    rest = (block - high.astype(F32) - low.astype(F32)).astype(BF16)
    count = block.shape[0]
    found = nn(jnp.concatenate([high.astype(F32), low.astype(F32), rest.astype(F32)], axis=0).astype(BF16), choice)
    return found[:count] + found[count : 2 * count] + found[2 * count :]


def by_tap(parts, choice):
    count = parts[0].shape[0]
    found = exact(rows(parts), choice)
    return sum(roll(found[count * dx : count * dx + count], 9 * dx) for dx in range(len(parts)))


def outputs(pos, mine, other, coarse, joined, first, down, up, final):
    lower = (pos[1] & 1) == 0
    total = rows([jnp.where(lower, mine[...], other[...]), jnp.where(lower, other[...], mine[...])])

    def slot(start, count, at, width):
        block = total[start : start + count]
        return roll(block, -at)[:, :width]

    for i in range(16):
        coarse[:, i, :] = slot(16 * (i // 4), 16, 32 * (i % 4), 27)
        joined[:, i, :] = slot(64 + 8 * (i // 4), 8, 32 * (i % 4), 27)
    for k in range(8):
        down[:, k // 2, k % 2, :] = slot(96 + 8 * (k % 2), 8, 32 * (k // 2), 16)
        up[:, k // 2, k % 2, :] = slot(96 + 8 * (k % 2), 8, 32 * (k // 2) + 16, 16)
    first[:, 0, :] = total[112:120, :27]
    lane, row = lane_of((8, 128)), lax.broadcasted_iota(jnp.int32, (8, 128), 0)
    row_sum = jnp.sum(jnp.where(lane == 64 + row, total[112:120], 0.0), axis=0, keepdims=True)
    final[...] = roll(row_sum, -64)[:, :8]


def summed(blocks):
    while len(blocks) > 1:
        blocks = [blocks[i] + blocks[i + 1] for i in range(0, len(blocks), 2)]
    return blocks[0]


def run_outputs(*args):
    vmem = pl.BlockSpec(memory_space=pltpu.VMEM)
    shapes = ((16, 16, 27), (8, 16, 27), (8, 1, 27), (8, 4, 2, 16), (8, 4, 2, 16), (1, 8))
    return pl.pallas_call(
        outputs,
        out_shape=tuple(jax.ShapeDtypeStruct(shape, F32) for shape in shapes),
        in_specs=[pl.BlockSpec(memory_space=pltpu.SMEM), vmem, vmem],
        out_specs=(vmem,) * len(shapes),
        compiler_params=pltpu.CompilerParams(vmem_limit_bytes=4 * 1024 * 1024),
    )(*args)


def run_kernel(args, scale, size_x, size_y):
    vmem = pl.BlockSpec(memory_space=pltpu.VMEM)

    def pair(*shape):
        return [pltpu.VMEM(shape, BF16)] * 2

    def plain(*shape):
        return [pltpu.VMEM(shape, F32)]

    scratch = (
        plain(14, 2, 16, 256)
        + pair(14, 2, 64, 128)
        + pair(6, 256, 256)
        + plain(6, 256, 256)
        + pair(6, 8, 48, 128)
        + plain(6, 128, 128)
        + plain(6, 3, 96, 128)
        + plain(4, 96, 128)
        + pair(4, 96, 128)
        + pair(3, 12, 64, 256)
        + pair(4, 128, 128)
        + pair(4, 14, 32, 128)
        + plain(4, 6, 64, 128)
        + pair(4, 384, 128)
        + pair(4, 10, 48, 128)
        + pair(4, 96, 128)
        + plain(4, 4, 96, 128)
        + pair(6, 128, 128)
    )

    def unet_tile(*refs):
        kernel(*refs, scale=scale, size_x=size_x, size_y=size_y)

    return pl.pallas_call(
        unet_tile,
        out_shape=(jax.ShapeDtypeStruct((2, 128, 256), F32), jax.ShapeDtypeStruct((128, 128), F32)),
        in_specs=[pl.BlockSpec(memory_space=pltpu.SMEM)] + [vmem] * (len(args) - 1),
        out_specs=(vmem, vmem),
        scratch_shapes=scratch,
        compiler_params=pltpu.CompilerParams(vmem_limit_bytes=48 * 1024 * 1024),
        cost_estimate=pl.CostEstimate(flops=3_000_000_000, bytes_accessed=2_000_000, transcendentals=2_000_000),
    )(*args)


def swap(first, second, axis, by):
    count = lax.axis_size(axis)

    def pairs(parity):
        return [(i, (i + (by if (i // by) % 2 == parity else -by)) % count) for i in range(count)]

    return lax.ppermute(first, axis, pairs(0)), lax.ppermute(second, axis, pairs(1))


def rounds(count, apart):
    groups = [[k * by for k in (1, 2, 3) if k * by < count] for by in (1, 4, 16, 64) if by < count]
    if apart and len(groups[0]) == 3:
        groups = [[1], [3]] + groups[1:]
    return groups


def padded(block, *shape):
    return jnp.pad(block, [(0, want - have) for want, have in zip(shape, block.shape)])


def bases_now(w_first, w_joined, w_final):
    first = w_first.reshape(3, 3, 3, 8).transpose(3, 0, 2, 1)
    first = padded(first, 8, 4, 4, 16).reshape(8, 256)
    joined = w_joined.reshape(3, 3, 3, 8, 2, 8)
    joined = padded(joined.transpose(0, 3, 1, 4, 2, 5), 3, 8, 4, 2, 4, 8).reshape(24, 256)
    return first, joined, padded(w_final, 1, 128)


def bases_later(w_down, w_coarse, w_up):
    down = padded(w_down.transpose(0, 2, 3, 4, 1).reshape(16, 2, 32), 16, 2, 128).reshape(16, 256)
    coarse = w_coarse.reshape(3, 3, 3, 16, 16)
    coarse = padded(coarse.transpose(0, 3, 1, 2, 4).reshape(48, 144), 48, 256)
    up = padded(w_up.transpose(2, 3, 4, 0, 1).reshape(64, 16), 64, 128)
    return down, coarse, up


def shards(in_field, cotangent, w_first, w_down, w_coarse, w_up, w_joined, w_final):
    size_x, size_y = 4 * lax.axis_size("gx"), 8 * lax.axis_size("gy")
    field, cot = in_field[0], cotangent[0]
    now = bases_now(w_first, w_joined, w_final)
    pos = jnp.stack([lax.axis_index("gx"), lax.axis_index("gy")]).astype(jnp.int32)
    even = ((lax.axis_index("gx") >> 1) & 1) == 0
    low, high = field[:1], field[3:]
    low, high = jnp.where(even, high, low), jnp.where(even, low, high)
    low, high, tile = lax.optimization_barrier((low, high, field))
    near = swap(tile, tile, "gx", 1)
    far = swap(low, high, "gx", 2)
    near, far, now, pos, (w_down, w_coarse, w_up) = lax.optimization_barrier(
        (near, far, now, pos, (w_down, w_coarse, w_up))
    )
    wide, *sent = run_strips([pos, field, *near, *far])
    beside = swap(*sent, "gy", 1)
    first, joined, last = now
    later = bases_later(w_down, w_coarse, w_up)
    weights = [first, *later, joined, last]

    scale = 1.0 / math.sqrt(size_x * size_y * in_field.shape[3])
    act_own, pay = run_kernel([pos, wide, *beside, cot, *weights], scale, size_x, size_y)

    block, imitated = pay, None
    for axis in ("gy", "gx"):
        count = lax.axis_size(axis)
        for partners in rounds(count, axis == "gx"):
            blocks = [block] + [lax.ppermute(block, axis, [(i, i ^ k) for i in range(count)]) for k in partners]
            if imitated is None:
                act_own, blocks = lax.optimization_barrier((act_own, blocks))
                imitated = run_image(act_own, last)
                block = lax.dynamic_slice_in_dim(summed(blocks), 64 * (lax.axis_index("gy") & 1), 64)
            else:
                block = summed(blocks)
    other = lax.ppermute(block, "gy", [(i, i ^ 1) for i in range(lax.axis_size("gy"))])
    coarse, joined, first, down, up, final = run_outputs(pos, block, other)
    return (
        imitated[None],
        first.transpose(2, 0, 1),
        down.reshape(8, 2, 2, 2, 16).transpose(4, 0, 1, 2, 3),
        coarse.transpose(2, 0, 1),
        up.reshape(8, 2, 2, 2, 16).transpose(0, 4, 1, 2, 3),
        joined.transpose(2, 0, 1),
        final,
    )


def solution(mesh):
    in_specs = (P(None, "gx", "gy", None), P(None, "gx", "gy", None), P(), P(), P(), P(), P(), P())
    out_specs = (P(None, "gx", "gy", None), P(), P(), P(), P(), P(), P())
    return jax.shard_map(shards, mesh=mesh, in_specs=in_specs, out_specs=out_specs, check_vma=False)
```

```python
import math

import jax
import jax.numpy as jnp
from jax import lax
from jax.experimental import pallas as pl
from jax.experimental.pallas import tpu as pltpu
from jax.sharding import PartitionSpec as P

F32 = jnp.float32
BF16 = jnp.bfloat16


def nn(a, b):
    return lax.dot_general(a, b, (((1,), (0,)), ((), ())), preferred_element_type=F32)


def nt(a, b):
    return lax.dot_general(a, b, (((1,), (1,)), ((), ())), preferred_element_type=F32)


def split(x):
    high = x.astype(BF16)
    return high, (x - high.astype(F32)).astype(BF16)


def rows(parts):
    return jnp.concatenate(parts, axis=0)


def lanes(parts):
    return jnp.concatenate(parts, axis=1)


def stacked(weight):
    return rows(list(split(weight)))


def mm3(both, high, low):
    count = both.shape[0] // 2
    first = nn(both, high)
    return first[:count] + first[count:] + nn(both[:count], low)


def nt3(left_high, left_low, right_high, right_low):
    count = left_high.shape[0]
    first = nt(rows([left_high, left_low]), right_high)
    return first[:count] + first[count:] + nt(left_high, right_low)


def thrice(base, depth):
    high, low = split(base)
    high = high.astype(F32)
    return high + roll(high, depth) + roll(low.astype(F32), 2 * depth)


def wider(base):
    return lanes([base, jnp.zeros((base.shape[0], 256 - base.shape[1]), F32)])


def turned(block):
    m, n = block.shape
    if m % 128:
        block = rows([block, jnp.zeros((128 - m % 128, n), F32)])
    return block.T


def joined_turned(base):
    block = turned(base)
    lane = lane_of((8, 128)) >> 3
    parts = []
    for f in (1, 0):
        groups = []
        for dx in (2, 1, 0):
            groups.append(sum(
                roll(
                    jnp.where(lane == dx, block[64 * dy + 32 * f + 8 * dz : 64 * dy + 32 * f + 8 * dz + 8], 0.0),
                    32 * (2 - dy) + 8 * (2 - dz) - 8 * dx,
                )
                for dy in range(3)
                for dz in range(3)
            ))
        parts.append(lanes(groups + [jnp.zeros((8, 128), F32)]))
    return rows(parts)


def coarse_turned(base):
    block = turned(base)
    lane = lane_of((16, 128)) >> 4
    groups = []
    for dx in (2, 1, 0):
        taps = [
            roll(jnp.where(lane == dx, block[16 * k : 16 * k + 16], 0.0), 16 * ((8 - k) % 8) - 16 * dx)
            for k in range(9)
        ]
        groups.append(lanes([sum(taps[1:]), taps[0]]))
    return groups


def roll(x, shift):
    shift = shift % x.shape[1]
    return x if shift == 0 else pltpu.roll(x, shift, 1)


def sigmoid(x):
    return 1.0 / (1.0 + jnp.exp(-x))


def lane_of(shape):
    return lax.broadcasted_iota(jnp.int32, shape, len(shape) - 1)


def back_one(x):
    return jnp.where(lane_of(x.shape) == 0, 0.0, pltpu.roll(x, 1, 1))


def ahead_one(x):
    return jnp.where(lane_of(x.shape) == 127, 0.0, pltpu.roll(x, 127, 1))


def four_depths(field):
    count = field.shape[0]
    even, odd = field[:, :8], field[:, 8:]
    before = back_one(odd.reshape(count * 8, 128)).reshape(count, 8, 128)
    after = ahead_one(even.reshape(count * 8, 128)).reshape(count, 8, 128)
    return jnp.concatenate([before, even, odd, after], axis=1)


def three_depths(field):
    count = field.shape[0]
    flat = field.reshape(count * 16, 128)
    return jnp.concatenate(
        [back_one(flat).reshape(count, 16, 128), field, ahead_one(flat).reshape(count, 16, 128)],
        axis=1,
    )


def inside(at, extent):
    return jnp.where((at >= 0) & (at < extent), 1.0, 0.0).astype(F32)


def plane_of(field, near, far, even_x, even_far):
    def plane(x):
        if 5 <= x < 9:
            return field[x - 5]
        pair, even, at = (far, even_far, 0) if x in (0, 13) else (near, even_x, x - 1 if x < 5 else x - 9)
        below = x < 5
        return jnp.where(even, pair[1 if below else 0][at], pair[0 if below else 1][at])

    return plane


def strips(pos, field, near_0, near_1, far_0, far_1, wide, out_0, out_1):
    px, py = pos[0], pos[1]
    even_y = (py & 1) == 0
    plane = plane_of(field, (near_0, near_1), (far_0, far_1), (px & 1) == 0, ((px >> 1) & 1) == 0)
    for x in range(14):
        own = plane(x)
        wide[x] = own
        low, high = own[0:5], own[3:8]
        out_0[5 * x : 5 * x + 5] = jnp.where(even_y, high, low)
        out_1[5 * x : 5 * x + 5] = jnp.where(even_y, low, high)


def run_strips(args):
    vmem = pl.BlockSpec(memory_space=pltpu.VMEM)
    return pl.pallas_call(
        strips,
        out_shape=tuple(jax.ShapeDtypeStruct(shape, F32) for shape in ((14, 8, 256), (70, 256), (70, 256))),
        in_specs=[pl.BlockSpec(memory_space=pltpu.SMEM)] + [vmem] * (len(args) - 1),
        out_specs=(vmem,) * 3,
        compiler_params=pltpu.CompilerParams(vmem_limit_bytes=4 * 1024 * 1024),
    )(*args)


def kernel(
    pos, wide, beside_0, beside_1, cot,
    b_first, b_down, b_coarse, b_up, b_joined, w_last,
    act_own, pay,
    fe, vh, vl, fh, fl, slope_f, pdh, pdl, slope_d, rc, slope_c, ch, cl, pjh, pjl, goh, gol,
    pgh, pgl, gdir, guh, gul, pch, pcl, gch, gcl, rd, gdh, gdl,
    *, scale, size_x, size_y,
):
    px, py = pos[0], pos[1]

    z = lax.broadcasted_iota(jnp.int32, (256, 512), 0)
    col = lane_of((256, 512))
    pick = jnp.where(z == 2 * (col & 127) + (col >> 7) - 1, 1.0, 0.0).astype(BF16)
    pick_two = pick[:, 128:384]

    even_y = (py & 1) == 0
    has_head, has_tail = inside(8 * py - 1, size_y), inside(8 * py + 8, size_y)
    for x in range(14):
        own = wide[x]
        first, second = beside_0[5 * x : 5 * x + 5], beside_1[5 * x : 5 * x + 5]
        head, tail = jnp.where(even_y, second, first), jnp.where(even_y, first, second)
        there = inside(4 * px + x - 5, size_x)
        head, own, tail = head * (there * has_head), own * there, tail * (there * has_tail)
        fe[x, 0] = rows([head, own, tail[0:3]])
        fe[x, 1] = rows([own[3:8], tail, jnp.zeros((6, 256), F32)])
    for source, target in zip(split(fe[...].reshape(448, 256)), (vh, vl)):
        found = nn(source, pick).astype(BF16)
        for v in range(4):
            target[:, :, 16 * v : 16 * v + 16, :] = found[:, 128 * v : 128 * v + 128].reshape(14, 2, 16, 128)

    def first_rhs(ref, at, window):
        return rows([lanes([ref[2 * at + a + dx, window] for a in range(2)]) for dx in range(3)])

    base = b_first[...]
    w_first = stacked(rows([roll(base, yo + 16 * c) for yo in range(8) for c in range(2)])[:, :192])
    row_y = (lax.broadcasted_iota(jnp.int32, (128, 256), 0) >> 4) + 8 * py - 4
    lane_a = lane_of((1, 256)) >> 7
    for at in range(6):
        mask_x = inside(4 * px + 2 * (at - 2) + lane_a, size_x)
        for window in range(2):
            mine = slice(128 * window, 128 * window + 128)
            pre = mm3(w_first, first_rhs(vh, at, window), first_rhs(vl, at, window))
            mask = inside(row_y + 8 * window, size_y) * mask_x
            sig = sigmoid(pre)
            act = pre * sig
            slope_f[at, mine] = (sig + act * (1.0 - sig)) * mask
            act = act * mask
            high, low = split(act)
            fh[at, mine] = high
            fl[at, mine] = low
            part = act.reshape(8, 16, 256)[2:8] if window == 0 else act.reshape(8, 16, 256)[0:6]
            for a in range(2):
                plane = 2 * (at - 1) + a - 1
                if 0 <= plane < 6:
                    half = slice(128 * (plane % 2), 128 * (plane % 2) + 128)
                    high, low = split(four_depths(part[:, :, 128 * a : 128 * a + 128]))
                    pjh[plane // 2, 6 * window : 6 * window + 6, 0:32, half] = high
                    pjl[plane // 2, 6 * window : 6 * window + 6, 0:32, half] = low

    base = b_down[...]
    w_down = stacked(rows([roll(base, 32 * k) for k in range(4)]))
    row_64 = lax.broadcasted_iota(jnp.int32, (64, 256), 0) >> 4
    for pair in range(3):
        mask_x = inside(2 * px + 2 * pair + lane_a - 2, size_x // 2)
        for y0 in (0, 4):
            def down_rhs(ref):
                return rows([
                    lanes([ref[2 * pair + j, 32 * y0 : 32 * y0 + 128, 128 * a : 128 * a + 128] for j in range(2)])
                    for a in range(2)
                ])
            pre = mm3(w_down, down_rhs(fh), down_rhs(fl))
            mask = inside(row_64 + y0 - 2 + 4 * py, size_y // 2) * mask_x
            sig = sigmoid(pre)
            act = pre * sig
            sloped = (sig + act * (1.0 - sig)) * mask
            act = act * mask
            for j in range(2):
                mine = slice(128 * j, 128 * j + 128)
                high, low = split(three_depths(act[:, mine].reshape(4, 16, 128)))
                pdh[2 * pair + j, y0 : y0 + 4] = high
                pdl[2 * pair + j, y0 : y0 + 4] = low
                slope_d[2 * pair + j, 16 * y0 : 16 * y0 + 64] = sloped[:, mine]

    base = b_coarse[...]
    w_coarse = stacked(
        rows([roll(base[16 * dx : 16 * dx + 16], 48 * k) for dx in range(3) for k in range(2)])[:, :192]
    )
    for pair in range(3):
        for k in range(3):
            def coarse_rhs(ref):
                return lanes([ref[2 * pair + j, 2 * k : 2 * k + 4].reshape(192, 128) for j in range(2)])
            part = mm3(w_coarse, coarse_rhs(pdh), coarse_rhs(pdl))
            for j in range(2):
                rc[2 * pair + j, k] = part[:, 128 * j : 128 * j + 128]
    row_32 = lax.broadcasted_iota(jnp.int32, (32, 128), 0) >> 4
    for at in range(4):
        mask_x = inside(2 * px + at - 1, size_x // 2)
        for k in range(3):
            mine = slice(32 * k, 32 * k + 32)
            pre = rc[at, k, 0:32] + rc[at + 1, k, 32:64] + rc[at + 2, k, 64:96]
            mask = inside(row_32 + 2 * k - 1 + 4 * py, size_y // 2) * mask_x
            sig = sigmoid(pre)
            act = pre * sig
            slope_c[at, mine] = (sig + act * (1.0 - sig)) * mask
            high, low = split(act * mask)
            ch[at, mine] = high
            cl[at, mine] = low

    base = b_up[...]
    base = thrice(wider(base), 48)
    w_up = rows([roll(base[32 * a : 32 * a + 32], 16 * k) for a in range(2) for k in range(3)])[:, :144].astype(BF16)
    for pair in range(2):
        for block in range(2):
            mine = slice(48 * block, 48 * block + 48)
            high = lanes([ch[2 * pair, mine], ch[2 * pair + 1, mine]])
            low = lanes([cl[2 * pair, mine], cl[2 * pair + 1, mine]])
            part = nn(w_up, rows([high, low, high]))
            for j in range(2):
                for a in range(2):
                    plane = 2 * (2 * pair + j) + a - 1
                    if 0 <= plane < 6:
                        half = slice(128 * (plane % 2), 128 * (plane % 2) + 128)
                        cells = part[96 * a : 96 * a + 96, 128 * j : 128 * j + 128].reshape(6, 16, 128)
                        high_part, low_part = split(four_depths(cells))
                        pjh[plane // 2, 6 * block : 6 * block + 6, 32:64, half] = high_part
                        pjl[plane // 2, 6 * block : 6 * block + 6, 32:64, half] = low_part

    found = nn(rows(list(split(cot[...].reshape(32, 256)))), pick_two)
    sel_row = lax.broadcasted_iota(jnp.int32, (128, 32), 0)
    sel_col = lane_of((128, 32)) & 15
    spread = jnp.where(sel_col == ((sel_row >> 3) & 1) * 8 + (sel_row >> 4), 1.0, 0.0).astype(BF16)
    cb = [
        nn(
            spread,
            rows([
                lanes([
                    found[32 * s + 16 * at + 8 * a : 32 * s + 16 * at + 8 * a + 8, 128 * c : 128 * c + 128]
                    for a in range(2)
                ])
                for s in range(2)
                for c in range(2)
            ]).astype(BF16),
        )
        for at in range(2)
    ]

    base = b_joined[...]
    w_joined = stacked(
        rows([
            roll(base[8 * dx : 8 * dx + 8], 64 * b + 8 * c) for dx in range(3) for b in range(2) for c in range(2)
        ])
    )
    square = (8, 8)
    diagonal = lane_of(square) == lax.broadcasted_iota(jnp.int32, square, 0)
    column = jnp.sum(jnp.where(diagonal, jnp.broadcast_to(w_last[...][:, :8], square), 0.0), axis=1, keepdims=True)
    wf_rows = rows([column] * 4) * scale
    for x in range(4):
        for ref in (pgh, pgl):
            ref[x, 0:3] = jnp.zeros((3, 32, 128), BF16)
            ref[x, 11:14] = jnp.zeros((3, 32, 128), BF16)

    def around_pair(ref, pair, k):
        return ref[pair, 2 * k + 1 : 2 * k + 5].reshape(256, 256)

    for k in range(4):
        part = [mm3(w_joined, around_pair(pjh, pair, k), around_pair(pjl, pair, k)) for pair in range(3)]
        for x in range(4):
            pre = sum(
                part[(x + dx) // 2][32 * dx : 32 * dx + 32, 128 * ((x + dx) % 2) : 128 * ((x + dx) % 2) + 128]
                for dx in range(3)
            )
            at, half = x // 2, slice(128 * (x % 2), 128 * (x % 2) + 128)
            mine = slice(32 * k, 32 * k + 32)
            sig = sigmoid(pre)
            act = pre * sig
            grad = cb[at][mine, half] * wf_rows * (sig + act * (1.0 - sig))
            high, low = split(four_depths(grad.reshape(2, 16, 128)))
            pgh[x, 2 * k + 3 : 2 * k + 5] = high
            pgl[x, 2 * k + 3 : 2 * k + 5] = low
            act_own[at, mine, half] = act
            high, low = split(grad)
            goh[x, mine] = high
            gol[x, mine] = low

    part_final = sum(jnp.sum((act_own[at] * cb[at]).reshape(16, 8, 256), axis=0) for at in range(2))
    part_final = jnp.sum(part_final, axis=1, keepdims=True) * scale

    nothing = jnp.zeros((32, 128), BF16)
    total = jnp.zeros((96, 256), F32)
    for pair in range(3):
        for k in range(4):
            def moved_rows(ref):
                return rows([
                    lanes([
                        ref[2 * pair + j - dx, 32 * k : 32 * k + 32] if 0 <= 2 * pair + j - dx < 4 else nothing
                        for j in range(2)
                    ])
                    for dx in range(3)
                ])
            total = total + nt3(
                moved_rows(goh), moved_rows(gol), around_pair(pjh, pair, k), around_pair(pjl, pair, k)
            )
    part_joined = rows([
        sum(
            roll(total[32 * dx + 16 * b + 8 * c : 32 * dx + 16 * b + 8 * c + 8], -(64 * b + 8 * c))
            for b in range(2)
            for c in range(2)
        )
        for dx in range(3)
    ])

    base = joined_turned(b_joined[...])
    w_back = stacked(
        rows([
            roll(base[8 * f : 8 * f + 8], 128 * a + 32 * b + 8 * c)
            for f in range(2)
            for a in range(2)
            for b in range(2)
            for c in range(2)
        ])
    )
    w_up_t = stacked(turned(b_up[...])[:16, :64])
    for ref in (pch, pcl):
        for at in range(4):
            ref[at, 0:2] = jnp.zeros((2, 48, 128), BF16)
            ref[at, 8:10] = jnp.zeros((2, 48, 128), BF16)
    for at in range(4):
        planes = [(2 * at - 3 + xw, xw) for xw in range(4) if 0 <= 2 * at - 3 + xw < 4]
        weight = w_back[:, 128 * planes[0][1] : 128 * planes[-1][1] + 128]
        for pair in range(3):
            def back_rhs(ref):
                return rows([
                    lanes([ref[x, 4 * pair + 2 * j : 4 * pair + 2 * j + 4].reshape(128, 128) for j in range(2)])
                    for x, _ in planes
                ])
            result = mm3(weight, back_rhs(pgh), back_rhs(pgl))
            high, low = split(result[:64])
            grad_act = mm3(w_up_t, high, low)
            for j in range(2):
                cell = 2 * pair + j
                mine = slice(128 * j, 128 * j + 128)
                gdir[at, cell] = result[64:, mine]
                guh[at, 64 * cell : 64 * cell + 64] = high[:, mine]
                gul[at, 64 * cell : 64 * cell + 64] = low[:, mine]
                grad_pre = grad_act[:, mine] * slope_c[at, 16 * cell : 16 * cell + 16]
                part_high, part_low = split(three_depths(grad_pre.reshape(1, 16, 128)))
                pch[at, cell + 2] = part_high.reshape(48, 128)
                pcl[at, cell + 2] = part_low.reshape(48, 128)
                part_high, part_low = split(grad_pre)
                gch[at, 16 * cell : 16 * cell + 16] = part_high
                gcl[at, 16 * cell : 16 * cell + 16] = part_low

    total = jnp.zeros((384, 96), F32)
    for pair in range(2):
        def two(ref):
            return lanes([ref[2 * pair], ref[2 * pair + 1]])
        total = total + nt3(two(guh), two(gul), two(ch), two(cl))
    total = lanes([total, jnp.zeros((384, 32), F32)])
    part_up = sum(roll(total[64 * y : 64 * y + 64], -16 * y) for y in range(6))

    nothing = jnp.zeros((96, 128), BF16)
    total = jnp.zeros((288, 384), F32)
    for pair in range(3):
        def moved_cells(ref):
            return rows([
                lanes([ref[2 * pair + j - dx] if 0 <= 2 * pair + j - dx < 4 else nothing for j in range(2)])
                for dx in range(3)
            ])
        def plane_pair(ref):
            return lanes([ref[2 * pair + j].reshape(384, 128) for j in range(2)])
        total = total + nt3(moved_cells(gch), moved_cells(gcl), plane_pair(pdh), plane_pair(pdl))
    lane_512 = lane_of((1, 512))
    tap, chan = lane_512 & 31, lane_512 >> 5
    tap_y = (tap * 11) >> 5
    row_256 = lax.broadcasted_iota(jnp.int32, (256, 512), 0)
    to_taps = jnp.where(row_256 == jnp.where(tap < 9, 16 * tap + chan, -1), 1.0, 0.0).astype(BF16)
    parts = [
        sum(roll(total[96 * dx + 16 * y : 96 * dx + 16 * y + 16], -48 * y) for y in range(6))[:, 0:256]
        for dx in range(3)
    ]
    part_coarse = by_tap(parts, to_taps)
    key = 64 * tap_y + 32 * (chan >> 3) + 8 * (tap - 3 * tap_y) + (chan & 7)
    to_taps = jnp.where(row_256 == jnp.where(tap < 9, key, -1), 1.0, 0.0).astype(BF16)
    part_joined = by_tap([part_joined[8 * dx : 8 * dx + 8] for dx in range(3)], to_taps)

    w_back_coarse = stacked(
        rows([roll(group, 48 * k) for group in coarse_turned(b_coarse[...]) for k in range(2)])[:, :192]
    )
    for pair in range(2):
        for k in range(4):
            def shifted(ref):
                return lanes([ref[2 * pair + j, 2 * k : 2 * k + 4].reshape(192, 128) for j in range(2)])
            part = mm3(w_back_coarse, shifted(pch), shifted(pcl))
            for j in range(2):
                rd[2 * pair + j, k] = part[:, 128 * j : 128 * j + 128]
    for at in range(6):
        for k in range(4):
            mine = slice(32 * k, 32 * k + 32)
            grad = sum(rd[at - 2 + dx, k, 32 * dx : 32 * dx + 32] for dx in range(3) if 0 <= at - 2 + dx < 4)
            high, low = split(grad * slope_d[at, mine])
            gdh[at, mine] = high
            gdl[at, mine] = low

    total = jnp.zeros((1024, 256), F32)
    for pair in range(3):
        def cells(ref):
            return lanes([ref[2 * pair], ref[2 * pair + 1]])
        def fine(ref):
            return rows([lanes([ref[2 * pair + j, :, 128 * a : 128 * a + 128] for j in range(2)]) for a in range(2)])
        total = total + nt(rows([fine(fh), fine(fl)]), rows([cells(gdh), cells(gdl)]))
    total = total[:512, :128] + total[:512, 128:] + total[512:, :128]
    part_down = rows([
        sum(roll(total[256 * a + 32 * y : 256 * a + 32 * y + 32], -16 * y) for y in range(8)) for a in range(2)
    ])

    base = turned(b_down[...])
    base = rows([base[0:32], base[128:160]])
    base = thrice(wider(base), 64)
    w_back_down = rows([roll(base[32 * a : 32 * a + 32], 16 * k) for a in range(2) for k in range(4)])
    w_back_down = w_back_down[:, :192].astype(BF16)
    total = jnp.zeros((128, 192), F32)
    for pair in range(3):
        for window in range(2):
            mine = slice(64 * window, 64 * window + 64)
            high = lanes([gdh[2 * pair, mine], gdh[2 * pair + 1, mine]])
            low = lanes([gdl[2 * pair, mine], gdl[2 * pair + 1, mine]])
            back = nn(w_back_down, rows([high, low, high]))
            for j in range(2):
                at = 2 * pair + j
                halves = []
                for a in range(2):
                    half = back[128 * a : 128 * a + 128, 128 * j : 128 * j + 128]
                    if 1 <= at <= 4:
                        blocks = [
                            gdir[at - 1, y - 1, 32 * a : 32 * a + 32] if 1 <= y <= 6 else jnp.zeros((32, 128), F32)
                            for y in range(4 * window, 4 * window + 4)
                        ]
                        half = half + rows(blocks)
                    halves.append(half)
                high, low = split(lanes(halves) * slope_f[at, 128 * window : 128 * window + 128])
                total = total + nt3(high, low, first_rhs(vh, at, window), first_rhs(vl, at, window))
    total = lanes([total, jnp.zeros((128, 64), F32)])
    part_first = sum(
        roll(total[16 * y + 8 * c : 16 * y + 8 * c + 8], -(y + 16 * c)) for y in range(8) for c in range(2)
    )

    tap = lane_of((1, 128))
    tap_x = (tap * 57) >> 9
    tap_y = ((tap - 9 * tap_x) * 11) >> 5
    key = jnp.where(tap < 27, 64 * tap_x + 16 * (tap - 9 * tap_x - 3 * tap_y) + tap_y, -1)
    row_256 = lax.broadcasted_iota(jnp.int32, (256, 128), 0)
    part_first = exact(part_first, jnp.where(row_256 == key, 1.0, 0.0).astype(BF16))
    for m in range(4):
        pay[16 * m : 16 * m + 16] = part_coarse[:, 128 * m : 128 * m + 128]
        pay[64 + 8 * m : 72 + 8 * m] = part_joined[:, 128 * m : 128 * m + 128]
    lane = lane_of((16, 128))
    pay[96:112] = sum(
        roll(jnp.where(lane < 16, part[16 * m : 16 * m + 16], 0.0), 32 * m + at)
        for m in range(4)
        for part, at in ((part_down, 0), (part_up, 16))
    )
    lane, row = lane_of((8, 128)), lax.broadcasted_iota(jnp.int32, (8, 128), 0)
    pay[112:120] = part_first + jnp.where(lane == 64 + row, part_final, 0.0)


def image(act_own, w_last, img):
    zt = lane_of((256, 256))
    rt = lax.broadcasted_iota(jnp.int32, (256, 256), 0)
    merge = jnp.where(zt == 2 * (rt & 127) + (rt >> 7), 1.0, 0.0).astype(BF16)
    f_row = lax.broadcasted_iota(jnp.int32, (16, 128), 0)
    f_col = lane_of((16, 128))
    wf_lanes = w_last[...]
    for by in (8, 16, 32, 64):
        wf_lanes = wf_lanes + roll(wf_lanes, by)
    w_final = stacked(
        jnp.where((f_row >> 3 == (f_col >> 3) & 1) & (f_row & 7 == f_col >> 4), wf_lanes, 0.0)
    )
    out_rows = []
    for at in range(2):
        result = mm3(w_final, *split(act_own[at]))
        for a in range(2):
            out_rows.append(lanes([result[8 * c : 8 * c + 8, 128 * a : 128 * a + 128] for c in range(2)]))
    whole = nn(stacked(rows(out_rows)), merge)
    img[...] = (whole[:32] + whole[32:]).reshape(4, 8, 256)


def run_image(act_own, w_last):
    vmem = pl.BlockSpec(memory_space=pltpu.VMEM)
    return pl.pallas_call(
        image,
        out_shape=jax.ShapeDtypeStruct((4, 8, 256), F32),
        in_specs=[vmem, vmem],
        out_specs=vmem,
        compiler_params=pltpu.CompilerParams(vmem_limit_bytes=8 * 1024 * 1024),
        cost_estimate=pl.CostEstimate(flops=200_000_000, bytes_accessed=400_000, transcendentals=0),
    )(act_own, w_last)


def exact(block, choice):
    high, low = split(block)
    rest = (block - high.astype(F32) - low.astype(F32)).astype(BF16)
    count = block.shape[0]
    found = nn(jnp.concatenate([high.astype(F32), low.astype(F32), rest.astype(F32)], axis=0).astype(BF16), choice)
    return found[:count] + found[count : 2 * count] + found[2 * count :]


def by_tap(parts, choice):
    count = parts[0].shape[0]
    found = exact(rows(parts), choice)
    return sum(roll(found[count * dx : count * dx + count], 9 * dx) for dx in range(len(parts)))


def outputs(*refs):
    blocks, (coarse, joined, first, down, up, final) = refs[:-6], refs[-6:]
    total = [ref[...] for ref in blocks]
    while len(total) > 1:
        total = [total[i] + total[i + 1] for i in range(0, len(total), 2)]
    total = total[0]

    def slot(start, count, at, width):
        block = total[start : start + count]
        return roll(block, -at)[:, :width]

    for i in range(16):
        coarse[:, i, :] = slot(16 * (i // 4), 16, 32 * (i % 4), 27)
        joined[:, i, :] = slot(64 + 8 * (i // 4), 8, 32 * (i % 4), 27)
    for k in range(8):
        down[:, k // 2, k % 2, :] = slot(96 + 8 * (k % 2), 8, 32 * (k // 2), 16)
        up[:, k // 2, k % 2, :] = slot(96 + 8 * (k % 2), 8, 32 * (k // 2) + 16, 16)
    first[:, 0, :] = total[112:120, :27]
    lane, row = lane_of((8, 128)), lax.broadcasted_iota(jnp.int32, (8, 128), 0)
    row_sum = jnp.sum(jnp.where(lane == 64 + row, total[112:120], 0.0), axis=0, keepdims=True)
    final[...] = roll(row_sum, -64)[:, :8]


def run_outputs(blocks):
    vmem = pl.BlockSpec(memory_space=pltpu.VMEM)
    shapes = ((16, 16, 27), (8, 16, 27), (8, 1, 27), (8, 4, 2, 16), (8, 4, 2, 16), (1, 8))
    return pl.pallas_call(
        outputs,
        out_shape=tuple(jax.ShapeDtypeStruct(shape, F32) for shape in shapes),
        in_specs=[vmem] * len(blocks),
        out_specs=(vmem,) * len(shapes),
        compiler_params=pltpu.CompilerParams(vmem_limit_bytes=4 * 1024 * 1024),
    )(*blocks)


def run_kernel(args, scale, size_x, size_y):
    vmem = pl.BlockSpec(memory_space=pltpu.VMEM)

    def pair(*shape):
        return [pltpu.VMEM(shape, BF16)] * 2

    def plain(*shape):
        return [pltpu.VMEM(shape, F32)]

    scratch = (
        plain(14, 2, 16, 256)
        + pair(14, 2, 64, 128)
        + pair(6, 256, 256)
        + plain(6, 256, 256)
        + pair(6, 8, 48, 128)
        + plain(6, 128, 128)
        + plain(6, 3, 96, 128)
        + plain(4, 96, 128)
        + pair(4, 96, 128)
        + pair(3, 12, 64, 256)
        + pair(4, 128, 128)
        + pair(4, 14, 32, 128)
        + plain(4, 6, 64, 128)
        + pair(4, 384, 128)
        + pair(4, 10, 48, 128)
        + pair(4, 96, 128)
        + plain(4, 4, 96, 128)
        + pair(6, 128, 128)
    )

    def unet_tile(*refs):
        kernel(*refs, scale=scale, size_x=size_x, size_y=size_y)

    return pl.pallas_call(
        unet_tile,
        out_shape=(jax.ShapeDtypeStruct((2, 128, 256), F32), jax.ShapeDtypeStruct((120, 128), F32)),
        in_specs=[pl.BlockSpec(memory_space=pltpu.SMEM)] + [vmem] * (len(args) - 1),
        out_specs=(vmem, vmem),
        scratch_shapes=scratch,
        compiler_params=pltpu.CompilerParams(vmem_limit_bytes=48 * 1024 * 1024),
        cost_estimate=pl.CostEstimate(flops=3_000_000_000, bytes_accessed=2_000_000, transcendentals=2_000_000),
    )(*args)


def swap(first, second, axis, by):
    count = lax.axis_size(axis)

    def pairs(parity):
        return [(i, (i + (by if (i // by) % 2 == parity else -by)) % count) for i in range(count)]

    return lax.ppermute(first, axis, pairs(0)), lax.ppermute(second, axis, pairs(1))


def rounds(count, apart):
    groups = [[k * by for k in (1, 2, 3) if k * by < count] for by in (1, 4, 16, 64) if by < count]
    if apart and len(groups[0]) == 3:
        groups = [[1], [3]] + groups[1:]
    return groups


def padded(block, *shape):
    return jnp.pad(block, [(0, want - have) for want, have in zip(shape, block.shape)])


def bases_now(w_first, w_joined, w_final):
    first = w_first.reshape(3, 3, 3, 8).transpose(3, 0, 2, 1)
    first = padded(first, 8, 4, 4, 16).reshape(8, 256)
    joined = w_joined.reshape(3, 3, 3, 8, 2, 8)
    joined = padded(joined.transpose(0, 3, 1, 4, 2, 5), 3, 8, 4, 2, 4, 8).reshape(24, 256)
    return first, joined, padded(w_final, 1, 128)


def bases_later(w_down, w_coarse, w_up):
    down = padded(w_down.transpose(0, 2, 3, 4, 1).reshape(16, 2, 32), 16, 2, 128).reshape(16, 256)
    coarse = w_coarse.reshape(3, 3, 3, 16, 16)
    coarse = padded(coarse.transpose(0, 3, 1, 2, 4).reshape(48, 144), 48, 256)
    up = padded(w_up.transpose(2, 3, 4, 0, 1).reshape(64, 16), 64, 128)
    return down, coarse, up


def shards(in_field, cotangent, w_first, w_down, w_coarse, w_up, w_joined, w_final):
    size_x, size_y = 4 * lax.axis_size("gx"), 8 * lax.axis_size("gy")
    field, cot = in_field[0], cotangent[0]
    now = bases_now(w_first, w_joined, w_final)
    pos = jnp.stack([lax.axis_index("gx"), lax.axis_index("gy")]).astype(jnp.int32)
    even = ((lax.axis_index("gx") >> 1) & 1) == 0
    low, high = field[:1], field[3:]
    low, high = jnp.where(even, high, low), jnp.where(even, low, high)
    low, high, tile = lax.optimization_barrier((low, high, field))
    near = swap(tile, tile, "gx", 1)
    far = swap(low, high, "gx", 2)
    near, far, now, pos, (w_down, w_coarse, w_up) = lax.optimization_barrier(
        (near, far, now, pos, (w_down, w_coarse, w_up))
    )
    wide, *sent = run_strips([pos, field, *near, *far])
    beside = swap(*sent, "gy", 1)
    first, joined, last = now
    later = bases_later(w_down, w_coarse, w_up)
    weights = [first, *later, joined, last]

    scale = 1.0 / math.sqrt(size_x * size_y * in_field.shape[3])
    act_own, pay = run_kernel([pos, wide, *beside, cot, *weights], scale, size_x, size_y)

    blocks, imitated = [pay], None
    for axis in ("gx", "gy"):
        count = lax.axis_size(axis)
        for partners in rounds(count, axis == "gx"):
            while len(blocks) > 1:
                blocks = [blocks[i] + blocks[i + 1] for i in range(0, len(blocks), 2)]
            mine = blocks[0]
            blocks = [mine] + [lax.ppermute(mine, axis, [(i, i ^ k) for i in range(count)]) for k in partners]
            if imitated is None:
                act_own, blocks = lax.optimization_barrier((act_own, blocks))
                imitated = run_image(act_own, last)
    coarse, joined, first, down, up, final = run_outputs(blocks)
    return (
        imitated[None],
        first.transpose(2, 0, 1),
        down.reshape(8, 2, 2, 2, 16).transpose(4, 0, 1, 2, 3),
        coarse.transpose(2, 0, 1),
        up.reshape(8, 2, 2, 2, 16).transpose(0, 4, 1, 2, 3),
        joined.transpose(2, 0, 1),
        final,
    )


def solution(mesh):
    in_specs = (P(None, "gx", "gy", None), P(None, "gx", "gy", None), P(), P(), P(), P(), P(), P())
    out_specs = (P(None, "gx", "gy", None), P(), P(), P(), P(), P(), P())
    return jax.shard_map(shards, mesh=mesh, in_specs=in_specs, out_specs=out_specs, check_vma=False)
```
